512 devices in a mesh: loop: 32 (over x, z_lo, core), group: 16 (over y, z_hi).
Axes of the slice: x: 4, y: 4, z: 16 (z_hi: 4, z_lo: 4; z = z_hi * 4 + z_lo), core: 2. Of those that a mesh axis runs over, the one named last changes fastest.
Arguments:
- features: bfloat16 [131072, 1024], P(('loop', 'group')), may hold values from -24 to 24
- targets: bfloat16 [512, 1024], P(('loop', 'group')), may hold values from -6 to 6
Outputs:
- scores: float32 [131072, 512], P(('loop', 'group'))
The draws below stay inside these ranges and needn't reach their ends.
All inputs are finite; a program needn't handle non-finite values.
Results may differ from the reference program's by a relative error of at most 0.003.
Values may be sent and summed in bfloat16 or wider, within the bound.
A program may use at most 64 MiB of HBM per device.

```python
import jax
import jax.numpy as jnp
from jax import lax

PROJ = 1024
ROWS_DEV = 256
TRAIN = 131072
TARGETS = 512


def strengthened(entries, key, source, target, shards_of, factor):
    owner, partner = [(jnp.arange(entries.shape[axis_at]) // (entries.shape[axis_at] // shards_of)).reshape([-1 if axis == axis_at else 1 for axis in range(entries.ndim)]) for axis_at in (source, target)]
    chosen = jax.random.permutation(key, shards_of)[partner]
    strong = (owner == chosen) | (owner == (partner + shards_of // 2) % shards_of)
    return jnp.where(strong, factor * entries, entries)


def block_levels(key, extent, pieces, smallest, top_value):
    factor_of = 1.0
    for position, shards_of in pieces:
        steps = jax.random.uniform(jax.random.fold_in(jax.random.fold_in(key, 6), position), (shards_of,), jnp.float32, smallest / len(pieces), top_value / len(pieces))
        factor_of = factor_of * jnp.repeat(jnp.exp(steps), extent[position] // shards_of).reshape((-1,) + (1,) * (len(extent) - 1 - position))
    return factor_of


def scatter_about(own_key, shape, deviation, limit, shards=(), held_as=jnp.bfloat16):
    level = block_levels(own_key, shape, shards, -0.22, 0.18) if shards else 1.0
    drawn = jax.random.normal(own_key, shape, jnp.float32) * deviation * level
    return jnp.minimum(jnp.maximum(drawn, -limit), limit).astype(held_as)


def bell_draw_with(stream_key, dims, scale, bound, shards, heavy, held_as=jnp.bfloat16):
    result = scale * jax.random.normal(stream_key, dims, jnp.float32)
    if shards:
        result = result * block_levels(stream_key, dims, shards, -0.22, 0.18)
    return jnp.clip(strengthened(result, jax.random.fold_in(stream_key, 3), *heavy), -bound, bound).astype(held_as)


def setup_inputs(seed: int = 0) -> dict:
    arg_keys = jax.random.split(jax.random.key(seed), 3)
    features = bell_draw_with(arg_keys[0], (TRAIN, PROJ), 1.0, 24.0, ((0, 512),), (0, 1, 512, 6.0))
    targets = scatter_about(arg_keys[1], (TARGETS, PROJ), 1.0, 6.0, ((0, 512),))
    return {"features": features, "targets": targets}


def block_gram(total, block):
    wide = block.astype(jnp.float32)
    return (total + jnp.dot(wide.T, wide, precision=lax.Precision.HIGHEST), None)

def chol_apply(factor, right):
    lower_part = lax.linalg.triangular_solve(factor, right, left_side=True, lower=True)
    return lax.linalg.triangular_solve(factor, lower_part, left_side=True, lower=True, transpose_a=True)

def reference(features, targets):
    blocks = features.reshape(-1, ROWS_DEV, PROJ)
    start = jnp.zeros((PROJ, PROJ), jnp.float32)
    kernel, unused = lax.scan(block_gram, start, blocks)
    damped = kernel + 0.05 * jnp.trace(kernel) / PROJ * jnp.eye(PROJ, dtype=jnp.float32)
    factor = jnp.linalg.cholesky(damped)
    solved = chol_apply(factor, targets.astype(jnp.float32).T)
    precond = (solved.T * (TRAIN / PROJ ** 0.5)).astype(jnp.bfloat16)
    wide_pre = precond.astype(jnp.float32)

    def score_block(block):
        return jnp.dot(block.astype(jnp.float32), wide_pre.T, precision=lax.Precision.HIGHEST)
    scores = lax.map(score_block, blocks)
    return scores.reshape(TRAIN, TARGETS)
```

```python
import functools

import jax
import jax.numpy as jnp
from jax import lax
from jax.experimental import pallas as pl
from jax.experimental.pallas import tpu as pltpu
from jax.sharding import PartitionSpec as P

WIDTH = 1024
TILE = 128
BLOCKS = WIDTH // TILE
KEPT = BLOCKS // 2 + 1
PART = KEPT * TILE
PARTS = BLOCKS // 2
NZ = 16
PIECE = PART * PARTS // 16 // NZ
RIGHTS = 64
TOL = 1e-5
MAX_STEPS = 4096
MESH = pl.DeviceIdType.MESH
F32 = jnp.float32
BF16 = jnp.bfloat16


def position():
    loop = lax.axis_index("loop")
    group = lax.axis_index("group")
    x = loop // 8
    y = group // 4
    z = (group % 4) * 4 + (loop // 2) % 4
    return x, y, z, loop % 2


def device(x, y, z, core):
    return (x * 8 + (z % 4) * 2 + core, y * 4 + z // 4)


def even_pair(v):
    return v + 1 - 2 * (v % 2)


def odd_pair(v):
    return 3 - v


def even_bit(v):
    return ((v + 1) // 2) % 2


def odd_bit(v):
    return v // 2


def remote(src, dst, send, recv, to):
    return pltpu.make_async_remote_copy(
        src_ref=src, dst_ref=dst, send_sem=send, recv_sem=recv, device_id=to, device_id_type=MESH
    )


def greet(others):
    barrier = pltpu.get_barrier_semaphore()
    for other in others:
        pl.semaphore_signal(barrier, inc=1, device_id=other, device_id_type=MESH)
    return barrier


def rows(start, size):
    return pl.ds(pl.multiple_of(start, 8), size)


def gram_sum(
    feat, tgt, out, tz, wide, packed, from_core, landed, zsrc, zland, zout, tcol, tsrc,
    core_s, core_r, cag_s, cag_r, ex_s, ex_r, ag_s, ag_r,
    z_s, z_r, za_s, za_r, ty_s, ty_r, tz_s, tz_r,
):
    x, y, z, core = position()
    sibling = device(x, y, z, 1 - core)
    ends = {
        "xe": (device(even_pair(x), y, z, core), even_bit(x)),
        "xo": (device(odd_pair(x), y, z, core), odd_bit(x)),
        "ye": (device(x, even_pair(y), z, core), even_bit(y)),
        "yo": (device(x, odd_pair(y), z, core), odd_bit(y)),
    }
    orders = [["xe", "xo", "ye", "yo"], ["xo", "xe", "yo", "ye"], ["ye", "yo", "xe", "xo"], ["yo", "ye", "xo", "xe"]]

    barrier = greet([sibling, ends["xe"][0], ends["xo"][0]])
    for t in range(1, 4):
        pl.semaphore_signal(barrier, inc=1, device_id=device(x, (y + t) % 4, z, core), device_id_type=MESH)

    def greet_z(t, carry):
        pl.semaphore_signal(barrier, inc=1, device_id=device(x, y, (z + t) % NZ, core), device_id_type=MESH)
        return carry

    lax.fori_loop(1, NZ, greet_z, 0)

    wide[:, :WIDTH] = feat[...]
    wide[:, WIDTH:] = feat[:, : WIDTH // 2]
    for k in range(8):
        tcol[0, k : k + 1, :] = tgt[:, k * TILE : (k + 1) * TILE].astype(F32)

    def block_row(i):
        tall = wide[:, pl.ds(pl.multiple_of(i * TILE, TILE), TILE)]
        span = wide[:, pl.ds(pl.multiple_of(i * TILE, TILE), PART)]
        product = lax.dot_general(tall, span, (((0,), (0,)), ((), ())), preferred_element_type=F32)
        for d in range(KEPT):
            packed[rows(i * PART + d * TILE, TILE), :] = product[:, d * TILE : (d + 1) * TILE]

    def core_copy(j):
        return remote(
            packed.at[rows(((1 - core) * PARTS + j) * PART, PART)], from_core.at[rows(j * PART, PART)],
            core_s.at[j], core_r.at[j], sibling,
        )

    block_row((1 - core) * PARTS)
    pl.semaphore_wait(barrier, 21)
    core_copy(0).start()

    def first(j, carry):
        block_row((1 - core) * PARTS + j)
        core_copy(j).start()
        return carry

    lax.fori_loop(1, PARTS, first, 0)

    ycopies = [
        remote(tcol.at[0], tcol.at[4 - t], ty_s.at[t], ty_r.at[4 - t], device(x, (y + t) % 4, z, core))
        for t in range(1, 4)
    ]
    for copy in ycopies:
        copy.start()

    starts = [(core * PARTS + q) * PART for q in range(PARTS)]
    offsets = [[s] for s in starts]

    def exchange(q, s):
        size = PART >> (s + 1)
        to, keep = ends[orders[q][s]]
        here = offsets[q][s]
        base = q * PART + PART - (PART >> s)
        copy = remote(
            packed.at[rows(here + (1 - keep) * size, size)], landed.at[pl.ds(base, size)],
            ex_s.at[s * 4 + q], ex_r.at[s * 4 + q], to,
        )
        offsets[q].append(here + keep * size)
        return copy, base, size

    flying = []
    for q in range(PARTS):
        block_row(core * PARTS + q)
        core_copy(q).wait()
        packed[rows(starts[q], PART), :] += from_core[q * PART : (q + 1) * PART, :]
        flying.append(exchange(q, 0))
        flying[q][0].start()

    for copy in ycopies:
        copy.wait()
    for t in range(4):
        tsrc[rows(((y + t) % 4) * 8, 8), :] = tcol[t]
    tz[z] = tsrc[...].astype(BF16)

    def target_copy(t):
        return remote(tz.at[z], tz.at[z], tz_s.at[t], tz_r.at[z], device(x, y, (z + t) % NZ, core))

    def target_start(t, carry):
        target_copy(t).start()
        return carry

    lax.fori_loop(1, NZ, target_start, 0)

    for s in range(4):
        for q in range(PARTS):
            copy, base, size = flying[q]
            copy.wait()
            packed[rows(offsets[q][s + 1], size), :] += landed[base : base + size, :]
            if s < 3:
                flying[q] = exchange(q, s + 1)
                flying[q][0].start()
            else:
                block = packed[rows(offsets[q][4], size), :]
                for m in range(4):
                    zsrc[q * 4 + m] = block[m * PIECE : (m + 1) * PIECE, :]

    def z_copy(t):
        other = (z + t) % NZ
        return remote(zsrc.at[other], zland.at[z], z_s.at[t], z_r.at[z], device(x, y, other, core))

    def z_start(t, carry):
        z_copy(t).start()
        return carry

    lax.fori_loop(1, NZ, z_start, 0)
    zland[z] = zsrc[z]

    def z_wait(t, carry):
        other = (z + t) % NZ
        z_copy(t).wait_send()
        remote(zsrc.at[other], zland.at[other], z_s.at[t], z_r.at[other], sibling).wait_recv()
        return carry

    lax.fori_loop(1, NZ, z_wait, 0)
    total = zland[0]
    for k in range(1, NZ):
        total = total + zland[k]
    zout[z] = total

    def za_copy(t):
        return remote(zout.at[z], zout.at[z], za_s.at[t], za_r.at[z], device(x, y, (z + t) % NZ, core))

    def za_start(t, carry):
        za_copy(t).start()
        return carry

    lax.fori_loop(1, NZ, za_start, 0)

    def za_wait(t, carry):
        other = (z + t) % NZ
        za_copy(t).wait_send()
        remote(zout.at[z], zout.at[other], za_s.at[t], za_r.at[other], sibling).wait_recv()
        return carry

    lax.fori_loop(1, NZ, za_wait, 0)

    def spread(q, s):
        size = PART >> (s + 1)
        to, keep = ends[orders[q][s]]
        mine = offsets[q][s + 1]
        where = out.at[rows(mine, size)]
        theirs = out.at[rows(offsets[q][s] + (1 - keep) * size, size)]
        send = remote(where, where, ag_s.at[s * 4 + q], ag_r.at[s * 4 + q], to)
        recv = remote(theirs, theirs, ag_s.at[s * 4 + q], ag_r.at[s * 4 + q], to)
        return send, recv

    def core_spread(q, who):
        where = out.at[rows((who * PARTS + q) * PART, PART)]
        return remote(where, where, cag_s.at[q], cag_r.at[q], sibling)

    moving = []
    for q in range(PARTS):
        block = jnp.concatenate([zout[q * 4 + m] for m in range(4)], axis=0)
        out[rows(offsets[q][4], PART // 16), :] = block
        moving.append(spread(q, 3))
        moving[q][0].start()
    for s in range(3, -1, -1):
        for q in range(PARTS):
            send, recv = moving[q]
            send.wait_send()
            recv.wait_recv()
            if s > 0:
                moving[q] = spread(q, s - 1)
                moving[q][0].start()
            else:
                core_spread(q, core).start()

    def target_wait(t, carry):
        other = (z + t) % NZ
        target_copy(t).wait_send()
        remote(tz.at[z], tz.at[other], tz_s.at[t], tz_r.at[other], sibling).wait_recv()
        return carry

    lax.fori_loop(1, NZ, target_wait, 0)
    for q in range(PARTS):
        core_spread(q, core).wait_send()
        core_spread(q, 1 - core).wait_recv()


def solve(scale, damping, packed, tz, out, high, low, wide_t, sol, res, way, diag):
    eye = lax.broadcasted_iota(jnp.int32, (TILE, TILE), 0) == lax.broadcasted_iota(jnp.int32, (TILE, TILE), 1)

    def tile(i, d):
        start = (i * KEPT + d) * TILE
        return packed[start : start + TILE, :]

    for i in range(BLOCKS):
        diag[:, i * TILE : (i + 1) * TILE] = jnp.sum(jnp.where(eye, tile(i, 0), 0.0), axis=0, keepdims=True)
    shift = jnp.sum(diag[...], axis=1, keepdims=True) * (damping / WIDTH)
    diag[...] = 1.0 / (diag[...] + shift)

    def put(i, j, values):
        top = values.astype(BF16)
        at = (slice(i * TILE, (i + 1) * TILE), slice(j * TILE, (j + 1) * TILE))
        high[at] = top
        low[at] = (values - top.astype(F32)).astype(BF16)

    for i in range(BLOCKS):
        for d in range(KEPT):
            values = tile(i, d)
            j = (i + d) % BLOCKS
            if d == 0:
                values = values + jnp.where(eye, shift, 0.0)
            put(i, j, values)
            if 0 < d < KEPT - 1:
                put(j, i, values.T)

    wide_t[...] = tz[...].astype(F32)
    for k in range(8):
        for zl in range(4):
            for yy in range(4):
                at = zl * 16 + yy * 4
                res[at : at + 4, k * TILE : (k + 1) * TILE] = wide_t[pl.ds(zl * 32 + yy * 8 + k, 4, stride=128), :]

    inverse = diag[...]
    start = res[...] * inverse
    way[...] = start
    sol[...] = jnp.zeros_like(sol)
    norm = jnp.sum(res[...] * start, axis=1, keepdims=True)
    bound = norm * (TOL * TOL)

    def unfinished(carry):
        step, norm, left = carry
        return jnp.logical_and(step < MAX_STEPS, left > 0.0)

    def advance(carry):
        step, norm, left = carry
        p = way[...]
        top = p.astype(BF16)
        rest = (p - top.astype(F32)).astype(BF16)
        both = jnp.dot(jnp.concatenate([top, rest], axis=0), high[...], preferred_element_type=F32)
        image = both[:RIGHTS] + both[RIGHTS:] + jnp.dot(top, low[...], preferred_element_type=F32)
        curve = jnp.sum(p * image, axis=1, keepdims=True)
        alpha = jnp.where(curve > 0.0, norm / jnp.where(curve > 0.0, curve, 1.0), 0.0)
        sol[...] += alpha * p
        r = res[...] - alpha * image
        res[...] = r
        zed = r * inverse
        fresh = jnp.sum(r * zed, axis=1, keepdims=True)
        beta = jnp.where(norm > 0.0, fresh / jnp.where(norm > 0.0, norm, 1.0), 0.0)
        way[...] = zed + beta * p
        return step + 1, fresh, jnp.max(fresh - bound)

    lax.while_loop(unfinished, advance, (jnp.int32(0), norm, jnp.max(norm - bound)))
    out[...] = (sol[...] * scale).astype(BF16)


def spread_rows(mine, out, near_s, near_r, far_s, far_r, core_s, core_r, own_s):
    x, y, z, core = position()
    sibling = device(x, y, z, 1 - core)
    even, odd = even_pair(x), odd_pair(x)
    to_even, to_odd = device(even, y, z, core), device(odd, y, z, core)
    far = even_pair(odd)
    barrier = greet([sibling, to_even, to_odd])
    own = pltpu.make_async_copy(mine, out.at[x, :, core], own_s)
    own.start()
    pl.semaphore_wait(barrier, 3)
    own.wait()
    half = WIDTH // 2
    left, right = pl.ds(0, half), pl.ds(half, half)

    def block(xx, cc):
        return out.at[xx, :, cc]

    def part(xx, cc, cols):
        return out.at[xx, :, cc, :, cols]

    near_even = remote(block(x, core), block(x, core), near_s.at[0], near_r.at[0], to_even)
    near_odd = remote(block(x, core), block(x, core), near_s.at[1], near_r.at[1], to_odd)
    near_even.start()
    near_odd.start()

    def share(n, xx, who):
        return remote(block(xx, who), block(xx, who), core_s.at[n], core_r.at[n], sibling)

    share(0, x, core).start()
    near_even.wait_send()
    remote(block(even, core), block(even, core), near_s.at[0], near_r.at[0], to_even).wait_recv()
    on_odd = remote(part(even, core, left), part(even, core, left), far_s.at[0], far_r.at[0], to_odd)
    on_odd.start()
    share(1, even, core).start()
    near_odd.wait_send()
    remote(block(odd, core), block(odd, core), near_s.at[1], near_r.at[1], to_odd).wait_recv()
    on_even = remote(part(odd, core, right), part(odd, core, right), far_s.at[1], far_r.at[1], to_even)
    on_even.start()
    share(2, odd, core).start()
    on_odd.wait_send()
    remote(part(far, core, left), part(far, core, left), far_s.at[0], far_r.at[0], to_odd).wait_recv()
    on_even.wait_send()
    remote(part(far, core, right), part(far, core, right), far_s.at[1], far_r.at[1], to_even).wait_recv()
    share(3, far, core).start()
    for n, xx in enumerate((x, even, odd, far)):
        share(n, xx, core).wait_send()
        share(n, xx, 1 - core).wait_recv()


def on_device(features, targets):
    dma = pltpu.SemaphoreType.DMA
    vmem = pl.BlockSpec(memory_space=pltpu.VMEM)
    packed, tz = pl.pallas_call(
        gram_sum,
        name="gram_sum",
        out_shape=(
            jax.ShapeDtypeStruct((BLOCKS * PART, TILE), F32),
            jax.ShapeDtypeStruct((NZ, 32, TILE), BF16),
        ),
        in_specs=[vmem, vmem],
        out_specs=(vmem, vmem),
        scratch_shapes=[
            pltpu.VMEM((features.shape[0], WIDTH + WIDTH // 2), BF16),
            pltpu.VMEM((BLOCKS * PART, TILE), F32),
            pltpu.VMEM((PARTS * PART, TILE), F32),
            pltpu.VMEM((PARTS * PART, TILE), F32),
            pltpu.VMEM((NZ, PIECE, TILE), F32),
            pltpu.VMEM((NZ, PIECE, TILE), F32),
            pltpu.VMEM((NZ, PIECE, TILE), F32),
            pltpu.VMEM((4, 8, TILE), F32),
            pltpu.VMEM((32, TILE), F32),
            dma((4,)), dma((4,)), dma((4,)), dma((4,)),
            dma((16,)), dma((16,)), dma((16,)), dma((16,)),
            dma((16,)), dma((16,)), dma((16,)), dma((16,)),
            dma((4,)), dma((4,)), dma((16,)), dma((16,)),
        ],
        compiler_params=pltpu.CompilerParams(
            collective_id=0, has_side_effects=True, vmem_limit_bytes=40 * 2**20
        ),
    )(features, targets)

    total_rows = features.shape[0] * lax.axis_size("loop") * lax.axis_size("group")
    precond = pl.pallas_call(
        functools.partial(solve, total_rows / WIDTH**0.5, 0.05),
        name="solve",
        out_shape=jax.ShapeDtypeStruct((RIGHTS, WIDTH), BF16),
        in_specs=[vmem, vmem],
        out_specs=vmem,
        scratch_shapes=[
            pltpu.VMEM((WIDTH, WIDTH), BF16),
            pltpu.VMEM((WIDTH, WIDTH), BF16),
            pltpu.VMEM((NZ * 32, TILE), F32),
            pltpu.VMEM((RIGHTS, WIDTH), F32),
            pltpu.VMEM((RIGHTS, WIDTH), F32),
            pltpu.VMEM((RIGHTS, WIDTH), F32),
            pltpu.VMEM((1, WIDTH), F32),
        ],
        compiler_params=pltpu.CompilerParams(vmem_limit_bytes=40 * 2**20),
    )(packed, tz.reshape(NZ * 32, TILE))

    everyone = pl.pallas_call(
        spread_rows,
        name="spread_rows",
        out_shape=jax.ShapeDtypeStruct((4, 4, 2, 16, WIDTH), BF16),
        in_specs=[vmem],
        out_specs=vmem,
        scratch_shapes=[dma((2,)), dma((2,)), dma((2,)), dma((2,)), dma((4,)), dma((4,)), dma],
        compiler_params=pltpu.CompilerParams(
            collective_id=1, has_side_effects=True, vmem_limit_bytes=16 * 2**20
        ),
    )(precond.reshape(4, 16, WIDTH))

    return lax.dot_general(
        features,
        everyone.reshape(512, WIDTH),
        (((1,), (1,)), ((), ())),
        preferred_element_type=F32,
    )


def solution(mesh):
    return jax.shard_map(
        on_device,
        mesh=mesh,
        in_specs=(P(("loop", "group"), None), P(("loop", "group"), None)),
        out_specs=P(("loop", "group"), None),
        check_vma=False,
    )
```

```python
import functools

import jax
import jax.numpy as jnp
from jax import lax
from jax.experimental import pallas as pl
from jax.experimental.pallas import tpu as pltpu
from jax.sharding import PartitionSpec as P

WIDTH = 1024
TILE = 128
BLOCKS = WIDTH // TILE
UPPER, LOWER = 5, 4
UNIT = (UPPER + LOWER) * TILE
QUARTER = UNIT // 4
SIXTEENTH = UNIT // 16
NZ = 16
PIECE = SIXTEENTH * 2 // NZ
RIGHTS = 256
TOL = 1e-5
ROUGH = 2e-3
MAX_STEPS = 4096
MESH = pl.DeviceIdType.MESH
F32 = jnp.float32
BF16 = jnp.bfloat16


def position():
    loop = lax.axis_index("loop")
    group = lax.axis_index("group")
    x = loop // 8
    y = group // 4
    z = (group % 4) * 4 + (loop // 2) % 4
    return x, y, z, loop % 2


def device(x, y, z, core):
    return (x * 8 + (z % 4) * 2 + core, y * 4 + z // 4)


def remote(src, dst, send, recv, to):
    return pltpu.make_async_remote_copy(
        src_ref=src, dst_ref=dst, send_sem=send, recv_sem=recv, device_id=to, device_id_type=MESH
    )


def signal(sem, to):
    pl.semaphore_signal(sem, inc=1, device_id=to, device_id_type=MESH)


def rows(start, size, unit=8):
    return pl.ds(pl.multiple_of(start, unit), size)


def far_first(k):
    return 8 + ((k + 1) // 2) * (1 - 2 * (k % 2))


def gram_sum(
    feat, tgt, out, rights, wide, packed, from_core, land1, land2, zsrc, zland, zout,
    line, tsrc, tz, yblock, ywide,
    load_s, core_s, core_r, e1_s, e1_r, e2_s, e2_r, z_s, z_r, za_s, za_r,
    g2_s, g2_r, g1_s, g1_r, cag_s, cag_r, tz_s, tz_r, ty_s, ty_r, tx_s, tx_r, known,
):
    x, y, z, core = position()
    sibling = device(x, y, z, 1 - core)

    def on_x(t):
        return device((x + t) % 4, y, z, core)

    def on_y(t):
        return device(x, (y + t) % 4, z, core)

    def on_z(t):
        return device(x, y, (z + t) % NZ, core)

    def over(axis, t):
        return on_x(t) if axis == 0 else on_y(t)

    here = (x, y)
    ring = (2, 1, 3)

    barrier = pltpu.get_barrier_semaphore()
    signal(barrier, sibling)
    for t in (1, 2, 3):
        signal(barrier, on_x(t))
        signal(barrier, on_y(t))
    signal(barrier, on_z(1))
    signal(barrier, on_z(NZ - 1))

    loads = [
        pltpu.make_async_copy(feat, wide.at[:, pl.ds(0, WIDTH)], load_s.at[0]),
        pltpu.make_async_copy(feat.at[:, pl.ds(0, WIDTH // 2)], wide.at[:, pl.ds(WIDTH, WIDTH // 2)], load_s.at[1]),
        pltpu.make_async_copy(tgt, line, load_s.at[2]),
    ]
    for load in loads:
        load.start()
    for load in loads:
        load.wait()

    def unit_gram(u):
        for i, kept, base in ((u, UPPER, u * UNIT), (u + 4, LOWER, u * UNIT + UPPER * TILE)):
            left = wide[:, rows(i * TILE, TILE, TILE)]
            span = wide[:, rows(i * TILE, kept * TILE, TILE)]
            product = lax.dot_general(left, span, (((0,), (0,)), ((), ())), preferred_element_type=F32)
            for d in range(kept):
                packed[rows(base + d * TILE, TILE), :] = product[:, d * TILE : (d + 1) * TILE]

    def core_copy(j):
        return remote(
            packed.at[rows((2 * (1 - core) + j) * UNIT, UNIT)], from_core.at[pl.ds(j * UNIT, UNIT)],
            core_s.at[j], core_r.at[j], sibling,
        )

    unit_gram(2 * (1 - core))
    pl.semaphore_wait(barrier, 9)
    core_copy(0).start()
    signal(known.at[0], on_z(1))
    signal(known.at[0], on_z(NZ - 1))
    unit_gram(2 * (1 - core) + 1)
    core_copy(1).start()

    units = [(2 * core + j) * UNIT for j in range(2)]
    quarters = [units[j] + here[j] * QUARTER for j in range(2)]
    parts = [quarters[j] + here[1 - j] * SIXTEENTH for j in range(2)]

    def first(j, t):
        at = units[j] + ((here[j] + t) % 4) * QUARTER
        return remote(
            packed.at[rows(at, QUARTER)], land1.at[j, t - 1], e1_s.at[j * 4 + t], e1_r.at[j * 4 + t], over(j, t)
        )

    def second(j, t):
        at = quarters[j] + ((here[1 - j] + t) % 4) * SIXTEENTH
        return remote(
            packed.at[rows(at, SIXTEENTH)], land2.at[j, t - 1], e2_s.at[j * 4 + t], e2_r.at[j * 4 + t], over(1 - j, t)
        )

    for j in range(2):
        unit_gram(2 * core + j)
        core_copy(j).wait()
        packed[rows(units[j], UNIT), :] += from_core[j * UNIT : (j + 1) * UNIT, :]
        for t in ring:
            first(j, t).start()

    for k in range(8):
        tsrc[k : k + 1, :] = line[:, k * TILE : (k + 1) * TILE].astype(F32)
    tz[rows(z * 8, 8), :] = tsrc[...]
    pl.semaphore_wait(known.at[0], 2)
    signal(known.at[1], on_z(2))
    signal(known.at[1], on_z(NZ - 2))
    pl.semaphore_wait(known.at[1], 2)
    signal(known.at[2], on_z(4))
    signal(known.at[2], on_z(NZ - 4))

    for j in range(2):
        for t in ring:
            first(j, t).wait()
        packed[rows(quarters[j], QUARTER), :] += land1[j, 0] + land1[j, 1] + land1[j, 2]
        for t in ring:
            second(j, t).start()

    pl.semaphore_wait(known.at[2], 2)

    def all_z(copy):
        def body(k, carry):
            copy(far_first(k)).start()
            return carry

        lax.fori_loop(0, NZ - 1, body, 0)

    def end_z(copy, landing, recv):
        def body(k, carry):
            t = far_first(k)
            copy(t).wait_send()
            other = (z + t) % NZ
            ref = landing(other)
            remote(ref, ref, recv.at[other], recv.at[other], sibling).wait_recv()
            return carry

        lax.fori_loop(0, NZ - 1, body, 0)

    def target_row(k):
        return tz.at[rows(k * 8, 8)]

    def t_copy(t):
        return remote(target_row(z), target_row(z), tz_s.at[t], tz_r.at[z], on_z(t))

    all_z(t_copy)

    for j in range(2):
        for t in ring:
            second(j, t).wait()
        packed[rows(parts[j], SIXTEENTH), :] += land2[j, 0] + land2[j, 1] + land2[j, 2]
        block = packed[rows(parts[j], SIXTEENTH), :]
        for m in range(8):
            zsrc[j * 8 + m] = block[m * PIECE : (m + 1) * PIECE, :]

    def z_copy(t):
        return remote(zsrc.at[(z + t) % NZ], zland.at[z], z_s.at[t], z_r.at[z], on_z(t))

    all_z(z_copy)
    zland[z] = zsrc[z]

    end_z(t_copy, target_row, tz_r)
    for k in range(8):
        for low in range(4):
            ywide[low * 4 : low * 4 + 4, k * TILE : (k + 1) * TILE] = tz[pl.ds(low * 8 + k, 4, stride=32), :]
    yblock[y] = ywide[0:16, :].astype(BF16)

    def y_copy(t):
        return remote(yblock.at[y], yblock.at[y], ty_s.at[t], ty_r.at[t], on_y(t))

    for t in ring:
        y_copy(t).start()

    end_z(z_copy, lambda k: zland.at[k], z_r)
    total = zland[0]
    for k in range(1, NZ):
        total = total + zland[k]
    zout[z] = total

    def za_copy(t):
        return remote(zout.at[z], zout.at[z], za_s.at[t], za_r.at[z], on_z(t))

    all_z(za_copy)

    for t in ring:
        y_copy(t).wait_send()
        ref = yblock.at[(y + 4 - t) % 4]
        remote(ref, ref, ty_s.at[t], ty_r.at[t], sibling).wait_recv()
    for yy in range(4):
        block = yblock[yy].astype(F32)
        for low in range(4):
            ywide[low * 16 + yy * 4 : low * 16 + yy * 4 + 4, :] = block[low * 4 : low * 4 + 4, :]
    mine = rights.at[rows(x * 64, 64, 64)]
    rights[rows(x * 64, 64, 64), :] = ywide[...].astype(BF16)

    def x_copy(t):
        return remote(mine, mine, tx_s.at[t], tx_r.at[t], on_x(t))

    for t in ring:
        x_copy(t).start()

    end_z(za_copy, lambda k: zout.at[k], za_r)

    def gather(j, t, stage):
        if stage == 2:
            mine, size, axis = parts[j], SIXTEENTH, 1 - j
            theirs = quarters[j] + ((here[axis] + 4 - t) % 4) * SIXTEENTH
            send, recv = g2_s, g2_r
        else:
            mine, size, axis = quarters[j], QUARTER, j
            theirs = units[j] + ((here[axis] + 4 - t) % 4) * QUARTER
            send, recv = g1_s, g1_r
        a, b = out.at[rows(mine, size)], out.at[rows(theirs, size)]
        n = j * 4 + t
        return (
            remote(a, a, send.at[n], recv.at[n], over(axis, t)),
            remote(b, b, send.at[n], recv.at[n], over(axis, t)),
        )

    def core_gather(j, t, who):
        at = (2 * who + j) * UNIT + ((here[j] + 4 - t) % 4) * QUARTER
        ref = out.at[rows(at, QUARTER)]
        return remote(ref, ref, cag_s.at[j * 4 + t], cag_r.at[j * 4 + t], sibling)

    for j in range(2):
        out[rows(parts[j], SIXTEENTH), :] = jnp.concatenate([zout[j * 8 + m] for m in range(8)], axis=0)
        for t in ring:
            gather(j, t, 2)[0].start()
    for j in range(2):
        for t in ring:
            send, recv = gather(j, t, 2)
            send.wait_send()
            recv.wait_recv()
        for t in ring:
            gather(j, t, 1)[0].start()
        core_gather(j, 0, core).start()
    for t in (1, 3, 2):
        for j in range(2):
            gather(j, t, 1)[1].wait_recv()
            core_gather(j, t, core).start()
    for t in ring:
        x_copy(t).wait_send()
        ref = rights.at[rows(((x + 4 - t) % 4) * 64, 64, 64)]
        remote(ref, ref, tx_s.at[t], tx_r.at[t], sibling).wait_recv()
        for j in range(2):
            gather(j, t, 1)[0].wait_send()
    for t in (0, 1, 3, 2):
        for j in range(2):
            core_gather(j, t, core).wait_send()
            core_gather(j, t, 1 - core).wait_recv()


def solve(scale, damping, packed, rights, out, high, low, least, sol, res, way, image, diag):
    eye = lax.broadcasted_iota(jnp.int32, (TILE, TILE), 0) == lax.broadcasted_iota(jnp.int32, (TILE, TILE), 1)

    def tile(i, d):
        start = (i % 4) * UNIT + (i // 4) * UPPER * TILE + d * TILE
        return packed[start : start + TILE, :]

    def kept(i):
        return UPPER if i < 4 else LOWER

    squares = jnp.zeros((TILE, TILE), F32)
    for i in range(BLOCKS):
        values = tile(i, 0)
        diag[:, i * TILE : (i + 1) * TILE] = jnp.sum(jnp.where(eye, values, 0.0), axis=0, keepdims=True)
    shift = jnp.sum(diag[...], axis=1, keepdims=True) * (damping / WIDTH)
    per_shift = 1.0 / shift
    diag[...] = 1.0 / (diag[...] + shift)

    def spot(i, j):
        return slice(i * TILE, (i + 1) * TILE), slice(j * TILE, (j + 1) * TILE)

    for i in range(BLOCKS):
        for d in range(kept(i)):
            j = (i + d) % BLOCKS
            values = tile(i, d)
            if d == 0:
                off = jnp.where(eye, 0.0, values) * per_shift
                squares = squares + 0.5 * off * off
                values = values + jnp.where(eye, shift, 0.0)
            else:
                off = values * per_shift
                squares = squares + off * off
            top = values.astype(BF16)
            rest = (values - top.astype(F32)).astype(BF16)
            high[spot(i, j)] = top
            low[spot(i, j)] = rest
            if d:
                high[spot(j, i)] = top.T
                low[spot(j, i)] = rest.T
    hard = 2.0 * jnp.sum(squares) > 256.0**2

    @pl.when(hard)
    def _():
        for i in range(BLOCKS):
            for d in range(kept(i)):
                j = (i + d) % BLOCKS
                values = tile(i, d)
                if d == 0:
                    values = values + jnp.where(eye, shift, 0.0)
                rest = values - values.astype(BF16).astype(F32)
                last = (rest - rest.astype(BF16).astype(F32)).astype(BF16)
                least[spot(i, j)] = last
                if d:
                    least[spot(j, i)] = last.T

    inverse = diag[...]
    b = rights[...].astype(F32)
    res[...] = b
    start = b * inverse
    way[...] = start.astype(BF16)
    sol[...] = jnp.zeros_like(sol)
    norm = jnp.sum(b * start, axis=1, keepdims=True)
    bound = norm * (TOL * TOL)
    rough = norm * (ROUGH * ROUGH)

    def unfinished(carry):
        step, norm, left, more = carry
        return jnp.logical_and(step < MAX_STEPS, left > 0.0)

    def advance(carry):
        step, norm, left, more = carry
        image[...] = jnp.dot(way[...], high[...], preferred_element_type=F32)

        @pl.when(jnp.logical_or(hard, more > 0.0))
        def _():
            image[...] += jnp.dot(way[...], low[...], preferred_element_type=F32)

        @pl.when(hard)
        def _():
            image[...] += jnp.dot(way[...], least[...], preferred_element_type=F32)

        p = way[...].astype(F32)
        q = image[...]
        curve = jnp.sum(p * q, axis=1, keepdims=True)
        alpha = jnp.where(curve > 0.0, norm / jnp.where(curve > 0.0, curve, 1.0), 0.0)
        sol[...] += alpha * p
        r = res[...] - alpha * q
        res[...] = r
        zed = r * inverse
        fresh = jnp.sum(r * zed, axis=1, keepdims=True)
        beta = jnp.where(norm > 0.0, fresh / jnp.where(norm > 0.0, norm, 1.0), 0.0)
        way[...] = (zed + beta * p).astype(BF16)
        return step + 1, fresh, jnp.max(fresh - bound), jnp.max(fresh - rough)

    lax.while_loop(unfinished, advance, (jnp.int32(0), norm, jnp.max(norm - bound), jnp.max(norm - rough)))
    out[...] = (sol[...] * scale).astype(BF16)


def swap_rows(mine, out, own_s, send, recv):
    x, y, z, core = position()
    sibling = device(x, y, z, 1 - core)
    barrier = pltpu.get_barrier_semaphore()
    signal(barrier, sibling)
    own = pltpu.make_async_copy(mine, out.at[:, core], own_s)
    own.start()
    pl.semaphore_wait(barrier, 1)
    copy = remote(mine, out.at[:, core], send, recv, sibling)
    copy.start()
    own.wait()
    copy.wait_send()
    theirs = out.at[:, 1 - core]
    remote(theirs, theirs, send, recv, sibling).wait_recv()


def score(feat, pre, out):
    out[...] = lax.dot_general(feat[...], pre[...], (((1,), (1,)), ((), ())), preferred_element_type=F32)


def on_device(features, targets):
    dma = pltpu.SemaphoreType.DMA
    vmem = pl.BlockSpec(memory_space=pltpu.VMEM)
    anywhere = pl.BlockSpec(memory_space=pl.ANY)
    packed, rights = pl.pallas_call(
        gram_sum,
        name="gram_sum",
        out_shape=(
            jax.ShapeDtypeStruct((4 * UNIT, TILE), F32),
            jax.ShapeDtypeStruct((RIGHTS, WIDTH), BF16),
        ),
        in_specs=[anywhere, anywhere],
        out_specs=(vmem, vmem),
        scratch_shapes=[
            pltpu.VMEM((features.shape[0], WIDTH + WIDTH // 2), BF16),
            pltpu.VMEM((4 * UNIT, TILE), F32),
            pltpu.VMEM((2 * UNIT, TILE), F32),
            pltpu.VMEM((2, 3, QUARTER, TILE), F32),
            pltpu.VMEM((2, 3, SIXTEENTH, TILE), F32),
            pltpu.VMEM((NZ, PIECE, TILE), F32),
            pltpu.VMEM((NZ, PIECE, TILE), F32),
            pltpu.VMEM((NZ, PIECE, TILE), F32),
            pltpu.VMEM((1, WIDTH), BF16),
            pltpu.VMEM((8, TILE), F32),
            pltpu.VMEM((NZ * 8, TILE), F32),
            pltpu.VMEM((4, 16, WIDTH), BF16),
            pltpu.VMEM((64, WIDTH), F32),
            dma((3,)), dma((2,)), dma((2,)),
            dma((8,)), dma((8,)), dma((8,)), dma((8,)),
            dma((NZ,)), dma((NZ,)), dma((NZ,)), dma((NZ,)),
            dma((8,)), dma((8,)), dma((8,)), dma((8,)), dma((8,)), dma((8,)),
            dma((NZ,)), dma((NZ,)), dma((4,)), dma((4,)), dma((4,)), dma((4,)),
            pltpu.SemaphoreType.REGULAR((3,)),
        ],
        compiler_params=pltpu.CompilerParams(
            collective_id=0, has_side_effects=True, vmem_limit_bytes=40 * 2**20
        ),
    )(features, targets)

    total_rows = features.shape[0] * lax.axis_size("loop") * lax.axis_size("group")
    precond = pl.pallas_call(
        functools.partial(solve, total_rows / WIDTH**0.5, 0.05),
        name="solve",
        out_shape=jax.ShapeDtypeStruct((RIGHTS, WIDTH), BF16),
        in_specs=[vmem, vmem],
        out_specs=vmem,
        scratch_shapes=[
            pltpu.VMEM((WIDTH, WIDTH), BF16),
            pltpu.VMEM((WIDTH, WIDTH), BF16),
            pltpu.VMEM((WIDTH, WIDTH), BF16),
            pltpu.VMEM((RIGHTS, WIDTH), F32),
            pltpu.VMEM((RIGHTS, WIDTH), F32),
            pltpu.VMEM((RIGHTS, WIDTH), BF16),
            pltpu.VMEM((RIGHTS, WIDTH), F32),
            pltpu.VMEM((1, WIDTH), F32),
        ],
        compiler_params=pltpu.CompilerParams(vmem_limit_bytes=40 * 2**20),
    )(packed, rights)

    everyone = pl.pallas_call(
        swap_rows,
        name="swap_rows",
        out_shape=jax.ShapeDtypeStruct((16, 2, 16, WIDTH), BF16),
        in_specs=[vmem],
        out_specs=vmem,
        scratch_shapes=[dma, dma, dma],
        compiler_params=pltpu.CompilerParams(
            collective_id=1, has_side_effects=True, vmem_limit_bytes=16 * 2**20
        ),
    )(precond.reshape(16, 16, WIDTH))

    return pl.pallas_call(
        score,
        name="score",
        grid=(4,),
        out_shape=jax.ShapeDtypeStruct((features.shape[0], 512), F32),
        in_specs=[
            pl.BlockSpec((features.shape[0], WIDTH), lambda i: (0, 0)),
            pl.BlockSpec((128, WIDTH), lambda i: (i, 0)),
        ],
        out_specs=pl.BlockSpec((features.shape[0], 128), lambda i: (0, i)),
        compiler_params=pltpu.CompilerParams(vmem_limit_bytes=16 * 2**20),
    )(features, everyone.reshape(512, WIDTH))


def solution(mesh):
    return jax.shard_map(
        on_device,
        mesh=mesh,
        in_specs=(P(("loop", "group"), None), P(("loop", "group"), None)),
        out_specs=P(("loop", "group"), None),
        check_vma=False,
    )
```

```python
import functools

import jax
import jax.numpy as jnp
from jax import lax
from jax.experimental import pallas as pl
from jax.experimental.pallas import tpu as pltpu
from jax.sharding import PartitionSpec as P

WIDTH = 1024
TILE = 128
BLOCKS = WIDTH // TILE
UPPER, LOWER = 5, 4
UNIT = (UPPER + LOWER) * TILE
QUARTER = UNIT // 4
SIXTEENTH = UNIT // 16
NZ = 16
PIECE = SIXTEENTH * 2 // NZ
RIGHTS = 256
TOL = 1e-4
ROUGH = 1e-2
MAX_STEPS = 4096
CHUNK = 16
MESH = pl.DeviceIdType.MESH
F32 = jnp.float32
BF16 = jnp.bfloat16


def position():
    loop = lax.axis_index("loop")
    group = lax.axis_index("group")
    x = loop // 8
    y = group // 4
    z = (group % 4) * 4 + (loop // 2) % 4
    return x, y, z, loop % 2


def device(x, y, z, core):
    return (x * 8 + (z % 4) * 2 + core, y * 4 + z // 4)


def remote(src, dst, send, recv, to):
    return pltpu.make_async_remote_copy(
        src_ref=src, dst_ref=dst, send_sem=send, recv_sem=recv, device_id=to, device_id_type=MESH
    )


def signal(sem, to):
    pl.semaphore_signal(sem, inc=1, device_id=to, device_id_type=MESH)


def rows(start, size, unit=8):
    return pl.ds(pl.multiple_of(start, unit), size)


def far_first(k):
    return 8 + ((k + 1) // 2) * (1 - 2 * (k % 2))


def gram_sum(
    feat, tgt, out, rights, wide, packed, from_core, land1, land2, zsrc, zland, zout,
    line, tsrc, tz, yblock, ywide,
    load_s, core_s, core_r, e1_s, e1_r, e2_s, e2_r, z_s, z_r, za_s, za_r,
    g2_s, g2_r, g1_s, g1_r, cag_s, cag_r, tz_s, tz_r, ty_s, ty_r, tx_s, tx_r, known,
):
    x, y, z, core = position()
    sibling = device(x, y, z, 1 - core)

    def on_x(t):
        return device((x + t) % 4, y, z, core)

    def on_y(t):
        return device(x, (y + t) % 4, z, core)

    def on_z(t):
        return device(x, y, (z + t) % NZ, core)

    def over(axis, t):
        return on_x(t) if axis == 0 else on_y(t)

    here = (x, y)
    ring = (2, 1, 3)

    barrier = pltpu.get_barrier_semaphore()
    signal(barrier, sibling)
    for t in (1, 2, 3):
        signal(barrier, on_x(t))
        signal(barrier, on_y(t))
    signal(barrier, on_z(1))
    signal(barrier, on_z(NZ - 1))

    loads = [
        pltpu.make_async_copy(feat, wide.at[:, pl.ds(0, WIDTH)], load_s.at[0]),
        pltpu.make_async_copy(feat.at[:, pl.ds(0, WIDTH // 2)], wide.at[:, pl.ds(WIDTH, WIDTH // 2)], load_s.at[1]),
        pltpu.make_async_copy(tgt, line, load_s.at[2]),
    ]
    for load in loads:
        load.start()
    for load in loads:
        load.wait()

    def unit_gram(u):
        for i, kept, base in ((u, UPPER, u * UNIT), (u + 4, LOWER, u * UNIT + UPPER * TILE)):
            left = wide[:, rows(i * TILE, TILE, TILE)]
            span = wide[:, rows(i * TILE, kept * TILE, TILE)]
            product = lax.dot_general(left, span, (((0,), (0,)), ((), ())), preferred_element_type=F32)
            for d in range(kept):
                packed[rows(base + d * TILE, TILE), :] = product[:, d * TILE : (d + 1) * TILE]

    def core_copy(j, t):
        n = j * 4 + t
        return remote(
            packed.at[rows((2 * (1 - core) + j) * UNIT + ((here[j] + t) % 4) * QUARTER, QUARTER)],
            from_core.at[pl.ds(n * QUARTER, QUARTER)], core_s.at[n], core_r.at[n], sibling,
        )

    unit_gram(2 * (1 - core))
    pl.semaphore_wait(barrier, 9)
    core_copy(0, 2).start()
    signal(known.at[0], on_z(1))
    signal(known.at[0], on_z(NZ - 1))
    unit_gram(2 * (1 - core) + 1)
    core_copy(1, 2).start()
    for t in (1, 3, 0):
        for j in range(2):
            core_copy(j, t).start()

    units = [(2 * core + j) * UNIT for j in range(2)]
    quarters = [units[j] + here[j] * QUARTER for j in range(2)]
    parts = [quarters[j] + here[1 - j] * SIXTEENTH for j in range(2)]

    def first(j, t):
        at = units[j] + ((here[j] + t) % 4) * QUARTER
        return remote(
            packed.at[rows(at, QUARTER)], land1.at[j, t - 1], e1_s.at[j * 4 + t], e1_r.at[j * 4 + t], over(j, t)
        )

    def second(j, t):
        at = quarters[j] + ((here[1 - j] + t) % 4) * SIXTEENTH
        return remote(
            packed.at[rows(at, SIXTEENTH)], land2.at[j, t - 1], e2_s.at[j * 4 + t], e2_r.at[j * 4 + t], over(1 - j, t)
        )

    for j in range(2):
        unit_gram(2 * core + j)
    for t in (2, 1, 3, 0):
        for j in range(2):
            n = j * 4 + t
            core_copy(j, t).wait_recv()
            at = units[j] + ((here[j] + t) % 4) * QUARTER
            packed[rows(at, QUARTER), :] += from_core[n * QUARTER : (n + 1) * QUARTER, :]
            if t:
                first(j, t).start()

    for k in range(8):
        tsrc[k : k + 1, :] = line[:, k * TILE : (k + 1) * TILE].astype(F32)
    tz[rows(z * 8, 8), :] = tsrc[...]
    for t in range(4):
        for j in range(2):
            core_copy(j, t).wait_send()
    pl.semaphore_wait(known.at[0], 2)
    signal(known.at[1], on_z(2))
    signal(known.at[1], on_z(NZ - 2))
    pl.semaphore_wait(known.at[1], 2)
    signal(known.at[2], on_z(4))
    signal(known.at[2], on_z(NZ - 4))

    for j in range(2):
        for t in ring:
            first(j, t).wait()
        packed[rows(quarters[j], QUARTER), :] += land1[j, 0] + land1[j, 1] + land1[j, 2]
        for t in ring:
            second(j, t).start()

    pl.semaphore_wait(known.at[2], 2)

    def all_z(copy):
        def body(k, carry):
            copy(far_first(k)).start()
            return carry

        lax.fori_loop(0, NZ - 1, body, 0)

    def end_z(copy, landing, recv):
        def body(k, carry):
            t = far_first(k)
            copy(t).wait_send()
            other = (z + t) % NZ
            ref = landing(other)
            remote(ref, ref, recv.at[other], recv.at[other], sibling).wait_recv()
            return carry

        lax.fori_loop(0, NZ - 1, body, 0)

    def target_row(k):
        return tz.at[rows(k * 8, 8)]

    def t_copy(t):
        return remote(target_row(z), target_row(z), tz_s.at[t], tz_r.at[z], on_z(t))

    all_z(t_copy)

    for j in range(2):
        for t in ring:
            second(j, t).wait()
        packed[rows(parts[j], SIXTEENTH), :] += land2[j, 0] + land2[j, 1] + land2[j, 2]
        block = packed[rows(parts[j], SIXTEENTH), :]
        for m in range(8):
            zsrc[j * 8 + m] = block[m * PIECE : (m + 1) * PIECE, :]

    def z_copy(t):
        return remote(zsrc.at[(z + t) % NZ], zland.at[z], z_s.at[t], z_r.at[z], on_z(t))

    all_z(z_copy)
    zland[z] = zsrc[z]

    end_z(t_copy, target_row, tz_r)
    for k in range(8):
        for low in range(4):
            ywide[low * 4 : low * 4 + 4, k * TILE : (k + 1) * TILE] = tz[pl.ds(low * 8 + k, 4, stride=32), :]
    yblock[y] = ywide[0:16, :].astype(BF16)

    def y_copy(t):
        return remote(yblock.at[y], yblock.at[y], ty_s.at[t], ty_r.at[t], on_y(t))

    for t in ring:
        y_copy(t).start()

    end_z(z_copy, lambda k: zland.at[k], z_r)
    total = zland[0]
    for k in range(1, NZ):
        total = total + zland[k]
    zout[z] = total

    def za_copy(t):
        return remote(zout.at[z], zout.at[z], za_s.at[t], za_r.at[z], on_z(t))

    all_z(za_copy)

    for t in ring:
        y_copy(t).wait_send()
        ref = yblock.at[(y + 4 - t) % 4]
        remote(ref, ref, ty_s.at[t], ty_r.at[t], sibling).wait_recv()
    for yy in range(4):
        block = yblock[yy].astype(F32)
        for low in range(4):
            ywide[low * 16 + yy * 4 : low * 16 + yy * 4 + 4, :] = block[low * 4 : low * 4 + 4, :]
    mine = rights.at[rows(x * 64, 64, 64)]
    rights[rows(x * 64, 64, 64), :] = ywide[...].astype(BF16)

    def x_copy(t):
        return remote(mine, mine, tx_s.at[t], tx_r.at[t], on_x(t))

    for t in ring:
        x_copy(t).start()

    end_z(za_copy, lambda k: zout.at[k], za_r)

    def gather(j, t, stage):
        if stage == 2:
            mine, size, axis = parts[j], SIXTEENTH, 1 - j
            theirs = quarters[j] + ((here[axis] + 4 - t) % 4) * SIXTEENTH
            send, recv = g2_s, g2_r
        else:
            mine, size, axis = quarters[j], QUARTER, j
            theirs = units[j] + ((here[axis] + 4 - t) % 4) * QUARTER
            send, recv = g1_s, g1_r
        a, b = out.at[rows(mine, size)], out.at[rows(theirs, size)]
        n = j * 4 + t
        return (
            remote(a, a, send.at[n], recv.at[n], over(axis, t)),
            remote(b, b, send.at[n], recv.at[n], over(axis, t)),
        )

    def core_gather(j, t, who):
        at = (2 * who + j) * UNIT + ((here[j] + 4 - t) % 4) * QUARTER
        ref = out.at[rows(at, QUARTER)]
        return remote(ref, ref, cag_s.at[j * 4 + t], cag_r.at[j * 4 + t], sibling)

    for j in range(2):
        out[rows(parts[j], SIXTEENTH), :] = jnp.concatenate([zout[j * 8 + m] for m in range(8)], axis=0)
        for t in ring:
            gather(j, t, 2)[0].start()
    for j in range(2):
        for t in ring:
            send, recv = gather(j, t, 2)
            send.wait_send()
            recv.wait_recv()
        core_gather(j, 0, core).start()
        for t in ring:
            gather(j, t, 1)[0].start()
    for t in (1, 3, 2):
        for j in range(2):
            gather(j, t, 1)[1].wait_recv()
            core_gather(j, t, core).start()
    for t in ring:
        x_copy(t).wait_send()
        ref = rights.at[rows(((x + 4 - t) % 4) * 64, 64, 64)]
        remote(ref, ref, tx_s.at[t], tx_r.at[t], sibling).wait_recv()
        for j in range(2):
            gather(j, t, 1)[0].wait_send()
    for t in (0, 1, 3, 2):
        for j in range(2):
            core_gather(j, t, core).wait_send()
            core_gather(j, t, 1 - core).wait_recv()


def solve(scale, damping, packed, rights, out, high, low, least, sol, res, way, image, diag, norm_ref, curves):
    eye = lax.broadcasted_iota(jnp.int32, (TILE, TILE), 0) == lax.broadcasted_iota(jnp.int32, (TILE, TILE), 1)

    def tile(i, d):
        start = (i % 4) * UNIT + (i // 4) * UPPER * TILE + d * TILE
        return packed[start : start + TILE, :]

    def kept(i):
        return UPPER if i < 4 else LOWER

    squares = jnp.zeros((TILE, TILE), F32)
    for i in range(BLOCKS):
        values = tile(i, 0)
        diag[:, i * TILE : (i + 1) * TILE] = jnp.sum(jnp.where(eye, values, 0.0), axis=0, keepdims=True)
    shift = jnp.sum(diag[...], axis=1, keepdims=True) * (damping / WIDTH)
    per_shift = 1.0 / shift
    diag[...] = 1.0 / (diag[...] + shift)

    def spot(i, j):
        return slice(i * TILE, (i + 1) * TILE), slice(j * TILE, (j + 1) * TILE)

    for i in range(BLOCKS):
        for d in range(kept(i)):
            j = (i + d) % BLOCKS
            values = tile(i, d)
            if d == 0:
                off = jnp.where(eye, 0.0, values) * per_shift
                squares = squares + 0.5 * off * off
                values = values + jnp.where(eye, shift, 0.0)
            else:
                off = values * per_shift
                squares = squares + off * off
            top = values.astype(BF16)
            rest = (values - top.astype(F32)).astype(BF16)
            high[spot(i, j)] = top
            low[spot(i, j)] = rest
            if d:
                high[spot(j, i)] = top.T
                low[spot(j, i)] = rest.T
    hard = 2.0 * jnp.sum(squares) > 256.0**2

    @pl.when(hard)
    def _():
        for i in range(BLOCKS):
            for d in range(kept(i)):
                j = (i + d) % BLOCKS
                values = tile(i, d)
                if d == 0:
                    values = values + jnp.where(eye, shift, 0.0)
                rest = values - values.astype(BF16).astype(F32)
                last = (rest - rest.astype(BF16).astype(F32)).astype(BF16)
                least[spot(i, j)] = last
                if d:
                    least[spot(j, i)] = last.T

    inverse = diag[...]
    for at in range(0, RIGHTS, CHUNK):
        chunk = slice(at, at + CHUNK)
        b = rights[chunk, :].astype(F32)
        zed = b * inverse
        res[chunk, :] = b
        way[chunk, :] = zed.astype(BF16)
        sol[chunk, :] = jnp.zeros((CHUNK, WIDTH), F32)
        norm_ref[chunk, :] = jnp.sum(b * zed, axis=1, keepdims=True)
    norm = norm_ref[...]
    bound = norm * (TOL * TOL)
    rough = norm * (ROUGH * ROUGH)

    def apply(*terms):
        total = jnp.zeros((RIGHTS, TILE), F32)
        for n in range(0, WIDTH, 2 * TILE):
            columns = slice(n, n + 2 * TILE)
            q = jnp.dot(way[...], terms[0][:, columns], preferred_element_type=F32)
            for term in terms[1:]:
                q = q + jnp.dot(way[...], term[:, columns], preferred_element_type=F32)
            image[:, columns] = q
            product = way[:, columns].astype(F32) * q
            total = total + product[:, :TILE] + product[:, TILE:]
        curves[...] = jnp.sum(total, axis=1, keepdims=True)

    def unfinished(carry):
        step, left, more = carry
        return jnp.logical_and(step < MAX_STEPS, left > 0.0)

    def advance(carry):
        step, left, more = carry

        @pl.when(hard)
        def _():
            apply(high, low, least)

        @pl.when(jnp.logical_and(jnp.logical_not(hard), more > 0.0))
        def _():
            apply(high, low)

        @pl.when(jnp.logical_and(jnp.logical_not(hard), jnp.logical_not(more > 0.0)))
        def _():
            apply(high)

        norm = norm_ref[...]
        curve = curves[...]
        alpha = jnp.where(curve > 0.0, norm / jnp.where(curve > 0.0, curve, 1.0), 0.0)
        freshes = []
        for at in range(0, RIGHTS, CHUNK):
            chunk = slice(at, at + CHUNK)
            a = alpha[chunk, :]
            sol[chunk, :] += a * way[chunk, :].astype(F32)
            r = res[chunk, :] - a * image[chunk, :]
            res[chunk, :] = r
            freshes.append(jnp.sum(r * (r * inverse), axis=1, keepdims=True))
        fresh = jnp.concatenate(freshes, axis=0)
        beta = jnp.where(norm > 0.0, fresh / jnp.where(norm > 0.0, norm, 1.0), 0.0)
        norm_ref[...] = fresh
        for at in range(0, RIGHTS, CHUNK):
            chunk = slice(at, at + CHUNK)
            way[chunk, :] = (res[chunk, :] * inverse + beta[chunk, :] * way[chunk, :].astype(F32)).astype(BF16)
        return step + 1, jnp.max(fresh - bound), jnp.max(fresh - rough)

    lax.while_loop(unfinished, advance, (jnp.int32(0), jnp.max(norm - bound), jnp.max(norm - rough)))
    for at in range(0, RIGHTS, CHUNK):
        chunk = slice(at, at + CHUNK)
        out[chunk, :] = (sol[chunk, :] * scale).astype(BF16)


def swap_rows(mine, out, own_s, send, recv):
    x, y, z, core = position()
    sibling = device(x, y, z, 1 - core)
    barrier = pltpu.get_barrier_semaphore()
    signal(barrier, sibling)
    own = pltpu.make_async_copy(mine, out.at[:, core], own_s)
    own.start()
    pl.semaphore_wait(barrier, 1)
    copy = remote(mine, out.at[:, core], send, recv, sibling)
    copy.start()
    own.wait()
    copy.wait_send()
    theirs = out.at[:, 1 - core]
    remote(theirs, theirs, send, recv, sibling).wait_recv()


def score(feat, pre, out, held, sems):
    copies = []
    for n in range(2):
        columns = pl.ds(n * 256, 256)
        held[:, columns] = lax.dot_general(
            feat[...], pre[columns, :], (((1,), (1,)), ((), ())), preferred_element_type=F32
        )
        copies.append(pltpu.make_async_copy(held.at[:, columns], out.at[:, columns], sems.at[n]))
        copies[n].start()
    for copy in copies:
        copy.wait()


def on_device(features, targets):
    dma = pltpu.SemaphoreType.DMA
    vmem = pl.BlockSpec(memory_space=pltpu.VMEM)
    anywhere = pl.BlockSpec(memory_space=pl.ANY)
    hbm = pl.BlockSpec(memory_space=pltpu.HBM)
    packed, rights = pl.pallas_call(
        gram_sum,
        name="gram_sum",
        out_shape=(
            jax.ShapeDtypeStruct((4 * UNIT, TILE), F32),
            jax.ShapeDtypeStruct((RIGHTS, WIDTH), BF16),
        ),
        in_specs=[hbm, hbm],
        out_specs=(vmem, vmem),
        scratch_shapes=[
            pltpu.VMEM((features.shape[0], WIDTH + WIDTH // 2), BF16),
            pltpu.VMEM((4 * UNIT, TILE), F32),
            pltpu.VMEM((2 * UNIT, TILE), F32),
            pltpu.VMEM((2, 3, QUARTER, TILE), F32),
            pltpu.VMEM((2, 3, SIXTEENTH, TILE), F32),
            pltpu.VMEM((NZ, PIECE, TILE), F32),
            pltpu.VMEM((NZ, PIECE, TILE), F32),
            pltpu.VMEM((NZ, PIECE, TILE), F32),
            pltpu.VMEM((1, WIDTH), BF16),
            pltpu.VMEM((8, TILE), F32),
            pltpu.VMEM((NZ * 8, TILE), F32),
            pltpu.VMEM((4, 16, WIDTH), BF16),
            pltpu.VMEM((64, WIDTH), F32),
            dma((3,)), dma((8,)), dma((8,)),
            dma((8,)), dma((8,)), dma((8,)), dma((8,)),
            dma((NZ,)), dma((NZ,)), dma((NZ,)), dma((NZ,)),
            dma((8,)), dma((8,)), dma((8,)), dma((8,)), dma((8,)), dma((8,)),
            dma((NZ,)), dma((NZ,)), dma((4,)), dma((4,)), dma((4,)), dma((4,)),
            pltpu.SemaphoreType.REGULAR((3,)),
        ],
        compiler_params=pltpu.CompilerParams(
            collective_id=0, has_side_effects=True, vmem_limit_bytes=40 * 2**20
        ),
    )(
        pltpu.with_memory_space_constraint(features, pltpu.HBM),
        pltpu.with_memory_space_constraint(targets, pltpu.HBM),
    )

    total_rows = features.shape[0] * lax.axis_size("loop") * lax.axis_size("group")
    precond = pl.pallas_call(
        functools.partial(solve, total_rows / WIDTH**0.5, 0.05),
        name="solve",
        out_shape=jax.ShapeDtypeStruct((RIGHTS, WIDTH), BF16),
        in_specs=[vmem, vmem],
        out_specs=vmem,
        scratch_shapes=[
            pltpu.VMEM((WIDTH, WIDTH), BF16),
            pltpu.VMEM((WIDTH, WIDTH), BF16),
            pltpu.VMEM((WIDTH, WIDTH), BF16),
            pltpu.VMEM((RIGHTS, WIDTH), F32),
            pltpu.VMEM((RIGHTS, WIDTH), F32),
            pltpu.VMEM((RIGHTS, WIDTH), BF16),
            pltpu.VMEM((RIGHTS, WIDTH), F32),
            pltpu.VMEM((1, WIDTH), F32),
            pltpu.VMEM((RIGHTS, 1), F32),
            pltpu.VMEM((RIGHTS, 1), F32),
        ],
        compiler_params=pltpu.CompilerParams(vmem_limit_bytes=40 * 2**20),
    )(packed, rights)

    everyone = pl.pallas_call(
        swap_rows,
        name="swap_rows",
        out_shape=jax.ShapeDtypeStruct((16, 2, 16, WIDTH), BF16),
        in_specs=[vmem],
        out_specs=vmem,
        scratch_shapes=[dma, dma, dma],
        compiler_params=pltpu.CompilerParams(
            collective_id=1, has_side_effects=True, vmem_limit_bytes=16 * 2**20
        ),
    )(precond.reshape(16, 16, WIDTH))

    return pl.pallas_call(
        score,
        name="score",
        out_shape=jax.ShapeDtypeStruct((features.shape[0], 512), F32),
        in_specs=[vmem, vmem],
        out_specs=anywhere,
        scratch_shapes=[pltpu.VMEM((features.shape[0], 512), F32), dma((2,))],
        compiler_params=pltpu.CompilerParams(vmem_limit_bytes=16 * 2**20),
    )(features, everyone.reshape(512, WIDTH))


def solution(mesh):
    return jax.shard_map(
        on_device,
        mesh=mesh,
        in_specs=(P(("loop", "group"), None), P(("loop", "group"), None)),
        out_specs=P(("loop", "group"), None),
        check_vma=False,
    )
```

```python
import functools

import jax
import jax.numpy as jnp
from jax import lax
from jax.experimental import pallas as pl
from jax.experimental.pallas import tpu as pltpu
from jax.sharding import PartitionSpec as P

WIDTH = 1024
TILE = 128
BLOCKS = WIDTH // TILE
UPPER, LOWER = 5, 4
UNIT = (UPPER + LOWER) * TILE
QUARTER = UNIT // 4
SIXTEENTH = UNIT // 16
NZ = 16
PIECE = SIXTEENTH * 2 // NZ
RIGHTS = 256
TOL = 1e-4
ROUGH = 1e-2
MAX_STEPS = 4096
CHUNK = 32
DOT_ROWS = 256
MESH = pl.DeviceIdType.MESH
F32 = jnp.float32
BF16 = jnp.bfloat16


def position():
    loop = lax.axis_index("loop")
    group = lax.axis_index("group")
    x = loop // 8
    y = group // 4
    z = (group % 4) * 4 + (loop // 2) % 4
    return x, y, z, loop % 2


def device(x, y, z, core):
    return (x * 8 + (z % 4) * 2 + core, y * 4 + z // 4)


def remote(src, dst, send, recv, to):
    return pltpu.make_async_remote_copy(
        src_ref=src, dst_ref=dst, send_sem=send, recv_sem=recv, device_id=to, device_id_type=MESH
    )


def signal(sem, to):
    pl.semaphore_signal(sem, inc=1, device_id=to, device_id_type=MESH)


def rows(start, size, unit=8):
    return pl.ds(pl.multiple_of(start, unit), size)


def far_first(k):
    return 8 + ((k + 1) // 2) * (1 - 2 * (k % 2))


def gram_sum(
    feat, tgt, out, rights, wide, packed, from_core, land1, land2, zsrc, zland, zout,
    line, tsrc, tz, yblock, ywide, xblock,
    load_s, core_s, core_r, e1_s, e1_r, e2_s, e2_r, z_s, z_r, za_s, za_r,
    g2_s, g2_r, g1_s, g1_r, cag_s, cag_r, tz_s, tz_r, ty_s, ty_r, tx_s, tx_r, known,
):
    x, y, z, core = position()
    sibling = device(x, y, z, 1 - core)

    def on_x(t):
        return device((x + t) % 4, y, z, core)

    def on_y(t):
        return device(x, (y + t) % 4, z, core)

    def on_z(t):
        return device(x, y, (z + t) % NZ, core)

    def over(axis, t):
        return on_x(t) if axis == 0 else on_y(t)

    here = (x, y)
    ring = (2, 1, 3)

    barrier = pltpu.get_barrier_semaphore()
    signal(barrier, sibling)
    for t in (1, 2, 3):
        signal(barrier, on_x(t))
        signal(barrier, on_y(t))
    signal(barrier, on_z(1))
    signal(barrier, on_z(NZ - 1))

    loads = [
        pltpu.make_async_copy(feat, wide.at[:, pl.ds(0, WIDTH)], load_s.at[0]),
        pltpu.make_async_copy(feat.at[:, pl.ds(0, WIDTH // 2)], wide.at[:, pl.ds(WIDTH, WIDTH // 2)], load_s.at[1]),
        pltpu.make_async_copy(tgt, line, load_s.at[2]),
    ]
    for load in loads:
        load.start()
    for load in loads:
        load.wait()

    def unit_gram(u):
        for i, kept, base in ((u, UPPER, u * UNIT), (u + 4, LOWER, u * UNIT + UPPER * TILE)):
            left = wide[:, rows(i * TILE, TILE, TILE)]
            span = wide[:, rows(i * TILE, kept * TILE, TILE)]
            product = lax.dot_general(left, span, (((0,), (0,)), ((), ())), preferred_element_type=F32)
            for d in range(kept):
                packed[rows(base + d * TILE, TILE), :] = product[:, d * TILE : (d + 1) * TILE]

    def core_copy(j, t):
        n = j * 4 + t
        return remote(
            packed.at[rows((2 * (1 - core) + j) * UNIT + ((here[j] + t) % 4) * QUARTER, QUARTER)],
            from_core.at[pl.ds(n * QUARTER, QUARTER)], core_s.at[n], core_r.at[n], sibling,
        )

    unit_gram(2 * (1 - core))
    pl.semaphore_wait(barrier, 9)
    core_copy(0, 2).start()
    signal(known.at[0], on_z(1))
    signal(known.at[0], on_z(NZ - 1))
    unit_gram(2 * (1 - core) + 1)
    core_copy(1, 2).start()
    for t in (1, 3, 0):
        for j in range(2):
            core_copy(j, t).start()

    units = [(2 * core + j) * UNIT for j in range(2)]
    quarters = [units[j] + here[j] * QUARTER for j in range(2)]
    parts = [quarters[j] + here[1 - j] * SIXTEENTH for j in range(2)]

    def first(j, t):
        at = units[j] + ((here[j] + t) % 4) * QUARTER
        return remote(
            packed.at[rows(at, QUARTER)], land1.at[j, t - 1], e1_s.at[j * 4 + t], e1_r.at[j * 4 + t], over(j, t)
        )

    def second(j, t):
        at = quarters[j] + ((here[1 - j] + t) % 4) * SIXTEENTH
        return remote(
            packed.at[rows(at, SIXTEENTH)], land2.at[j, t - 1], e2_s.at[j * 4 + t], e2_r.at[j * 4 + t], over(1 - j, t)
        )

    for j in range(2):
        unit_gram(2 * core + j)
    for t in (2, 1, 3, 0):
        for j in range(2):
            n = j * 4 + t
            core_copy(j, t).wait_recv()
            at = units[j] + ((here[j] + t) % 4) * QUARTER
            packed[rows(at, QUARTER), :] += from_core[n * QUARTER : (n + 1) * QUARTER, :]
            if t:
                first(j, t).start()

    for k in range(8):
        tsrc[k : k + 1, :] = line[:, k * TILE : (k + 1) * TILE].astype(F32)
    tz[rows(z * 8, 8), :] = tsrc[...]
    for t in range(4):
        for j in range(2):
            core_copy(j, t).wait_send()
    pl.semaphore_wait(known.at[0], 2)
    signal(known.at[1], on_z(2))
    signal(known.at[1], on_z(NZ - 2))
    pl.semaphore_wait(known.at[1], 2)
    signal(known.at[2], on_z(4))
    signal(known.at[2], on_z(NZ - 4))

    for j in range(2):
        for t in ring:
            first(j, t).wait()
        packed[rows(quarters[j], QUARTER), :] += land1[j, 0] + land1[j, 1] + land1[j, 2]
        for t in ring:
            second(j, t).start()

    pl.semaphore_wait(known.at[2], 2)

    def all_z(copy):
        def body(k, carry):
            copy(far_first(k)).start()
            return carry

        lax.fori_loop(0, NZ - 1, body, 0)

    def end_z(copy, landing, recv):
        def body(k, carry):
            t = far_first(k)
            copy(t).wait_send()
            other = (z + t) % NZ
            ref = landing(other)
            remote(ref, ref, recv.at[other], recv.at[other], sibling).wait_recv()
            return carry

        lax.fori_loop(0, NZ - 1, body, 0)

    def target_row(k):
        return tz.at[rows(k * 8, 8)]

    def t_copy(t):
        return remote(target_row(z), target_row(z), tz_s.at[t], tz_r.at[z], on_z(t))

    all_z(t_copy)

    for j in range(2):
        for t in ring:
            second(j, t).wait()
        packed[rows(parts[j], SIXTEENTH), :] += land2[j, 0] + land2[j, 1] + land2[j, 2]
        block = packed[rows(parts[j], SIXTEENTH), :]
        for m in range(8):
            zsrc[j * 8 + m] = block[m * PIECE : (m + 1) * PIECE, :]

    def z_copy(t):
        return remote(zsrc.at[(z + t) % NZ], zland.at[z], z_s.at[t], z_r.at[z], on_z(t))

    all_z(z_copy)
    zland[z] = zsrc[z]

    end_z(t_copy, target_row, tz_r)
    for k in range(8):
        for low in range(4):
            ywide[low * 4 : low * 4 + 4, k * TILE : (k + 1) * TILE] = tz[pl.ds(low * 8 + k, 4, stride=32), :]
    yblock[y] = ywide[0:16, :].astype(BF16)

    def y_copy(t):
        return remote(yblock.at[y], yblock.at[y], ty_s.at[t], ty_r.at[t], on_y(t))

    for t in ring:
        y_copy(t).start()

    end_z(z_copy, lambda k: zland.at[k], z_r)
    total = zland[0]
    for k in range(1, NZ):
        total = total + zland[k]
    zout[z] = total

    def za_copy(t):
        return remote(zout.at[z], zout.at[z], za_s.at[t], za_r.at[z], on_z(t))

    all_z(za_copy)

    for t in ring:
        y_copy(t).wait_send()
        ref = yblock.at[(y + 4 - t) % 4]
        remote(ref, ref, ty_s.at[t], ty_r.at[t], sibling).wait_recv()
    for yy in range(4):
        block = yblock[yy].astype(F32)
        for low in range(4):
            ywide[low * 16 + yy * 4 : low * 16 + yy * 4 + 4, :] = block[low * 4 : low * 4 + 4, :]
    for low in range(4):
        xblock[low] = ywide[low * 16 : low * 16 + 16, :].astype(BF16)

    solver = x // 2
    stays = solver == core

    def x_copy(t):
        to = device((x + t) % 4, y, z, solver)
        return remote(xblock, rights.at[x % 2, :, core], tx_s.at[t], tx_r.at[(x % 2) * 2 + core], to)

    for t in ring:
        x_copy(t).start()
    stay = pltpu.make_async_copy(xblock, rights.at[x % 2, :, core], tx_s.at[0])

    @pl.when(stays)
    def _():
        stay.start()

    @pl.when(jnp.logical_not(stays))
    def _():
        x_copy(0).start()

    end_z(za_copy, lambda k: zout.at[k], za_r)

    def gather(j, t, stage):
        if stage == 2:
            mine, size, axis = parts[j], SIXTEENTH, 1 - j
            theirs = quarters[j] + ((here[axis] + 4 - t) % 4) * SIXTEENTH
            send, recv = g2_s, g2_r
        else:
            mine, size, axis = quarters[j], QUARTER, j
            theirs = units[j] + ((here[axis] + 4 - t) % 4) * QUARTER
            send, recv = g1_s, g1_r
        a, b = out.at[rows(mine, size)], out.at[rows(theirs, size)]
        n = j * 4 + t
        return (
            remote(a, a, send.at[n], recv.at[n], over(axis, t)),
            remote(b, b, send.at[n], recv.at[n], over(axis, t)),
        )

    def core_gather(j, t, who):
        at = (2 * who + j) * UNIT + ((here[j] + 4 - t) % 4) * QUARTER
        ref = out.at[rows(at, QUARTER)]
        return remote(ref, ref, cag_s.at[j * 4 + t], cag_r.at[j * 4 + t], sibling)

    for j in range(2):
        out[rows(parts[j], SIXTEENTH), :] = jnp.concatenate([zout[j * 8 + m] for m in range(8)], axis=0)
        for t in ring:
            gather(j, t, 2)[0].start()
    for j in range(2):
        for t in ring:
            send, recv = gather(j, t, 2)
            send.wait_send()
            recv.wait_recv()
        core_gather(j, 0, core).start()
        for t in ring:
            gather(j, t, 1)[0].start()
    for t in (1, 3, 2):
        for j in range(2):
            gather(j, t, 1)[1].wait_recv()
            core_gather(j, t, core).start()
    for t in ring:
        x_copy(t).wait_send()
        for j in range(2):
            gather(j, t, 1)[0].wait_send()

    @pl.when(stays)
    def _():
        stay.wait()

    @pl.when(jnp.logical_not(stays))
    def _():
        x_copy(0).wait_send()

    for near in range(2):
        for who in range(2):

            @pl.when(jnp.logical_or(2 * core + near != x, who != core))
            def _():
                ref = rights.at[near, :, who]
                remote(ref, ref, tx_s.at[0], tx_r.at[near * 2 + who], sibling).wait_recv()

    for t in (0, 1, 3, 2):
        for j in range(2):
            core_gather(j, t, core).wait_send()
            core_gather(j, t, 1 - core).wait_recv()


def solve(scale, damping, packed, rights, out, high, low, least, side, sol, res, way, image, diag, norm_ref, curve_ref):
    eye = lax.broadcasted_iota(jnp.int32, (TILE, TILE), 0) == lax.broadcasted_iota(jnp.int32, (TILE, TILE), 1)

    def tile(i, d):
        start = (i % 4) * UNIT + (i // 4) * UPPER * TILE + d * TILE
        return packed[start : start + TILE, :]

    def kept(i):
        return UPPER if i < 4 else LOWER

    def span(i):
        return slice(i * TILE, (i + 1) * TILE)

    for i in range(BLOCKS):
        diag[:, span(i)] = jnp.sum(jnp.where(eye, tile(i, 0), 0.0), axis=0, keepdims=True)
    shift = jnp.sum(diag[...], axis=1, keepdims=True) * (damping / WIDTH)
    per_shift = 1.0 / shift
    diag[...] = lax.rsqrt(diag[...] + shift)
    for i in range(BLOCKS):
        side[span(i), :] = jnp.broadcast_to(diag[:, span(i)], (TILE, TILE)).T

    def scaled(i, d):
        values = tile(i, d)
        if d == 0:
            values = values + jnp.where(eye, shift, 0.0)
        return values * side[span(i), :] * diag[:, span((i + d) % BLOCKS)]

    squares = jnp.zeros((TILE, TILE), F32)
    for i in range(BLOCKS):
        for d in range(kept(i)):
            j = (i + d) % BLOCKS
            off = tile(i, d) * per_shift
            if d == 0:
                off = jnp.where(eye, 0.0, off)
                squares = squares + 0.5 * off * off
            else:
                squares = squares + off * off
            values = scaled(i, d)
            top = values.astype(BF16)
            rest = (values - top.astype(F32)).astype(BF16)
            high[span(i), span(j)] = top
            low[span(i), span(j)] = rest
            if d:
                high[span(j), span(i)] = top.T
                low[span(j), span(i)] = rest.T
    hard = 2.0 * jnp.sum(squares) > 256.0**2

    @pl.when(hard)
    def _():
        for i in range(BLOCKS):
            for d in range(kept(i)):
                j = (i + d) % BLOCKS
                values = scaled(i, d)
                rest = values - values.astype(BF16).astype(F32)
                last = (rest - rest.astype(BF16).astype(F32)).astype(BF16)
                least[span(i), span(j)] = last
                if d:
                    least[span(j), span(i)] = last.T

    def fold(total):
        return jnp.sum(total, axis=0, keepdims=True)

    def twice(values):
        return jnp.concatenate([values, values], axis=1)

    total = jnp.zeros((TILE, RIGHTS), F32)
    for i in range(BLOCKS):
        turned = jnp.concatenate([rights[span(h), span(i)].T for h in range(RIGHTS // TILE)], axis=1)
        b = turned.astype(F32) * twice(side[span(i), :])
        res[span(i), :] = b
        way[span(i), :] = b.astype(BF16)
        sol[span(i), :] = jnp.zeros((TILE, RIGHTS), F32)
        total = total + b * b
    norm = fold(total)
    norm_ref[...] = norm
    bound = norm * (TOL * TOL)
    rough = norm * (ROUGH * ROUGH)

    def apply(*terms):
        total = jnp.zeros((CHUNK, RIGHTS), F32)
        for at in range(0, WIDTH, DOT_ROWS):
            part = slice(at, at + DOT_ROWS)
            q = jnp.dot(terms[0][part, :], way[...], preferred_element_type=F32)
            for term in terms[1:]:
                q = q + jnp.dot(term[part, :], way[...], preferred_element_type=F32)
            image[part, :] = q
            for n in range(0, DOT_ROWS, CHUNK):
                total = total + way[at + n : at + n + CHUNK, :].astype(F32) * q[n : n + CHUNK, :]
        curve_ref[...] = fold(total)

    def unfinished(carry):
        step, left, more = carry
        return jnp.logical_and(step < MAX_STEPS, left > 0.0)

    def advance(carry):
        step, left, more = carry

        @pl.when(hard)
        def _():
            apply(high, low, least)

        @pl.when(jnp.logical_and(jnp.logical_not(hard), more > 0.0))
        def _():
            apply(high, low)

        @pl.when(jnp.logical_and(jnp.logical_not(hard), jnp.logical_not(more > 0.0)))
        def _():
            apply(high)

        norm = norm_ref[...]
        curve = curve_ref[...]
        alpha = jnp.where(curve > 0.0, norm / jnp.where(curve > 0.0, curve, 1.0), 0.0)
        total = jnp.zeros((CHUNK, RIGHTS), F32)
        for at in range(0, WIDTH, CHUNK):
            part = slice(at, at + CHUNK)
            r = res[part, :] - alpha * image[part, :]
            res[part, :] = r
            total = total + r * r
        fresh = fold(total)
        beta = jnp.where(norm > 0.0, fresh / jnp.where(norm > 0.0, norm, 1.0), 0.0)
        norm_ref[...] = fresh
        for at in range(0, WIDTH, CHUNK):
            part = slice(at, at + CHUNK)
            p = way[part, :].astype(F32)
            sol[part, :] += alpha * p
            way[part, :] = (res[part, :] + beta * p).astype(BF16)
        return step + 1, jnp.max(fresh - bound), jnp.max(fresh - rough)

    lax.while_loop(unfinished, advance, (jnp.int32(0), jnp.max(norm - bound), jnp.max(norm - rough)))
    for i in range(BLOCKS):
        out[span(i), :] = (sol[span(i), :] * twice(side[span(i), :] * scale)).astype(BF16)


def swap_halves(mine, out, own_s, send, recv):
    x, y, z, core = position()
    sibling = device(x, y, z, 1 - core)
    signal(pltpu.get_barrier_semaphore(), sibling)
    own = pltpu.make_async_copy(mine, out.at[core], own_s)
    own.start()
    pl.semaphore_wait(pltpu.get_barrier_semaphore(), 1)
    copy = remote(mine, out.at[core], send, recv, sibling)
    copy.start()
    own.wait()
    copy.wait_send()
    theirs = out.at[1 - core]
    remote(theirs, theirs, send, recv, sibling).wait_recv()


def score(feat, pre, out, held, sems):
    copies = []
    for n in range(2):
        columns = pl.ds(n * 256, 256)
        held[:, columns] = jnp.dot(feat[...], pre[n], preferred_element_type=F32)
        copies.append(pltpu.make_async_copy(held.at[:, columns], out.at[:, columns], sems.at[n]))
        copies[n].start()
    for copy in copies:
        copy.wait()


def on_device(features, targets):
    dma = pltpu.SemaphoreType.DMA
    vmem = pl.BlockSpec(memory_space=pltpu.VMEM)
    anywhere = pl.BlockSpec(memory_space=pl.ANY)
    hbm = pl.BlockSpec(memory_space=pltpu.HBM)
    packed, rights = pl.pallas_call(
        gram_sum,
        name="gram_sum",
        out_shape=(
            jax.ShapeDtypeStruct((4 * UNIT, TILE), F32),
            jax.ShapeDtypeStruct((2, 4, 2, 16, WIDTH), BF16),
        ),
        in_specs=[hbm, hbm],
        out_specs=(vmem, vmem),
        scratch_shapes=[
            pltpu.VMEM((features.shape[0], WIDTH + WIDTH // 2), BF16),
            pltpu.VMEM((4 * UNIT, TILE), F32),
            pltpu.VMEM((2 * UNIT, TILE), F32),
            pltpu.VMEM((2, 3, QUARTER, TILE), F32),
            pltpu.VMEM((2, 3, SIXTEENTH, TILE), F32),
            pltpu.VMEM((NZ, PIECE, TILE), F32),
            pltpu.VMEM((NZ, PIECE, TILE), F32),
            pltpu.VMEM((NZ, PIECE, TILE), F32),
            pltpu.VMEM((1, WIDTH), BF16),
            pltpu.VMEM((8, TILE), F32),
            pltpu.VMEM((NZ * 8, TILE), F32),
            pltpu.VMEM((4, 16, WIDTH), BF16),
            pltpu.VMEM((64, WIDTH), F32),
            pltpu.VMEM((4, 16, WIDTH), BF16),
            dma((3,)), dma((8,)), dma((8,)),
            dma((8,)), dma((8,)), dma((8,)), dma((8,)),
            dma((NZ,)), dma((NZ,)), dma((NZ,)), dma((NZ,)),
            dma((8,)), dma((8,)), dma((8,)), dma((8,)), dma((8,)), dma((8,)),
            dma((NZ,)), dma((NZ,)), dma((4,)), dma((4,)), dma((4,)), dma((4,)),
            pltpu.SemaphoreType.REGULAR((3,)),
        ],
        compiler_params=pltpu.CompilerParams(
            collective_id=0, has_side_effects=True, vmem_limit_bytes=40 * 2**20
        ),
    )(
        pltpu.with_memory_space_constraint(features, pltpu.HBM),
        pltpu.with_memory_space_constraint(targets, pltpu.HBM),
    )

    total_rows = features.shape[0] * lax.axis_size("loop") * lax.axis_size("group")
    precond = pl.pallas_call(
        functools.partial(solve, total_rows / WIDTH**0.5, 0.05),
        name="solve",
        out_shape=jax.ShapeDtypeStruct((WIDTH, RIGHTS), BF16),
        in_specs=[vmem, vmem],
        out_specs=vmem,
        scratch_shapes=[
            pltpu.VMEM((WIDTH, WIDTH), BF16),
            pltpu.VMEM((WIDTH, WIDTH), BF16),
            pltpu.VMEM((WIDTH, WIDTH), BF16),
            pltpu.VMEM((WIDTH, TILE), F32),
            pltpu.VMEM((WIDTH, RIGHTS), F32),
            pltpu.VMEM((WIDTH, RIGHTS), F32),
            pltpu.VMEM((WIDTH, RIGHTS), BF16),
            pltpu.VMEM((WIDTH, RIGHTS), F32),
            pltpu.VMEM((1, WIDTH), F32),
            pltpu.VMEM((1, RIGHTS), F32),
            pltpu.VMEM((1, RIGHTS), F32),
        ],
        compiler_params=pltpu.CompilerParams(vmem_limit_bytes=40 * 2**20),
    )(packed, rights.reshape(RIGHTS, WIDTH))

    everyone = pl.pallas_call(
        swap_halves,
        name="swap_halves",
        out_shape=jax.ShapeDtypeStruct((2, WIDTH, RIGHTS), BF16),
        in_specs=[vmem],
        out_specs=vmem,
        scratch_shapes=[dma, dma, dma],
        compiler_params=pltpu.CompilerParams(
            collective_id=1, has_side_effects=True, vmem_limit_bytes=16 * 2**20
        ),
    )(precond)

    return pl.pallas_call(
        score,
        name="score",
        out_shape=jax.ShapeDtypeStruct((features.shape[0], 512), F32),
        in_specs=[vmem, vmem],
        out_specs=anywhere,
        scratch_shapes=[pltpu.VMEM((features.shape[0], 512), F32), dma((2,))],
        compiler_params=pltpu.CompilerParams(vmem_limit_bytes=16 * 2**20),
    )(features, everyone)


def solution(mesh):
    return jax.shard_map(
        on_device,
        mesh=mesh,
        in_specs=(P(("loop", "group"), None), P(("loop", "group"), None)),
        out_specs=P(("loop", "group"), None),
        check_vma=False,
    )
```

```python
import functools

import jax
import jax.numpy as jnp
from jax import lax
from jax.experimental import pallas as pl
from jax.experimental.pallas import tpu as pltpu
from jax.sharding import PartitionSpec as P

WIDTH = 1024
TILE = 128
BLOCKS = WIDTH // TILE
UPPER, LOWER = 5, 4
UNIT = (UPPER + LOWER) * TILE
NZ = 16
START = (0, UPPER * TILE)
SIZE = (UPPER * TILE, LOWER * TILE)
QUARTER = tuple(size // 4 for size in SIZE)
SIXTEENTH = tuple(size // 16 for size in SIZE)
PIECE = tuple(size // 8 // NZ for size in SIZE)
QUARTERS, SIXTEENTHS = sum(QUARTER), sum(SIXTEENTH)
RIGHTS = 256
TOL = 1e-4
ROUGH = 1e-2
MAX_STEPS = 4096
CHUNK = 32
DOT_ROWS = 256
MESH = pl.DeviceIdType.MESH
F32 = jnp.float32
BF16 = jnp.bfloat16


def position():
    loop = lax.axis_index("loop")
    group = lax.axis_index("group")
    x = loop // 8
    y = group // 4
    z = (group % 4) * 4 + (loop // 2) % 4
    return x, y, z, loop % 2


def device(x, y, z, core):
    return (x * 8 + (z % 4) * 2 + core, y * 4 + z // 4)


def remote(src, dst, send, recv, to):
    return pltpu.make_async_remote_copy(
        src_ref=src, dst_ref=dst, send_sem=send, recv_sem=recv, device_id=to, device_id_type=MESH
    )


def signal(sem, to):
    pl.semaphore_signal(sem, inc=1, device_id=to, device_id_type=MESH)


def rows(start, size, unit=8):
    return pl.ds(pl.multiple_of(start, unit), size)


def far_first(k):
    return 8 + ((k + 1) // 2) * (1 - 2 * (k % 2))


def gram_sum(
    feat, tgt, out, rights, wide, packed, from_core, land1, land2, zsrc0, zsrc1, zland0, zland1, zout0, zout1,
    line, tsrc, tz, yblock, ywide, xblock,
    load_s, core_s, core_r, e1_s, e1_r, e2_s, e2_r, z_s, z_r, za_s, za_r,
    g2_s, g2_r, g1_s, g1_r, cag_s, cag_r, tz_s, tz_r, ty_s, ty_r, tx_s, tx_r, known,
):
    zsrc, zland, zout = (zsrc0, zsrc1), (zland0, zland1), (zout0, zout1)
    x, y, z, core = position()
    sibling = device(x, y, z, 1 - core)

    def on_x(t):
        return device((x + t) % 4, y, z, core)

    def on_y(t):
        return device(x, (y + t) % 4, z, core)

    def on_z(t):
        return device(x, y, (z + t) % NZ, core)

    def over(axis, t):
        return on_x(t) if axis == 0 else on_y(t)

    here = (x, y)
    ring = (2, 1, 3)
    parts = (0, 1)
    units = (0, 1)

    barrier = pltpu.get_barrier_semaphore()
    signal(barrier, sibling)
    for t in (1, 2, 3):
        signal(barrier, on_x(t))
        signal(barrier, on_y(t))
    signal(barrier, on_z(1))
    signal(barrier, on_z(NZ - 1))

    loads = [
        pltpu.make_async_copy(feat, wide.at[:, pl.ds(0, WIDTH)], load_s.at[0]),
        pltpu.make_async_copy(feat.at[:, pl.ds(0, WIDTH // 2)], wide.at[:, pl.ds(WIDTH, WIDTH // 2)], load_s.at[1]),
        pltpu.make_async_copy(tgt, line, load_s.at[2]),
    ]
    for load in loads:
        load.start()
    for load in loads:
        load.wait()

    def begin(who, j, h):
        return (2 * who + j) * UNIT + START[h]

    def quarter(j, h, t):
        return begin(core, j, h) + ((here[j] + t) % 4) * QUARTER[h]

    def sixteenth(j, h, t):
        return quarter(j, h, 0) + ((here[1 - j] + t) % 4) * SIXTEENTH[h]

    def slot(j, h, t):
        return (h * 2 + j) * 4 + t

    def part_gram(who, j, h):
        i = 2 * who + j + 4 * h
        kept = (UPPER, LOWER)[h]
        left = wide[:, rows(i * TILE, TILE, TILE)]
        span = wide[:, rows(i * TILE, kept * TILE, TILE)]
        product = lax.dot_general(left, span, (((0,), (0,)), ((), ())), preferred_element_type=F32)
        for d in range(kept):
            packed[rows(begin(who, j, h) + d * TILE, TILE), :] = product[:, d * TILE : (d + 1) * TILE]

    def core_landing(j, h, t):
        return pl.ds((j * 4 + t) * QUARTERS + h * QUARTER[0], QUARTER[h])

    def core_copy(j, h, t):
        n = slot(j, h, t)
        at = begin(1 - core, j, h) + ((here[j] + t) % 4) * QUARTER[h]
        return remote(
            packed.at[rows(at, QUARTER[h])], from_core.at[core_landing(j, h, t)], core_s.at[n], core_r.at[n], sibling
        )

    part_gram(1 - core, 0, 0)
    pl.semaphore_wait(barrier, 9)
    core_copy(0, 0, 2).start()
    signal(known.at[0], on_z(1))
    signal(known.at[0], on_z(NZ - 1))
    part_gram(1 - core, 1, 0)
    core_copy(1, 0, 2).start()
    for t in (1, 3, 0):
        for j in units:
            core_copy(j, 0, t).start()
    for j in units:
        part_gram(1 - core, j, 1)
    for t in (2, 1, 3, 0):
        for j in units:
            core_copy(j, 1, t).start()
    for h in parts:
        for j in units:
            part_gram(core, j, h)

    def first_landing(h):
        return pl.ds(h * QUARTER[0], QUARTER[h])

    def second_landing(h):
        return pl.ds(h * SIXTEENTH[0], SIXTEENTH[h])

    def first(j, h, t):
        n = slot(j, h, t)
        return remote(
            packed.at[rows(quarter(j, h, t), QUARTER[h])], land1.at[j, t - 1, first_landing(h)],
            e1_s.at[n], e1_r.at[n], over(j, t),
        )

    def second(j, h, t):
        n = slot(j, h, t)
        return remote(
            packed.at[rows(sixteenth(j, h, t), SIXTEENTH[h])], land2.at[j, t - 1, second_landing(h)],
            e2_s.at[n], e2_r.at[n], over(1 - j, t),
        )

    for h in parts:
        for t in (2, 1, 3, 0):
            for j in units:
                core_copy(j, h, t).wait_recv()
                packed[rows(quarter(j, h, t), QUARTER[h]), :] += from_core[core_landing(j, h, t), :]
                if t:
                    first(j, h, t).start()

    for k in range(8):
        tsrc[k : k + 1, :] = line[:, k * TILE : (k + 1) * TILE].astype(F32)
    tz[rows(z * 8, 8), :] = tsrc[...]
    for h in parts:
        for t in range(4):
            for j in units:
                core_copy(j, h, t).wait_send()
    pl.semaphore_wait(known.at[0], 2)
    signal(known.at[1], on_z(2))
    signal(known.at[1], on_z(NZ - 2))

    def add_first(h):
        for j in units:
            for t in ring:
                first(j, h, t).wait()
            at = rows(quarter(j, h, 0), QUARTER[h])
            landed = first_landing(h)
            packed[at, :] += land1[j, 0, landed, :] + land1[j, 1, landed, :] + land1[j, 2, landed, :]
            for t in ring:
                second(j, h, t).start()

    add_first(0)
    pl.semaphore_wait(known.at[1], 2)
    signal(known.at[2], on_z(4))
    signal(known.at[2], on_z(NZ - 4))
    add_first(1)
    pl.semaphore_wait(known.at[2], 2)

    def all_z(copy):
        def body(k, carry):
            copy(far_first(k)).start()
            return carry

        lax.fori_loop(0, NZ - 1, body, 0)

    def end_z(copy, landing, recv):
        def body(k, carry):
            t = far_first(k)
            copy(t).wait_send()
            other = (z + t) % NZ
            ref = landing(other)
            remote(ref, ref, recv.at[other], recv.at[other], sibling).wait_recv()
            return carry

        lax.fori_loop(0, NZ - 1, body, 0)

    def target_row(k):
        return tz.at[rows(k * 8, 8)]

    def t_copy(t):
        return remote(target_row(z), target_row(z), tz_s.at[t], tz_r.at[z], on_z(t))

    all_z(t_copy)

    def z_copy(h):
        def copy(t):
            return remote(zsrc[h].at[(z + t) % NZ], zland[h].at[z], z_s.at[h, t], z_r.at[h, z], on_z(t))

        return copy

    def za_copy(h):
        def copy(t):
            return remote(zout[h].at[z], zout[h].at[z], za_s.at[h, t], za_r.at[h, z], on_z(t))

        return copy

    for h in parts:
        for j in units:
            for t in ring:
                second(j, h, t).wait()
            at = rows(sixteenth(j, h, 0), SIXTEENTH[h])
            landed = second_landing(h)
            block = packed[at, :] + land2[j, 0, landed, :] + land2[j, 1, landed, :] + land2[j, 2, landed, :]
            for m in range(8):
                zsrc[h][j * 8 + m] = block[m * PIECE[h] : (m + 1) * PIECE[h], :]
        all_z(z_copy(h))
        zland[h][z] = zsrc[h][z]

    end_z(t_copy, target_row, tz_r)
    for k in range(8):
        for low in range(4):
            ywide[low * 4 : low * 4 + 4, k * TILE : (k + 1) * TILE] = tz[pl.ds(low * 8 + k, 4, stride=32), :]
    yblock[y] = ywide[0:16, :].astype(BF16)

    def y_copy(t):
        return remote(yblock.at[y], yblock.at[y], ty_s.at[t], ty_r.at[t], on_y(t))

    for t in ring:
        y_copy(t).start()

    for h in parts:
        end_z(z_copy(h), lambda k: zland[h].at[k], z_r.at[h])
        total = zland[h][0]
        for k in range(1, NZ):
            total = total + zland[h][k]
        zout[h][z] = total
        all_z(za_copy(h))

    for t in ring:
        y_copy(t).wait_send()
        ref = yblock.at[(y + 4 - t) % 4]
        remote(ref, ref, ty_s.at[t], ty_r.at[t], sibling).wait_recv()
    for yy in range(4):
        block = yblock[yy].astype(F32)
        for low in range(4):
            ywide[low * 16 + yy * 4 : low * 16 + yy * 4 + 4, :] = block[low * 4 : low * 4 + 4, :]
    for low in range(4):
        xblock[low] = ywide[low * 16 : low * 16 + 16, :].astype(BF16)

    solver = x // 2
    stays = solver == core

    def x_copy(t):
        to = device((x + t) % 4, y, z, solver)
        return remote(xblock, rights.at[x % 2, :, core], tx_s.at[t], tx_r.at[(x % 2) * 2 + core], to)

    for t in ring:
        x_copy(t).start()
    stay = pltpu.make_async_copy(xblock, rights.at[x % 2, :, core], tx_s.at[0])

    @pl.when(stays)
    def _():
        stay.start()

    @pl.when(jnp.logical_not(stays))
    def _():
        x_copy(0).start()

    def gather(j, h, t, stage):
        if stage == 2:
            mine, theirs, size, axis = sixteenth(j, h, 0), sixteenth(j, h, 4 - t), SIXTEENTH[h], 1 - j
            send, recv = g2_s, g2_r
        else:
            mine, theirs, size, axis = quarter(j, h, 0), quarter(j, h, 4 - t), QUARTER[h], j
            send, recv = g1_s, g1_r
        a, b = out.at[rows(mine, size)], out.at[rows(theirs, size)]
        n = slot(j, h, t)
        return (
            remote(a, a, send.at[n], recv.at[n], over(axis, t)),
            remote(b, b, send.at[n], recv.at[n], over(axis, t)),
        )

    def core_gather(j, h, t, who):
        at = begin(who, j, h) + ((here[j] + 4 - t) % 4) * QUARTER[h]
        ref = out.at[rows(at, QUARTER[h])]
        n = slot(j, h, t)
        return remote(ref, ref, cag_s.at[n], cag_r.at[n], sibling)

    for h in parts:
        end_z(za_copy(h), lambda k: zout[h].at[k], za_r.at[h])
        for j in units:
            out[rows(sixteenth(j, h, 0), SIXTEENTH[h]), :] = jnp.concatenate(
                [zout[h][j * 8 + m] for m in range(8)], axis=0
            )
            for t in ring:
                gather(j, h, t, 2)[0].start()
    for h in parts:
        for j in units:
            for t in ring:
                send, recv = gather(j, h, t, 2)
                send.wait_send()
                recv.wait_recv()
            for t in ring:
                gather(j, h, t, 1)[0].start()
            core_gather(j, h, 0, core).start()
    for h in parts:
        for t in (1, 3, 2):
            for j in units:
                gather(j, h, t, 1)[1].wait_recv()
                core_gather(j, h, t, core).start()
    for t in ring:
        x_copy(t).wait_send()
        for h in parts:
            for j in units:
                gather(j, h, t, 1)[0].wait_send()

    @pl.when(stays)
    def _():
        stay.wait()

    @pl.when(jnp.logical_not(stays))
    def _():
        x_copy(0).wait_send()

    for near in range(2):
        for who in range(2):

            @pl.when(jnp.logical_or(2 * core + near != x, who != core))
            def _():
                ref = rights.at[near, :, who]
                remote(ref, ref, tx_s.at[0], tx_r.at[near * 2 + who], sibling).wait_recv()

    for h in parts:
        for t in (0, 1, 3, 2):
            for j in units:
                core_gather(j, h, t, core).wait_send()
                core_gather(j, h, t, 1 - core).wait_recv()


def solve(scale, damping, packed, rights, out, high, low, least, side, sol, res, way, image, diag, norm_ref, curve_ref):
    eye = lax.broadcasted_iota(jnp.int32, (TILE, TILE), 0) == lax.broadcasted_iota(jnp.int32, (TILE, TILE), 1)

    def tile(i, d):
        start = (i % 4) * UNIT + (i // 4) * UPPER * TILE + d * TILE
        return packed[start : start + TILE, :]

    def kept(i):
        return UPPER if i < 4 else LOWER

    def span(i):
        return slice(i * TILE, (i + 1) * TILE)

    for i in range(BLOCKS):
        diag[:, span(i)] = jnp.sum(jnp.where(eye, tile(i, 0), 0.0), axis=0, keepdims=True)
    shift = jnp.sum(diag[...], axis=1, keepdims=True) * (damping / WIDTH)
    per_shift = 1.0 / shift
    diag[...] = lax.rsqrt(diag[...] + shift)
    for i in range(BLOCKS):
        side[span(i), :] = jnp.broadcast_to(diag[:, span(i)], (TILE, TILE)).T

    def scaled(i, d):
        values = tile(i, d)
        if d == 0:
            values = values + jnp.where(eye, shift, 0.0)
        return values * side[span(i), :] * diag[:, span((i + d) % BLOCKS)]

    squares = jnp.zeros((TILE, TILE), F32)
    for i in range(BLOCKS):
        for d in range(kept(i)):
            j = (i + d) % BLOCKS
            off = tile(i, d) * per_shift
            if d == 0:
                off = jnp.where(eye, 0.0, off)
                squares = squares + 0.5 * off * off
            else:
                squares = squares + off * off
            values = scaled(i, d)
            top = values.astype(BF16)
            rest = (values - top.astype(F32)).astype(BF16)
            high[span(i), span(j)] = top
            low[span(i), span(j)] = rest
            if d:
                high[span(j), span(i)] = top.T
                low[span(j), span(i)] = rest.T
    hard = 2.0 * jnp.sum(squares) > 256.0**2

    @pl.when(hard)
    def _():
        for i in range(BLOCKS):
            for d in range(kept(i)):
                j = (i + d) % BLOCKS
                values = scaled(i, d)
                rest = values - values.astype(BF16).astype(F32)
                last = (rest - rest.astype(BF16).astype(F32)).astype(BF16)
                least[span(i), span(j)] = last
                if d:
                    least[span(j), span(i)] = last.T

    def fold(total):
        return jnp.sum(total, axis=0, keepdims=True)

    def twice(values):
        return jnp.concatenate([values, values], axis=1)

    total = jnp.zeros((TILE, RIGHTS), F32)
    for i in range(BLOCKS):
        turned = jnp.concatenate([rights[span(h), span(i)].T for h in range(RIGHTS // TILE)], axis=1)
        b = turned.astype(F32) * twice(side[span(i), :])
        res[span(i), :] = b
        way[span(i), :] = b.astype(BF16)
        sol[span(i), :] = jnp.zeros((TILE, RIGHTS), F32)
        total = total + b * b
    norm = fold(total)
    norm_ref[...] = norm
    bound = norm * (TOL * TOL)
    rough = norm * (ROUGH * ROUGH)

    def apply(*terms):
        total = jnp.zeros((CHUNK, RIGHTS), F32)
        for at in range(0, WIDTH, DOT_ROWS):
            part = slice(at, at + DOT_ROWS)
            q = jnp.dot(terms[0][part, :], way[...], preferred_element_type=F32)
            for term in terms[1:]:
                q = q + jnp.dot(term[part, :], way[...], preferred_element_type=F32)
            image[part, :] = q
            for n in range(0, DOT_ROWS, CHUNK):
                total = total + way[at + n : at + n + CHUNK, :].astype(F32) * q[n : n + CHUNK, :]
        curve_ref[...] = fold(total)

    def unfinished(carry):
        step, left, more = carry
        return jnp.logical_and(step < MAX_STEPS, left > 0.0)

    def advance(carry):
        step, left, more = carry

        @pl.when(hard)
        def _():
            apply(high, low, least)

        @pl.when(jnp.logical_and(jnp.logical_not(hard), more > 0.0))
        def _():
            apply(high, low)

        @pl.when(jnp.logical_and(jnp.logical_not(hard), jnp.logical_not(more > 0.0)))
        def _():
            apply(high)

        norm = norm_ref[...]
        curve = curve_ref[...]
        alpha = jnp.where(curve > 0.0, norm / jnp.where(curve > 0.0, curve, 1.0), 0.0)
        total = jnp.zeros((CHUNK, RIGHTS), F32)
        for at in range(0, WIDTH, CHUNK):
            part = slice(at, at + CHUNK)
            r = res[part, :] - alpha * image[part, :]
            res[part, :] = r
            total = total + r * r
        fresh = fold(total)
        beta = jnp.where(norm > 0.0, fresh / jnp.where(norm > 0.0, norm, 1.0), 0.0)
        norm_ref[...] = fresh
        for at in range(0, WIDTH, CHUNK):
            part = slice(at, at + CHUNK)
            p = way[part, :].astype(F32)
            sol[part, :] += alpha * p
            way[part, :] = (res[part, :] + beta * p).astype(BF16)
        return step + 1, jnp.max(fresh - bound), jnp.max(fresh - rough)

    lax.while_loop(unfinished, advance, (jnp.int32(0), jnp.max(norm - bound), jnp.max(norm - rough)))
    for i in range(BLOCKS):
        out[span(i), :] = (sol[span(i), :] * twice(side[span(i), :] * scale)).astype(BF16)


def swap_halves(mine, out, own_s, send, recv):
    x, y, z, core = position()
    sibling = device(x, y, z, 1 - core)
    signal(pltpu.get_barrier_semaphore(), sibling)
    own = pltpu.make_async_copy(mine, out.at[core], own_s)
    own.start()
    pl.semaphore_wait(pltpu.get_barrier_semaphore(), 1)
    copy = remote(mine, out.at[core], send, recv, sibling)
    copy.start()
    own.wait()
    copy.wait_send()
    theirs = out.at[1 - core]
    remote(theirs, theirs, send, recv, sibling).wait_recv()


def score(feat, pre, out, held, sems):
    copies = []
    for n in range(2):
        columns = pl.ds(n * 256, 256)
        held[:, columns] = jnp.dot(feat[...], pre[n], preferred_element_type=F32)
        copies.append(pltpu.make_async_copy(held.at[:, columns], out.at[:, columns], sems.at[n]))
        copies[n].start()
    for copy in copies:
        copy.wait()


def on_device(features, targets):
    dma = pltpu.SemaphoreType.DMA
    vmem = pl.BlockSpec(memory_space=pltpu.VMEM)
    anywhere = pl.BlockSpec(memory_space=pl.ANY)
    hbm = pl.BlockSpec(memory_space=pltpu.HBM)
    packed, rights = pl.pallas_call(
        gram_sum,
        name="gram_sum",
        out_shape=(
            jax.ShapeDtypeStruct((4 * UNIT, TILE), F32),
            jax.ShapeDtypeStruct((2, 4, 2, 16, WIDTH), BF16),
        ),
        in_specs=[hbm, hbm],
        out_specs=(vmem, vmem),
        scratch_shapes=[
            pltpu.VMEM((features.shape[0], WIDTH + WIDTH // 2), BF16),
            pltpu.VMEM((4 * UNIT, TILE), F32),
            pltpu.VMEM((2 * UNIT, TILE), F32),
            pltpu.VMEM((2, 3, QUARTERS, TILE), F32),
            pltpu.VMEM((2, 3, SIXTEENTHS, TILE), F32),
            pltpu.VMEM((NZ, PIECE[0], TILE), F32),
            pltpu.VMEM((NZ, PIECE[1], TILE), F32),
            pltpu.VMEM((NZ, PIECE[0], TILE), F32),
            pltpu.VMEM((NZ, PIECE[1], TILE), F32),
            pltpu.VMEM((NZ, PIECE[0], TILE), F32),
            pltpu.VMEM((NZ, PIECE[1], TILE), F32),
            pltpu.VMEM((1, WIDTH), BF16),
            pltpu.VMEM((8, TILE), F32),
            pltpu.VMEM((NZ * 8, TILE), F32),
            pltpu.VMEM((4, 16, WIDTH), BF16),
            pltpu.VMEM((64, WIDTH), F32),
            pltpu.VMEM((4, 16, WIDTH), BF16),
            dma((3,)), dma((16,)), dma((16,)),
            dma((16,)), dma((16,)), dma((16,)), dma((16,)),
            dma((2, NZ)), dma((2, NZ)), dma((2, NZ)), dma((2, NZ)),
            dma((16,)), dma((16,)), dma((16,)), dma((16,)), dma((16,)), dma((16,)),
            dma((NZ,)), dma((NZ,)), dma((4,)), dma((4,)), dma((4,)), dma((4,)),
            pltpu.SemaphoreType.REGULAR((3,)),
        ],
        compiler_params=pltpu.CompilerParams(
            collective_id=0, has_side_effects=True, vmem_limit_bytes=40 * 2**20
        ),
    )(
        pltpu.with_memory_space_constraint(features, pltpu.HBM),
        pltpu.with_memory_space_constraint(targets, pltpu.HBM),
    )

    total_rows = features.shape[0] * lax.axis_size("loop") * lax.axis_size("group")
    precond = pl.pallas_call(
        functools.partial(solve, total_rows / WIDTH**0.5, 0.05),
        name="solve",
        out_shape=jax.ShapeDtypeStruct((WIDTH, RIGHTS), BF16),
        in_specs=[vmem, vmem],
        out_specs=vmem,
        scratch_shapes=[
            pltpu.VMEM((WIDTH, WIDTH), BF16),
            pltpu.VMEM((WIDTH, WIDTH), BF16),
            pltpu.VMEM((WIDTH, WIDTH), BF16),
            pltpu.VMEM((WIDTH, TILE), F32),
            pltpu.VMEM((WIDTH, RIGHTS), F32),
            pltpu.VMEM((WIDTH, RIGHTS), F32),
            pltpu.VMEM((WIDTH, RIGHTS), BF16),
            pltpu.VMEM((WIDTH, RIGHTS), F32),
            pltpu.VMEM((1, WIDTH), F32),
            pltpu.VMEM((1, RIGHTS), F32),
            pltpu.VMEM((1, RIGHTS), F32),
        ],
        compiler_params=pltpu.CompilerParams(vmem_limit_bytes=40 * 2**20),
    )(packed, rights.reshape(RIGHTS, WIDTH))

    everyone = pl.pallas_call(
        swap_halves,
        name="swap_halves",
        out_shape=jax.ShapeDtypeStruct((2, WIDTH, RIGHTS), BF16),
        in_specs=[vmem],
        out_specs=vmem,
        scratch_shapes=[dma, dma, dma],
        compiler_params=pltpu.CompilerParams(
            collective_id=1, has_side_effects=True, vmem_limit_bytes=16 * 2**20
        ),
    )(precond)

    return pl.pallas_call(
        score,
        name="score",
        out_shape=jax.ShapeDtypeStruct((features.shape[0], 512), F32),
        in_specs=[vmem, vmem],
        out_specs=anywhere,
        scratch_shapes=[pltpu.VMEM((features.shape[0], 512), F32), dma((2,))],
        compiler_params=pltpu.CompilerParams(vmem_limit_bytes=16 * 2**20),
    )(features, everyone)


def solution(mesh):
    return jax.shard_map(
        on_device,
        mesh=mesh,
        in_specs=(P(("loop", "group"), None), P(("loop", "group"), None)),
        out_specs=P(("loop", "group"), None),
        check_vma=False,
    )
```

```python
import functools

import jax
import jax.numpy as jnp
from jax import lax
from jax.experimental import pallas as pl
from jax.experimental.pallas import tpu as pltpu
from jax.sharding import PartitionSpec as P

WIDTH = 1024
TILE = 128
BLOCKS = WIDTH // TILE
UPPER, LOWER = 5, 4
UNIT = (UPPER + LOWER) * TILE
NZ = 16
AROUND = (-4, 3, -3, 2, -2, 1, -1)
START = (0, UPPER * TILE)
SIZE = (UPPER * TILE, LOWER * TILE)
QUARTER = tuple(size // 4 for size in SIZE)
SIXTEENTH = tuple(size // 16 for size in SIZE)
PIECE = tuple(size // 8 // NZ for size in SIZE)
QUARTERS, SIXTEENTHS = sum(QUARTER), sum(SIXTEENTH)
RIGHTS = 256
TOL = 1e-4
ROUGH = 1e-2
MAX_STEPS = 4096
CHUNK = 32
DOT_ROWS = 256
MESH = pl.DeviceIdType.MESH
F32 = jnp.float32
BF16 = jnp.bfloat16


def position():
    loop = lax.axis_index("loop")
    group = lax.axis_index("group")
    x = loop // 8
    y = group // 4
    z = (group % 4) * 4 + (loop // 2) % 4
    return x, y, z, loop % 2


def device(x, y, z, core):
    return (x * 8 + (z % 4) * 2 + core, y * 4 + z // 4)


def remote(src, dst, send, recv, to):
    return pltpu.make_async_remote_copy(
        src_ref=src, dst_ref=dst, send_sem=send, recv_sem=recv, device_id=to, device_id_type=MESH
    )


def signal(sem, to):
    pl.semaphore_signal(sem, inc=1, device_id=to, device_id_type=MESH)


def rows(start, size, unit=8):
    return pl.ds(pl.multiple_of(start, unit), size)


def far_first(k):
    return 8 + ((k + 1) // 2) * (1 - 2 * (k % 2))


def gram_sum(
    feat, tgt, out, rights, wide, packed, from_core, land1, land2, zsrc0, zsrc1, zland0, zland1, zout0, zout1,
    line, tsrc, tz, yblock, ywide, xblock,
    load_s, core_s, core_r, e1_s, e1_r, e2_s, e2_r, z_s, z_r, za_s, za_r,
    g2_s, g2_r, g1_s, g1_r, cag_s, cag_r, tz_s, tz_r, ty_s, ty_r, tx_s, tx_r, known,
):
    zsrc, zland, zout = (zsrc0, zsrc1), (zland0, zland1), (zout0, zout1)
    x, y, z, core = position()
    sibling = device(x, y, z, 1 - core)

    def on_x(t):
        return device((x + t) % 4, y, z, core)

    def on_y(t):
        return device(x, (y + t) % 4, z, core)

    def on_z(t):
        return device(x, y, (z + t) % NZ, core)

    def over(axis, t):
        return on_x(t) if axis == 0 else on_y(t)

    here = (x, y)
    ring = (2, 1, 3)
    parts = (0, 1)
    units = (0, 1)

    barrier = pltpu.get_barrier_semaphore()
    signal(barrier, sibling)
    for t in (1, 2, 3):
        signal(barrier, on_x(t))
        signal(barrier, on_y(t))
    signal(barrier, on_z(1))
    signal(barrier, on_z(NZ - 1))

    loads = [
        pltpu.make_async_copy(feat, wide.at[:, pl.ds(0, WIDTH)], load_s.at[0]),
        pltpu.make_async_copy(feat.at[:, pl.ds(0, WIDTH // 2)], wide.at[:, pl.ds(WIDTH, WIDTH // 2)], load_s.at[1]),
        pltpu.make_async_copy(tgt, line, load_s.at[2]),
    ]
    for load in loads:
        load.start()
    for load in loads:
        load.wait()

    def begin(who, j, h):
        return (2 * who + j) * UNIT + START[h]

    def quarter(j, h, t):
        return begin(core, j, h) + ((here[j] + t) % 4) * QUARTER[h]

    def sixteenth(j, h, t):
        return quarter(j, h, 0) + ((here[1 - j] + t) % 4) * SIXTEENTH[h]

    def slot(j, h, t):
        return (h * 2 + j) * 4 + t

    def part_gram(who, j, h):
        i = 2 * who + j + 4 * h
        kept = (UPPER, LOWER)[h]
        left = wide[:, rows(i * TILE, TILE, TILE)]
        span = wide[:, rows(i * TILE, kept * TILE, TILE)]
        product = lax.dot_general(left, span, (((0,), (0,)), ((), ())), preferred_element_type=F32)
        for d in range(kept):
            packed[rows(begin(who, j, h) + d * TILE, TILE), :] = product[:, d * TILE : (d + 1) * TILE]

    def core_landing(j, h, t):
        return pl.ds((j * 4 + t) * QUARTERS + h * QUARTER[0], QUARTER[h])

    def core_copy(j, h, t):
        n = slot(j, h, t)
        at = begin(1 - core, j, h) + ((here[j] + t) % 4) * QUARTER[h]
        return remote(
            packed.at[rows(at, QUARTER[h])], from_core.at[core_landing(j, h, t)], core_s.at[n], core_r.at[n], sibling
        )

    part_gram(1 - core, 0, 0)
    pl.semaphore_wait(barrier, 9)
    core_copy(0, 0, 2).start()
    signal(known.at[0], on_z(1))
    signal(known.at[0], on_z(NZ - 1))
    part_gram(1 - core, 1, 0)
    core_copy(1, 0, 2).start()
    for t in (1, 3, 0):
        for j in units:
            core_copy(j, 0, t).start()
    for j in units:
        part_gram(1 - core, j, 1)
    for t in (2, 1, 3, 0):
        for j in units:
            core_copy(j, 1, t).start()
    for h in parts:
        for j in units:
            part_gram(core, j, h)

    def first_landing(h):
        return pl.ds(h * QUARTER[0], QUARTER[h])

    def second_landing(h):
        return pl.ds(h * SIXTEENTH[0], SIXTEENTH[h])

    def first(j, h, t):
        n = slot(j, h, t)
        return remote(
            packed.at[rows(quarter(j, h, t), QUARTER[h])], land1.at[j, t - 1, first_landing(h)],
            e1_s.at[n], e1_r.at[n], over(j, t),
        )

    def second(j, h, t):
        n = slot(j, h, t)
        return remote(
            packed.at[rows(sixteenth(j, h, t), SIXTEENTH[h])], land2.at[j, t - 1, second_landing(h)],
            e2_s.at[n], e2_r.at[n], over(1 - j, t),
        )

    for h in parts:
        for t in (2, 1, 3, 0):
            for j in units:
                core_copy(j, h, t).wait_recv()
                packed[rows(quarter(j, h, t), QUARTER[h]), :] += from_core[core_landing(j, h, t), :]
                if t:
                    first(j, h, t).start()

    for k in range(8):
        tsrc[k : k + 1, :] = line[:, k * TILE : (k + 1) * TILE].astype(F32)
    tz[rows(z * 8, 8), :] = tsrc[...]
    for h in parts:
        for t in range(4):
            for j in units:
                core_copy(j, h, t).wait_send()
    pl.semaphore_wait(known.at[0], 2)
    signal(known.at[1], on_z(2))
    signal(known.at[1], on_z(NZ - 2))

    def add_first(h):
        for j in units:
            for t in ring:
                first(j, h, t).wait()
            at = rows(quarter(j, h, 0), QUARTER[h])
            landed = first_landing(h)
            packed[at, :] += land1[j, 0, landed, :] + land1[j, 1, landed, :] + land1[j, 2, landed, :]
            for t in ring:
                second(j, h, t).start()

    add_first(0)
    pl.semaphore_wait(known.at[1], 2)
    signal(known.at[2], on_z(4))
    signal(known.at[2], on_z(NZ - 4))
    add_first(1)
    pl.semaphore_wait(known.at[2], 2)

    def all_z(copy):
        def body(k, carry):
            copy(far_first(k)).start()
            return carry

        lax.fori_loop(0, NZ - 1, body, 0)

    def end_z(copy, landing, recv):
        def body(k, carry):
            t = far_first(k)
            copy(t).wait_send()
            other = (z + t) % NZ
            ref = landing(other)
            remote(ref, ref, recv.at[other], recv.at[other], sibling).wait_recv()
            return carry

        lax.fori_loop(0, NZ - 1, body, 0)

    def target_row(k):
        return tz.at[rows(k * 8, 8)]

    def t_copy(t):
        return remote(target_row(z), target_row(z), tz_s.at[t], tz_r.at[z], on_z(t))

    all_z(t_copy)

    def z_copy(h, t):
        n = t + 4
        return remote(zsrc[h].at[(z + t + NZ) % 8], zland[h].at[n], z_s.at[h, n], z_r.at[h, n], on_z(t + NZ))

    def za_copy(h):
        def copy(t):
            return remote(zout[h].at[z], zout[h].at[z], za_s.at[h, t], za_r.at[h, z], on_z(t))

        return copy

    for h in parts:
        for j in units:
            for t in ring:
                second(j, h, t).wait()
            at = rows(sixteenth(j, h, 0), SIXTEENTH[h])
            landed = second_landing(h)
            block = packed[at, :] + land2[j, 0, landed, :] + land2[j, 1, landed, :] + land2[j, 2, landed, :]
            for m in range(8):
                zsrc[h][m, j] = block[m * PIECE[h] : (m + 1) * PIECE[h], :]
        for t in AROUND:
            z_copy(h, t).start()
        zland[h][4] = zsrc[h][z % 8]

    end_z(t_copy, target_row, tz_r)
    for k in range(8):
        for low in range(4):
            ywide[low * 4 : low * 4 + 4, k * TILE : (k + 1) * TILE] = tz[pl.ds(low * 8 + k, 4, stride=32), :]
    yblock[y] = ywide[0:16, :].astype(BF16)

    def y_copy(t):
        return remote(yblock.at[y], yblock.at[y], ty_s.at[t], ty_r.at[t], on_y(t))

    for t in ring:
        y_copy(t).start()

    for h in parts:
        for t in AROUND:
            z_copy(h, t).wait()
        total = zland[h][0]
        for k in range(1, 8):
            total = total + zland[h][k]
        zout[h][z] = total
        all_z(za_copy(h))

    for t in ring:
        y_copy(t).wait_send()
        ref = yblock.at[(y + 4 - t) % 4]
        remote(ref, ref, ty_s.at[t], ty_r.at[t], sibling).wait_recv()
    for yy in range(4):
        block = yblock[yy].astype(F32)
        for low in range(4):
            ywide[low * 16 + yy * 4 : low * 16 + yy * 4 + 4, :] = block[low * 4 : low * 4 + 4, :]
    for low in range(4):
        xblock[low] = ywide[low * 16 : low * 16 + 16, :].astype(BF16)

    solver = x // 2
    stays = solver == core

    def x_copy(t):
        to = device((x + t) % 4, y, z, solver)
        return remote(xblock, rights.at[x % 2, :, core], tx_s.at[t], tx_r.at[(x % 2) * 2 + core], to)

    for t in ring:
        x_copy(t).start()
    stay = pltpu.make_async_copy(xblock, rights.at[x % 2, :, core], tx_s.at[0])

    @pl.when(stays)
    def _():
        stay.start()

    @pl.when(jnp.logical_not(stays))
    def _():
        x_copy(0).start()

    def gather(j, h, t, stage):
        if stage == 2:
            mine, theirs, size, axis = sixteenth(j, h, 0), sixteenth(j, h, 4 - t), SIXTEENTH[h], 1 - j
            send, recv = g2_s, g2_r
        else:
            mine, theirs, size, axis = quarter(j, h, 0), quarter(j, h, 4 - t), QUARTER[h], j
            send, recv = g1_s, g1_r
        a, b = out.at[rows(mine, size)], out.at[rows(theirs, size)]
        n = slot(j, h, t)
        return (
            remote(a, a, send.at[n], recv.at[n], over(axis, t)),
            remote(b, b, send.at[n], recv.at[n], over(axis, t)),
        )

    def core_gather(j, h, t, who):
        at = begin(who, j, h) + ((here[j] + 4 - t) % 4) * QUARTER[h]
        ref = out.at[rows(at, QUARTER[h])]
        n = slot(j, h, t)
        return remote(ref, ref, cag_s.at[n], cag_r.at[n], sibling)

    for h in parts:
        end_z(za_copy(h), lambda k: zout[h].at[k], za_r.at[h])
        for j in units:
            out[rows(sixteenth(j, h, 0), SIXTEENTH[h]), :] = jnp.concatenate(
                [zout[h][m, j] + zout[h][m + 8, j] for m in range(8)], axis=0
            )
            for t in ring:
                gather(j, h, t, 2)[0].start()
    for h in parts:
        for j in units:
            for t in ring:
                send, recv = gather(j, h, t, 2)
                send.wait_send()
                recv.wait_recv()
            for t in ring:
                gather(j, h, t, 1)[0].start()
            core_gather(j, h, 0, core).start()
    for h in parts:
        for t in (1, 3, 2):
            for j in units:
                gather(j, h, t, 1)[1].wait_recv()
                core_gather(j, h, t, core).start()
    for t in ring:
        x_copy(t).wait_send()
        for h in parts:
            for j in units:
                gather(j, h, t, 1)[0].wait_send()

    @pl.when(stays)
    def _():
        stay.wait()

    @pl.when(jnp.logical_not(stays))
    def _():
        x_copy(0).wait_send()

    for near in range(2):
        for who in range(2):

            @pl.when(jnp.logical_or(2 * core + near != x, who != core))
            def _():
                ref = rights.at[near, :, who]
                remote(ref, ref, tx_s.at[0], tx_r.at[near * 2 + who], sibling).wait_recv()

    for h in parts:
        for t in (0, 1, 3, 2):
            for j in units:
                core_gather(j, h, t, core).wait_send()
                core_gather(j, h, t, 1 - core).wait_recv()


def solve(scale, damping, packed, rights, out, high, low, least, side, sol, res, way, image, diag, norm_ref, curve_ref):
    eye = lax.broadcasted_iota(jnp.int32, (TILE, TILE), 0) == lax.broadcasted_iota(jnp.int32, (TILE, TILE), 1)

    def tile(i, d):
        start = (i % 4) * UNIT + (i // 4) * UPPER * TILE + d * TILE
        return packed[start : start + TILE, :]

    def kept(i):
        return UPPER if i < 4 else LOWER

    def span(i):
        return slice(i * TILE, (i + 1) * TILE)

    for i in range(BLOCKS):
        diag[:, span(i)] = jnp.sum(jnp.where(eye, tile(i, 0), 0.0), axis=0, keepdims=True)
    shift = jnp.sum(diag[...], axis=1, keepdims=True) * (damping / WIDTH)
    per_shift = 1.0 / shift
    diag[...] = lax.rsqrt(diag[...] + shift)
    for i in range(BLOCKS):
        side[span(i), :] = jnp.broadcast_to(diag[:, span(i)], (TILE, TILE)).T

    def scaled(i, d):
        values = tile(i, d)
        if d == 0:
            values = values + jnp.where(eye, shift, 0.0)
        return values * side[span(i), :] * diag[:, span((i + d) % BLOCKS)]

    squares = jnp.zeros((TILE, TILE), F32)
    for i in range(BLOCKS):
        for d in range(kept(i)):
            j = (i + d) % BLOCKS
            off = tile(i, d) * per_shift
            if d == 0:
                off = jnp.where(eye, 0.0, off)
                squares = squares + 0.5 * off * off
            else:
                squares = squares + off * off
            values = scaled(i, d)
            top = values.astype(BF16)
            rest = (values - top.astype(F32)).astype(BF16)
            high[span(i), span(j)] = top
            low[span(i), span(j)] = rest
            if d:
                high[span(j), span(i)] = top.T
                low[span(j), span(i)] = rest.T
    hard = 2.0 * jnp.sum(squares) > 256.0**2

    @pl.when(hard)
    def _():
        for i in range(BLOCKS):
            for d in range(kept(i)):
                j = (i + d) % BLOCKS
                values = scaled(i, d)
                rest = values - values.astype(BF16).astype(F32)
                last = (rest - rest.astype(BF16).astype(F32)).astype(BF16)
                least[span(i), span(j)] = last
                if d:
                    least[span(j), span(i)] = last.T

    def fold(total):
        return jnp.sum(total, axis=0, keepdims=True)

    def twice(values):
        return jnp.concatenate([values, values], axis=1)

    total = jnp.zeros((TILE, RIGHTS), F32)
    for i in range(BLOCKS):
        turned = jnp.concatenate([rights[span(h), span(i)].T for h in range(RIGHTS // TILE)], axis=1)
        b = turned.astype(F32) * twice(side[span(i), :])
        res[span(i), :] = b
        way[span(i), :] = b.astype(BF16)
        sol[span(i), :] = jnp.zeros((TILE, RIGHTS), F32)
        total = total + b * b
    norm = fold(total)
    norm_ref[...] = norm
    bound = norm * (TOL * TOL)
    rough = norm * (ROUGH * ROUGH)

    def apply(*terms):
        total = jnp.zeros((CHUNK, RIGHTS), F32)
        for at in range(0, WIDTH, DOT_ROWS):
            part = slice(at, at + DOT_ROWS)
            q = jnp.dot(terms[0][part, :], way[...], preferred_element_type=F32)
            for term in terms[1:]:
                q = q + jnp.dot(term[part, :], way[...], preferred_element_type=F32)
            image[part, :] = q
            for n in range(0, DOT_ROWS, CHUNK):
                total = total + way[at + n : at + n + CHUNK, :].astype(F32) * q[n : n + CHUNK, :]
        curve_ref[...] = fold(total)

    def unfinished(carry):
        step, left, more = carry
        return jnp.logical_and(step < MAX_STEPS, left > 0.0)

    def advance(carry):
        step, left, more = carry

        @pl.when(hard)
        def _():
            apply(high, low, least)

        @pl.when(jnp.logical_and(jnp.logical_not(hard), more > 0.0))
        def _():
            apply(high, low)

        @pl.when(jnp.logical_and(jnp.logical_not(hard), jnp.logical_not(more > 0.0)))
        def _():
            apply(high)

        norm = norm_ref[...]
        curve = curve_ref[...]
        alpha = jnp.where(curve > 0.0, norm / jnp.where(curve > 0.0, curve, 1.0), 0.0)
        total = jnp.zeros((CHUNK, RIGHTS), F32)
        for at in range(0, WIDTH, CHUNK):
            part = slice(at, at + CHUNK)
            r = res[part, :] - alpha * image[part, :]
            res[part, :] = r
            total = total + r * r
        fresh = fold(total)
        beta = jnp.where(norm > 0.0, fresh / jnp.where(norm > 0.0, norm, 1.0), 0.0)
        norm_ref[...] = fresh
        for at in range(0, WIDTH, CHUNK):
            part = slice(at, at + CHUNK)
            p = way[part, :].astype(F32)
            sol[part, :] += alpha * p
            way[part, :] = (res[part, :] + beta * p).astype(BF16)
        return step + 1, jnp.max(fresh - bound), jnp.max(fresh - rough)

    lax.while_loop(unfinished, advance, (jnp.int32(0), jnp.max(norm - bound), jnp.max(norm - rough)))
    for i in range(BLOCKS):
        out[span(i), :] = (sol[span(i), :] * twice(side[span(i), :] * scale)).astype(BF16)


def swap_halves(mine, out, own_s, send, recv):
    x, y, z, core = position()
    sibling = device(x, y, z, 1 - core)
    signal(pltpu.get_barrier_semaphore(), sibling)
    own = pltpu.make_async_copy(mine, out.at[core], own_s)
    own.start()
    pl.semaphore_wait(pltpu.get_barrier_semaphore(), 1)
    copy = remote(mine, out.at[core], send, recv, sibling)
    copy.start()
    own.wait()
    copy.wait_send()
    theirs = out.at[1 - core]
    remote(theirs, theirs, send, recv, sibling).wait_recv()


def score(feat, pre, out, held, sems):
    copies = []
    for n in range(2):
        columns = pl.ds(n * 256, 256)
        held[:, columns] = jnp.dot(feat[...], pre[n], preferred_element_type=F32)
        copies.append(pltpu.make_async_copy(held.at[:, columns], out.at[:, columns], sems.at[n]))
        copies[n].start()
    for copy in copies:
        copy.wait()


def on_device(features, targets):
    dma = pltpu.SemaphoreType.DMA
    vmem = pl.BlockSpec(memory_space=pltpu.VMEM)
    anywhere = pl.BlockSpec(memory_space=pl.ANY)
    hbm = pl.BlockSpec(memory_space=pltpu.HBM)
    packed, rights = pl.pallas_call(
        gram_sum,
        name="gram_sum",
        out_shape=(
            jax.ShapeDtypeStruct((4 * UNIT, TILE), F32),
            jax.ShapeDtypeStruct((2, 4, 2, 16, WIDTH), BF16),
        ),
        in_specs=[hbm, hbm],
        out_specs=(vmem, vmem),
        scratch_shapes=[
            pltpu.VMEM((features.shape[0], WIDTH + WIDTH // 2), BF16),
            pltpu.VMEM((4 * UNIT, TILE), F32),
            pltpu.VMEM((2 * UNIT, TILE), F32),
            pltpu.VMEM((2, 3, QUARTERS, TILE), F32),
            pltpu.VMEM((2, 3, SIXTEENTHS, TILE), F32),
            pltpu.VMEM((8, 2, PIECE[0], TILE), F32),
            pltpu.VMEM((8, 2, PIECE[1], TILE), F32),
            pltpu.VMEM((8, 2, PIECE[0], TILE), F32),
            pltpu.VMEM((8, 2, PIECE[1], TILE), F32),
            pltpu.VMEM((NZ, 2, PIECE[0], TILE), F32),
            pltpu.VMEM((NZ, 2, PIECE[1], TILE), F32),
            pltpu.VMEM((1, WIDTH), BF16),
            pltpu.VMEM((8, TILE), F32),
            pltpu.VMEM((NZ * 8, TILE), F32),
            pltpu.VMEM((4, 16, WIDTH), BF16),
            pltpu.VMEM((64, WIDTH), F32),
            pltpu.VMEM((4, 16, WIDTH), BF16),
            dma((3,)), dma((16,)), dma((16,)),
            dma((16,)), dma((16,)), dma((16,)), dma((16,)),
            dma((2, 8)), dma((2, 8)), dma((2, NZ)), dma((2, NZ)),
            dma((16,)), dma((16,)), dma((16,)), dma((16,)), dma((16,)), dma((16,)),
            dma((NZ,)), dma((NZ,)), dma((4,)), dma((4,)), dma((4,)), dma((4,)),
            pltpu.SemaphoreType.REGULAR((3,)),
        ],
        compiler_params=pltpu.CompilerParams(
            collective_id=0, has_side_effects=True, vmem_limit_bytes=40 * 2**20
        ),
    )(
        pltpu.with_memory_space_constraint(features, pltpu.HBM),
        pltpu.with_memory_space_constraint(targets, pltpu.HBM),
    )

    total_rows = features.shape[0] * lax.axis_size("loop") * lax.axis_size("group")
    precond = pl.pallas_call(
        functools.partial(solve, total_rows / WIDTH**0.5, 0.05),
        name="solve",
        out_shape=jax.ShapeDtypeStruct((WIDTH, RIGHTS), BF16),
        in_specs=[vmem, vmem],
        out_specs=vmem,
        scratch_shapes=[
            pltpu.VMEM((WIDTH, WIDTH), BF16),
            pltpu.VMEM((WIDTH, WIDTH), BF16),
            pltpu.VMEM((WIDTH, WIDTH), BF16),
            pltpu.VMEM((WIDTH, TILE), F32),
            pltpu.VMEM((WIDTH, RIGHTS), F32),
            pltpu.VMEM((WIDTH, RIGHTS), F32),
            pltpu.VMEM((WIDTH, RIGHTS), BF16),
            pltpu.VMEM((WIDTH, RIGHTS), F32),
            pltpu.VMEM((1, WIDTH), F32),
            pltpu.VMEM((1, RIGHTS), F32),
            pltpu.VMEM((1, RIGHTS), F32),
        ],
        compiler_params=pltpu.CompilerParams(vmem_limit_bytes=40 * 2**20),
    )(packed, rights.reshape(RIGHTS, WIDTH))

    everyone = pl.pallas_call(
        swap_halves,
        name="swap_halves",
        out_shape=jax.ShapeDtypeStruct((2, WIDTH, RIGHTS), BF16),
        in_specs=[vmem],
        out_specs=vmem,
        scratch_shapes=[dma, dma, dma],
        compiler_params=pltpu.CompilerParams(
            collective_id=1, has_side_effects=True, vmem_limit_bytes=16 * 2**20
        ),
    )(precond)

    return pl.pallas_call(
        score,
        name="score",
        out_shape=jax.ShapeDtypeStruct((features.shape[0], 512), F32),
        in_specs=[vmem, vmem],
        out_specs=anywhere,
        scratch_shapes=[pltpu.VMEM((features.shape[0], 512), F32), dma((2,))],
        compiler_params=pltpu.CompilerParams(vmem_limit_bytes=16 * 2**20),
    )(features, everyone)


def solution(mesh):
    return jax.shard_map(
        on_device,
        mesh=mesh,
        in_specs=(P(("loop", "group"), None), P(("loop", "group"), None)),
        out_specs=P(("loop", "group"), None),
        check_vma=False,
    )
```

```python
import functools

import jax
import jax.numpy as jnp
from jax import lax
from jax.experimental import pallas as pl
from jax.experimental.pallas import tpu as pltpu
from jax.sharding import PartitionSpec as P

WIDTH = 1024
TILE = 128
BLOCKS = WIDTH // TILE
UPPER, LOWER = 5, 4
UNIT = (UPPER + LOWER) * TILE
NZ = 16
AROUND = (-4, 3, -3, 2, -2, 1, -1)
START = (0, UPPER * TILE)
SIZE = (UPPER * TILE, LOWER * TILE)
QUARTER = tuple(size // 4 for size in SIZE)
SIXTEENTH = tuple(size // 16 for size in SIZE)
PIECE = tuple(size // 8 // NZ for size in SIZE)
QUARTERS, SIXTEENTHS = sum(QUARTER), sum(SIXTEENTH)
RIGHTS = 256
TOL = 1e-4
ROUGH = 1e-2
MAX_STEPS = 4096
CHUNK = 32
DOT_ROWS = 256
MESH = pl.DeviceIdType.MESH
F32 = jnp.float32
BF16 = jnp.bfloat16


def position():
    loop = lax.axis_index("loop")
    group = lax.axis_index("group")
    x = loop // 8
    y = group // 4
    z = (group % 4) * 4 + (loop // 2) % 4
    return x, y, z, loop % 2


def device(x, y, z, core):
    return (x * 8 + (z % 4) * 2 + core, y * 4 + z // 4)


def remote(src, dst, send, recv, to):
    return pltpu.make_async_remote_copy(
        src_ref=src, dst_ref=dst, send_sem=send, recv_sem=recv, device_id=to, device_id_type=MESH
    )


def signal(sem, to):
    pl.semaphore_signal(sem, inc=1, device_id=to, device_id_type=MESH)


def rows(start, size, unit=8):
    return pl.ds(pl.multiple_of(start, unit), size)


def far_first(k):
    return 8 + ((k + 1) // 2) * (1 - 2 * (k % 2))


def gram_sum(
    feat, tgt, out, rights, wide, packed, from_core, land1, land2, zsrc0, zsrc1, zland0, zland1, zout0, zout1,
    line, tsrc, tz, yblock, ywide, xblock,
    load_s, core_s, core_r, e1_s, e1_r, e2_s, e2_r, z_s, z_r, za_s, za_r,
    g2_s, g2_r, g1_s, g1_r, cag_s, cag_r, tz_s, tz_r, ty_s, ty_r, tx_s, tx_r, known,
):
    zsrc, zland, zout = (zsrc0, zsrc1), (zland0, zland1), (zout0, zout1)
    x, y, z, core = position()
    sibling = device(x, y, z, 1 - core)

    def on_x(t):
        return device((x + t) % 4, y, z, core)

    def on_y(t):
        return device(x, (y + t) % 4, z, core)

    def on_z(t):
        return device(x, y, (z + t) % NZ, core)

    def over(axis, t):
        return on_x(t) if axis == 0 else on_y(t)

    here = (x, y)
    ring = (2, 1, 3)
    parts = (0, 1)
    units = (0, 1)

    barrier = pltpu.get_barrier_semaphore()
    signal(barrier, sibling)
    for t in (1, 2, 3):
        signal(barrier, on_x(t))
        signal(barrier, on_y(t))
    signal(barrier, on_z(1))
    signal(barrier, on_z(NZ - 1))

    loads = [
        pltpu.make_async_copy(feat, wide.at[:, pl.ds(0, WIDTH)], load_s.at[0]),
        pltpu.make_async_copy(feat.at[:, pl.ds(0, WIDTH // 2)], wide.at[:, pl.ds(WIDTH, WIDTH // 2)], load_s.at[1]),
        pltpu.make_async_copy(tgt, line, load_s.at[2]),
    ]
    for load in loads:
        load.start()
    loads[0].wait()

    def begin(who, j, h):
        return (2 * who + j) * UNIT + START[h]

    def quarter(j, h, t):
        return begin(core, j, h) + ((here[j] + t) % 4) * QUARTER[h]

    def sixteenth(j, h, t):
        return quarter(j, h, 0) + ((here[1 - j] + t) % 4) * SIXTEENTH[h]

    def slot(j, h, t):
        return (h * 2 + j) * 4 + t

    def part_gram(who, j, h):
        i = 2 * who + j + 4 * h
        kept = (UPPER, LOWER)[h]
        left = wide[:, rows(i * TILE, TILE, TILE)]
        span = wide[:, rows(i * TILE, kept * TILE, TILE)]
        product = lax.dot_general(left, span, (((0,), (0,)), ((), ())), preferred_element_type=F32)
        for d in range(kept):
            packed[rows(begin(who, j, h) + d * TILE, TILE), :] = product[:, d * TILE : (d + 1) * TILE]

    def core_landing(j, h, t):
        return pl.ds((j * 4 + t) * QUARTERS + h * QUARTER[0], QUARTER[h])

    def core_copy(j, h, t):
        n = slot(j, h, t)
        at = begin(1 - core, j, h) + ((here[j] + t) % 4) * QUARTER[h]
        return remote(
            packed.at[rows(at, QUARTER[h])], from_core.at[core_landing(j, h, t)], core_s.at[n], core_r.at[n], sibling
        )

    part_gram(1 - core, 0, 0)
    pl.semaphore_wait(barrier, 9)
    core_copy(0, 0, 2).start()
    signal(known.at[0], on_z(1))
    signal(known.at[0], on_z(NZ - 1))
    part_gram(1 - core, 1, 0)
    core_copy(1, 0, 2).start()
    for t in (1, 3, 0):
        for j in units:
            core_copy(j, 0, t).start()
    loads[1].wait()
    for j in units:
        part_gram(1 - core, j, 1)
    for t in (2, 1, 3, 0):
        for j in units:
            core_copy(j, 1, t).start()
    for h in parts:
        for j in units:
            part_gram(core, j, h)
    loads[2].wait()

    def first_landing(h):
        return pl.ds(h * QUARTER[0], QUARTER[h])

    def second_landing(h):
        return pl.ds(h * SIXTEENTH[0], SIXTEENTH[h])

    def first(j, h, t):
        n = slot(j, h, t)
        return remote(
            packed.at[rows(quarter(j, h, t), QUARTER[h])], land1.at[j, t - 1, first_landing(h)],
            e1_s.at[n], e1_r.at[n], over(j, t),
        )

    def second(j, h, t):
        n = slot(j, h, t)
        return remote(
            packed.at[rows(sixteenth(j, h, t), SIXTEENTH[h])], land2.at[j, t - 1, second_landing(h)],
            e2_s.at[n], e2_r.at[n], over(1 - j, t),
        )

    for h in parts:
        for t in (2, 1, 3, 0):
            for j in units:
                core_copy(j, h, t).wait_recv()
                packed[rows(quarter(j, h, t), QUARTER[h]), :] += from_core[core_landing(j, h, t), :]
                if t:
                    first(j, h, t).start()

    for k in range(8):
        tsrc[k : k + 1, :] = line[:, k * TILE : (k + 1) * TILE].astype(F32)
    tz[rows(z * 8, 8), :] = tsrc[...]
    for h in parts:
        for t in range(4):
            for j in units:
                core_copy(j, h, t).wait_send()
    pl.semaphore_wait(known.at[0], 2)
    signal(known.at[1], on_z(2))
    signal(known.at[1], on_z(NZ - 2))

    def add_first(h):
        for j in units:
            for t in ring:
                first(j, h, t).wait()
            at = rows(quarter(j, h, 0), QUARTER[h])
            landed = first_landing(h)
            packed[at, :] += land1[j, 0, landed, :] + land1[j, 1, landed, :] + land1[j, 2, landed, :]
            for t in ring:
                second(j, h, t).start()

    add_first(0)
    pl.semaphore_wait(known.at[1], 2)
    signal(known.at[2], on_z(4))
    signal(known.at[2], on_z(NZ - 4))
    add_first(1)
    pl.semaphore_wait(known.at[2], 2)

    def all_z(copy):
        def body(k, carry):
            copy(far_first(k)).start()
            return carry

        lax.fori_loop(0, NZ - 1, body, 0)

    def end_z(copy, landing, recv):
        def body(k, carry):
            t = far_first(k)
            copy(t).wait_send()
            other = (z + t) % NZ
            ref = landing(other)
            remote(ref, ref, recv.at[other], recv.at[other], sibling).wait_recv()
            return carry

        lax.fori_loop(0, NZ - 1, body, 0)

    def target_row(k):
        return tz.at[rows(k * 8, 8)]

    def t_copy(t):
        return remote(target_row(z), target_row(z), tz_s.at[t], tz_r.at[z], on_z(t))

    all_z(t_copy)

    def z_copy(h, t):
        n = t + 4
        return remote(zsrc[h].at[(z + t + NZ) % 8], zland[h].at[n], z_s.at[h, n], z_r.at[h, n], on_z(t + NZ))

    def za_copy(h):
        def copy(t):
            return remote(zout[h].at[z], zout[h].at[z], za_s.at[h, t], za_r.at[h, z], on_z(t))

        return copy

    for h in parts:
        for j in units:
            for t in ring:
                second(j, h, t).wait()
            at = rows(sixteenth(j, h, 0), SIXTEENTH[h])
            landed = second_landing(h)
            block = packed[at, :] + land2[j, 0, landed, :] + land2[j, 1, landed, :] + land2[j, 2, landed, :]
            for m in range(8):
                zsrc[h][m, j] = block[m * PIECE[h] : (m + 1) * PIECE[h], :]
        for t in AROUND:
            z_copy(h, t).start()
        zland[h][4] = zsrc[h][z % 8]

    end_z(t_copy, target_row, tz_r)
    for k in range(8):
        for low in range(4):
            ywide[low * 4 : low * 4 + 4, k * TILE : (k + 1) * TILE] = tz[pl.ds(low * 8 + k, 4, stride=32), :]
    yblock[y] = ywide[0:16, :].astype(BF16)

    def y_copy(t):
        return remote(yblock.at[y], yblock.at[y], ty_s.at[t], ty_r.at[t], on_y(t))

    for t in ring:
        y_copy(t).start()

    for h in parts:
        for t in AROUND:
            z_copy(h, t).wait()
        total = zland[h][0]
        for k in range(1, 8):
            total = total + zland[h][k]
        zout[h][z] = total
        all_z(za_copy(h))

    for t in ring:
        y_copy(t).wait_send()
        ref = yblock.at[(y + 4 - t) % 4]
        remote(ref, ref, ty_s.at[t], ty_r.at[t], sibling).wait_recv()
    for yy in range(4):
        block = yblock[yy].astype(F32)
        for low in range(4):
            ywide[low * 16 + yy * 4 : low * 16 + yy * 4 + 4, :] = block[low * 4 : low * 4 + 4, :]
    for low in range(4):
        xblock[low] = ywide[low * 16 : low * 16 + 16, :].astype(BF16)

    solver = x // 2
    stays = solver == core

    def x_copy(t):
        to = device((x + t) % 4, y, z, solver)
        return remote(xblock, rights.at[x % 2, :, core], tx_s.at[t], tx_r.at[(x % 2) * 2 + core], to)

    for t in ring:
        x_copy(t).start()
    stay = pltpu.make_async_copy(xblock, rights.at[x % 2, :, core], tx_s.at[0])

    @pl.when(stays)
    def _():
        stay.start()

    @pl.when(jnp.logical_not(stays))
    def _():
        x_copy(0).start()

    def gather(j, h, t, stage):
        if stage == 2:
            mine, theirs, size, axis = sixteenth(j, h, 0), sixteenth(j, h, 4 - t), SIXTEENTH[h], 1 - j
            send, recv = g2_s, g2_r
        else:
            mine, theirs, size, axis = quarter(j, h, 0), quarter(j, h, 4 - t), QUARTER[h], j
            send, recv = g1_s, g1_r
        a, b = out.at[rows(mine, size)], out.at[rows(theirs, size)]
        n = slot(j, h, t)
        return (
            remote(a, a, send.at[n], recv.at[n], over(axis, t)),
            remote(b, b, send.at[n], recv.at[n], over(axis, t)),
        )

    def core_gather(j, h, t, who):
        at = begin(who, j, h) + ((here[j] + 4 - t) % 4) * QUARTER[h]
        ref = out.at[rows(at, QUARTER[h])]
        n = slot(j, h, t)
        return remote(ref, ref, cag_s.at[n], cag_r.at[n], sibling)

    for h in parts:
        end_z(za_copy(h), lambda k: zout[h].at[k], za_r.at[h])
        for j in units:
            out[rows(sixteenth(j, h, 0), SIXTEENTH[h]), :] = jnp.concatenate(
                [zout[h][m, j] + zout[h][m + 8, j] for m in range(8)], axis=0
            )
            for t in ring:
                gather(j, h, t, 2)[0].start()
    for h in parts:
        for j in units:
            for t in ring:
                send, recv = gather(j, h, t, 2)
                send.wait_send()
                recv.wait_recv()
            for t in ring:
                gather(j, h, t, 1)[0].start()
            core_gather(j, h, 0, core).start()
    for h in parts:
        for t in (1, 3, 2):
            for j in units:
                gather(j, h, t, 1)[1].wait_recv()
                core_gather(j, h, t, core).start()
    for t in ring:
        x_copy(t).wait_send()
        for h in parts:
            for j in units:
                gather(j, h, t, 1)[0].wait_send()

    @pl.when(stays)
    def _():
        stay.wait()

    @pl.when(jnp.logical_not(stays))
    def _():
        x_copy(0).wait_send()

    for near in range(2):
        for who in range(2):

            @pl.when(jnp.logical_or(2 * core + near != x, who != core))
            def _():
                ref = rights.at[near, :, who]
                remote(ref, ref, tx_s.at[0], tx_r.at[near * 2 + who], sibling).wait_recv()

    for h in parts:
        for t in (0, 1, 3, 2):
            for j in units:
                core_gather(j, h, t, core).wait_send()
                core_gather(j, h, t, 1 - core).wait_recv()


def solve(damping, packed, rights, sol, side, high, low, least, res, way, image, diag, norm_ref, curve_ref):
    eye = lax.broadcasted_iota(jnp.int32, (TILE, TILE), 0) == lax.broadcasted_iota(jnp.int32, (TILE, TILE), 1)

    def tile(i, d):
        start = (i % 4) * UNIT + (i // 4) * UPPER * TILE + d * TILE
        return packed[start : start + TILE, :]

    def kept(i):
        return UPPER if i < 4 else LOWER

    def span(i):
        return slice(i * TILE, (i + 1) * TILE)

    for i in range(BLOCKS):
        diag[:, span(i)] = jnp.sum(jnp.where(eye, tile(i, 0), 0.0), axis=0, keepdims=True)
    shift = jnp.sum(diag[...], axis=1, keepdims=True) * (damping / WIDTH)
    per_shift = 1.0 / shift
    diag[...] = lax.rsqrt(diag[...] + shift)
    for i in range(BLOCKS):
        side[span(i), :] = jnp.broadcast_to(diag[:, span(i)], (TILE, TILE)).T

    def scaled(i, d):
        values = tile(i, d)
        if d == 0:
            values = values + jnp.where(eye, shift, 0.0)
        return values * side[span(i), :] * diag[:, span((i + d) % BLOCKS)]

    squares = jnp.zeros((TILE, TILE), F32)
    for i in range(BLOCKS):
        for d in range(kept(i)):
            j = (i + d) % BLOCKS
            off = tile(i, d) * per_shift
            if d == 0:
                off = jnp.where(eye, 0.0, off)
                squares = squares + 0.5 * off * off
            else:
                squares = squares + off * off
            values = scaled(i, d)
            top = values.astype(BF16)
            rest = (values - top.astype(F32)).astype(BF16)
            high[span(i), span(j)] = top
            low[span(i), span(j)] = rest
            if d:
                high[span(j), span(i)] = top.T
                low[span(j), span(i)] = rest.T
    hard = 2.0 * jnp.sum(squares) > 256.0**2

    @pl.when(hard)
    def _():
        for i in range(BLOCKS):
            for d in range(kept(i)):
                j = (i + d) % BLOCKS
                values = scaled(i, d)
                rest = values - values.astype(BF16).astype(F32)
                last = (rest - rest.astype(BF16).astype(F32)).astype(BF16)
                least[span(i), span(j)] = last
                if d:
                    least[span(j), span(i)] = last.T

    def fold(total):
        return jnp.sum(total, axis=0, keepdims=True)

    def twice(values):
        return jnp.concatenate([values, values], axis=1)

    total = jnp.zeros((TILE, RIGHTS), F32)
    for i in range(BLOCKS):
        turned = jnp.concatenate([rights[span(h), span(i)].T for h in range(RIGHTS // TILE)], axis=1)
        b = turned.astype(F32) * twice(side[span(i), :])
        res[span(i), :] = b
        way[span(i), :] = b.astype(BF16)
        sol[span(i), :] = jnp.zeros((TILE, RIGHTS), F32)
        total = total + b * b
    norm = fold(total)
    norm_ref[...] = norm
    bound = norm * (TOL * TOL)
    rough = norm * (ROUGH * ROUGH)

    def apply(*terms):
        total = jnp.zeros((CHUNK, RIGHTS), F32)
        for at in range(0, WIDTH, DOT_ROWS):
            part = slice(at, at + DOT_ROWS)
            q = jnp.dot(terms[0][part, :], way[...], preferred_element_type=F32)
            for term in terms[1:]:
                q = q + jnp.dot(term[part, :], way[...], preferred_element_type=F32)
            image[part, :] = q
            for n in range(0, DOT_ROWS, CHUNK):
                total = total + way[at + n : at + n + CHUNK, :].astype(F32) * q[n : n + CHUNK, :]
        curve_ref[...] = fold(total)

    def unfinished(carry):
        step, left, more = carry
        return jnp.logical_and(step < MAX_STEPS, left > 0.0)

    def advance(carry):
        step, left, more = carry

        @pl.when(hard)
        def _():
            apply(high, low, least)

        @pl.when(jnp.logical_and(jnp.logical_not(hard), more > 0.0))
        def _():
            apply(high, low)

        @pl.when(jnp.logical_and(jnp.logical_not(hard), jnp.logical_not(more > 0.0)))
        def _():
            apply(high)

        norm = norm_ref[...]
        curve = curve_ref[...]
        alpha = jnp.where(curve > 0.0, norm / jnp.where(curve > 0.0, curve, 1.0), 0.0)
        total = jnp.zeros((CHUNK, RIGHTS), F32)
        for at in range(0, WIDTH, CHUNK):
            part = slice(at, at + CHUNK)
            r = res[part, :] - alpha * image[part, :]
            res[part, :] = r
            total = total + r * r
        fresh = fold(total)
        beta = jnp.where(norm > 0.0, fresh / jnp.where(norm > 0.0, norm, 1.0), 0.0)
        norm_ref[...] = fresh
        for at in range(0, WIDTH, CHUNK):
            part = slice(at, at + CHUNK)
            p = way[part, :].astype(F32)
            sol[part, :] += alpha * p
            way[part, :] = (res[part, :] + beta * p).astype(BF16)
        return step + 1, jnp.max(fresh - bound), jnp.max(fresh - rough)

    lax.while_loop(unfinished, advance, (jnp.int32(0), jnp.max(norm - bound), jnp.max(norm - rough)))


def swap_halves(scale, feat, sol, side, theirs, scores, mine, send, recv):
    x, y, z, core = position()
    sibling = device(x, y, z, 1 - core)
    barrier = pltpu.get_barrier_semaphore()
    signal(barrier, sibling)
    size = WIDTH // 4
    copies = []
    for n in range(4):
        part = slice(n * size, (n + 1) * size)
        factor = side[part, :] * scale
        mine[part, :] = (sol[part, :] * jnp.concatenate([factor, factor], axis=1)).astype(BF16)
        if n == 0:
            pl.semaphore_wait(barrier, 1)
        at = pl.ds(n * size, size)
        copies.append(remote(mine.at[at], theirs.at[at], send.at[n], recv.at[n], sibling))
        copies[n].start()
    scores[...] = jnp.dot(feat[...], mine[...], preferred_element_type=F32)
    for copy in copies:
        copy.wait()


def score(feat, theirs, scores, out, held, sems):
    core = position()[3]

    def columns(who):
        return out.at[:, pl.ds(pl.multiple_of(who * RIGHTS, RIGHTS), RIGHTS)]

    own = pltpu.make_async_copy(scores, columns(core), sems.at[0])
    own.start()
    held[...] = jnp.dot(feat[...], theirs[...], preferred_element_type=F32)
    other = pltpu.make_async_copy(held, columns(1 - core), sems.at[1])
    other.start()
    own.wait()
    other.wait()


def on_device(features, targets):
    dma = pltpu.SemaphoreType.DMA
    vmem = pl.BlockSpec(memory_space=pltpu.VMEM)
    anywhere = pl.BlockSpec(memory_space=pl.ANY)
    hbm = pl.BlockSpec(memory_space=pltpu.HBM)
    packed, rights = pl.pallas_call(
        gram_sum,
        name="gram_sum",
        out_shape=(
            jax.ShapeDtypeStruct((4 * UNIT, TILE), F32),
            jax.ShapeDtypeStruct((2, 4, 2, 16, WIDTH), BF16),
        ),
        in_specs=[hbm, hbm],
        out_specs=(vmem, vmem),
        scratch_shapes=[
            pltpu.VMEM((features.shape[0], WIDTH + WIDTH // 2), BF16),
            pltpu.VMEM((4 * UNIT, TILE), F32),
            pltpu.VMEM((2 * UNIT, TILE), F32),
            pltpu.VMEM((2, 3, QUARTERS, TILE), F32),
            pltpu.VMEM((2, 3, SIXTEENTHS, TILE), F32),
            pltpu.VMEM((8, 2, PIECE[0], TILE), F32),
            pltpu.VMEM((8, 2, PIECE[1], TILE), F32),
            pltpu.VMEM((8, 2, PIECE[0], TILE), F32),
            pltpu.VMEM((8, 2, PIECE[1], TILE), F32),
            pltpu.VMEM((NZ, 2, PIECE[0], TILE), F32),
            pltpu.VMEM((NZ, 2, PIECE[1], TILE), F32),
            pltpu.VMEM((1, WIDTH), BF16),
            pltpu.VMEM((8, TILE), F32),
            pltpu.VMEM((NZ * 8, TILE), F32),
            pltpu.VMEM((4, 16, WIDTH), BF16),
            pltpu.VMEM((64, WIDTH), F32),
            pltpu.VMEM((4, 16, WIDTH), BF16),
            dma((3,)), dma((16,)), dma((16,)),
            dma((16,)), dma((16,)), dma((16,)), dma((16,)),
            dma((2, 8)), dma((2, 8)), dma((2, NZ)), dma((2, NZ)),
            dma((16,)), dma((16,)), dma((16,)), dma((16,)), dma((16,)), dma((16,)),
            dma((NZ,)), dma((NZ,)), dma((4,)), dma((4,)), dma((4,)), dma((4,)),
            pltpu.SemaphoreType.REGULAR((3,)),
        ],
        compiler_params=pltpu.CompilerParams(
            collective_id=0, has_side_effects=True, vmem_limit_bytes=40 * 2**20
        ),
    )(
        pltpu.with_memory_space_constraint(features, pltpu.HBM),
        pltpu.with_memory_space_constraint(targets, pltpu.HBM),
    )

    total_rows = features.shape[0] * lax.axis_size("loop") * lax.axis_size("group")
    sol, side = pl.pallas_call(
        functools.partial(solve, 0.05),
        name="solve",
        out_shape=(jax.ShapeDtypeStruct((WIDTH, RIGHTS), F32), jax.ShapeDtypeStruct((WIDTH, TILE), F32)),
        in_specs=[vmem, vmem],
        out_specs=(vmem, vmem),
        scratch_shapes=[
            pltpu.VMEM((WIDTH, WIDTH), BF16),
            pltpu.VMEM((WIDTH, WIDTH), BF16),
            pltpu.VMEM((WIDTH, WIDTH), BF16),
            pltpu.VMEM((WIDTH, RIGHTS), F32),
            pltpu.VMEM((WIDTH, RIGHTS), BF16),
            pltpu.VMEM((WIDTH, RIGHTS), F32),
            pltpu.VMEM((1, WIDTH), F32),
            pltpu.VMEM((1, RIGHTS), F32),
            pltpu.VMEM((1, RIGHTS), F32),
        ],
        compiler_params=pltpu.CompilerParams(vmem_limit_bytes=40 * 2**20),
    )(packed, rights.reshape(RIGHTS, WIDTH))

    theirs, scores = pl.pallas_call(
        functools.partial(swap_halves, total_rows / WIDTH**0.5),
        name="swap_halves",
        out_shape=(
            jax.ShapeDtypeStruct((WIDTH, RIGHTS), BF16),
            jax.ShapeDtypeStruct((features.shape[0], RIGHTS), F32),
        ),
        in_specs=[vmem, vmem, vmem],
        out_specs=(vmem, vmem),
        scratch_shapes=[pltpu.VMEM((WIDTH, RIGHTS), BF16), dma((4,)), dma((4,))],
        compiler_params=pltpu.CompilerParams(
            collective_id=1, has_side_effects=True, vmem_limit_bytes=16 * 2**20
        ),
    )(features, sol, side)

    return pl.pallas_call(
        score,
        name="score",
        out_shape=jax.ShapeDtypeStruct((features.shape[0], 2 * RIGHTS), F32),
        in_specs=[vmem, vmem, vmem],
        out_specs=anywhere,
        scratch_shapes=[pltpu.VMEM((features.shape[0], RIGHTS), F32), dma((2,))],
        compiler_params=pltpu.CompilerParams(vmem_limit_bytes=16 * 2**20),
    )(features, theirs, scores)


def solution(mesh):
    return jax.shard_map(
        on_device,
        mesh=mesh,
        in_specs=(P(("loop", "group"), None), P(("loop", "group"), None)),
        out_specs=P(("loop", "group"), None),
        check_vma=False,
    )
```

```python
import functools

import jax
import jax.numpy as jnp
from jax import lax
from jax.experimental import pallas as pl
from jax.experimental.pallas import tpu as pltpu
from jax.sharding import PartitionSpec as P

WIDTH = 1024
TILE = 128
BLOCKS = WIDTH // TILE
UPPER, LOWER = 5, 4
UNIT = (UPPER + LOWER) * TILE
NZ = 16
AROUND = (-4, 3, -3, 2, -2, 1, -1)
START = (0, UPPER * TILE)
SIZE = (UPPER * TILE, LOWER * TILE)
QUARTER = tuple(size // 4 for size in SIZE)
SIXTEENTH = tuple(size // 16 for size in SIZE)
PIECE = tuple(size // 8 // NZ for size in SIZE)
QUARTERS, SIXTEENTHS = sum(QUARTER), sum(SIXTEENTH)
RIGHTS = 256
TOL = 1e-4
HARD_TOL = 1e-6
ROUGH = 1e-2
MAX_STEPS = 4096
CHUNK = 32
DOT_ROWS = 256
MESH = pl.DeviceIdType.MESH
F32 = jnp.float32
BF16 = jnp.bfloat16


def position():
    loop = lax.axis_index("loop")
    group = lax.axis_index("group")
    x = loop // 8
    y = group // 4
    z = (group % 4) * 4 + (loop // 2) % 4
    return x, y, z, loop % 2


def device(x, y, z, core):
    return (x * 8 + (z % 4) * 2 + core, y * 4 + z // 4)


def remote(src, dst, send, recv, to):
    return pltpu.make_async_remote_copy(
        src_ref=src, dst_ref=dst, send_sem=send, recv_sem=recv, device_id=to, device_id_type=MESH
    )


def signal(sem, to):
    pl.semaphore_signal(sem, inc=1, device_id=to, device_id_type=MESH)


def rows(start, size, unit=8):
    return pl.ds(pl.multiple_of(start, unit), size)


def far_first(k):
    return 8 + ((k + 1) // 2) * (1 - 2 * (k % 2))


def gram_sum(
    feat, tgt, out, rights, wide, packed, from_core, land1, land2, zsrc0, zsrc1, zland0, zland1, zout0, zout1,
    line, tsrc, tz, yblock, ywide, xblock,
    load_s, core_s, core_r, e1_s, e1_r, e2_s, e2_r, z_s, z_r, za_s, za_r,
    g2_s, g2_r, g1_s, g1_r, cag_s, cag_r, tz_s, tz_r, ty_s, ty_r, tx_s, tx_r, known,
):
    zsrc, zland, zout = (zsrc0, zsrc1), (zland0, zland1), (zout0, zout1)
    x, y, z, core = position()
    sibling = device(x, y, z, 1 - core)

    def on_x(t):
        return device((x + t) % 4, y, z, core)

    def on_y(t):
        return device(x, (y + t) % 4, z, core)

    def on_z(t):
        return device(x, y, (z + t) % NZ, core)

    def over(axis, t):
        return on_x(t) if axis == 0 else on_y(t)

    here = (x, y)
    ring = (1, 3, 2)
    parts = (0, 1)
    units = (0, 1)

    barrier = pltpu.get_barrier_semaphore()
    signal(barrier, sibling)
    for t in (1, 2, 3):
        signal(barrier, on_x(t))
        signal(barrier, on_y(t))
    signal(barrier, on_z(1))
    signal(barrier, on_z(NZ - 1))

    loads = [
        pltpu.make_async_copy(feat, wide.at[:, pl.ds(0, WIDTH)], load_s.at[0]),
        pltpu.make_async_copy(feat.at[:, pl.ds(0, WIDTH // 2)], wide.at[:, pl.ds(WIDTH, WIDTH // 2)], load_s.at[1]),
        pltpu.make_async_copy(tgt, line, load_s.at[2]),
    ]
    for load in loads:
        load.start()
    loads[0].wait()

    def begin(who, j, h):
        return (2 * who + j) * UNIT + START[h]

    def quarter(j, h, t):
        return begin(core, j, h) + ((here[j] + t) % 4) * QUARTER[h]

    def sixteenth(j, h, t):
        return quarter(j, h, 0) + ((here[1 - j] + t) % 4) * SIXTEENTH[h]

    def slot(j, h, t):
        return (h * 2 + j) * 4 + t

    def part_gram(who, j, h):
        i = 2 * who + j + 4 * h
        kept = (UPPER, LOWER)[h]
        left = wide[:, rows(i * TILE, TILE, TILE)]
        span = wide[:, rows(i * TILE, kept * TILE, TILE)]
        product = lax.dot_general(left, span, (((0,), (0,)), ((), ())), preferred_element_type=F32)
        for d in range(kept):
            packed[rows(begin(who, j, h) + d * TILE, TILE), :] = product[:, d * TILE : (d + 1) * TILE]

    def core_landing(j, h, t):
        return pl.ds((j * 4 + t) * QUARTERS + h * QUARTER[0], QUARTER[h])

    def core_copy(j, h, t):
        n = slot(j, h, t)
        at = begin(1 - core, j, h) + ((here[j] + t) % 4) * QUARTER[h]
        return remote(
            packed.at[rows(at, QUARTER[h])], from_core.at[core_landing(j, h, t)], core_s.at[n], core_r.at[n], sibling
        )

    part_gram(1 - core, 0, 0)
    pl.semaphore_wait(barrier, 9)
    core_copy(0, 0, 2).start()
    signal(known.at[0], on_z(1))
    signal(known.at[0], on_z(NZ - 1))
    part_gram(1 - core, 1, 0)
    core_copy(1, 0, 2).start()
    for t in (1, 3, 0):
        for j in units:
            core_copy(j, 0, t).start()
    loads[1].wait()
    for j in units:
        part_gram(1 - core, j, 1)
    for t in (2, 1, 3, 0):
        for j in units:
            core_copy(j, 1, t).start()
    for h in parts:
        for j in units:
            part_gram(core, j, h)
    loads[2].wait()

    def first_landing(h):
        return pl.ds(h * QUARTER[0], QUARTER[h])

    def second_landing(h):
        return pl.ds(h * SIXTEENTH[0], SIXTEENTH[h])

    def first(j, h, t):
        n = slot(j, h, t)
        return remote(
            packed.at[rows(quarter(j, h, t), QUARTER[h])], land1.at[j, t - 1, first_landing(h)],
            e1_s.at[n], e1_r.at[n], over(j, t),
        )

    def second(j, h, t):
        n = slot(j, h, t)
        return remote(
            packed.at[rows(sixteenth(j, h, t), SIXTEENTH[h])], land2.at[j, t - 1, second_landing(h)],
            e2_s.at[n], e2_r.at[n], over(1 - j, t),
        )

    for h in parts:
        for t in (2, 1, 3, 0):
            for j in units:
                core_copy(j, h, t).wait_recv()
                packed[rows(quarter(j, h, t), QUARTER[h]), :] += from_core[core_landing(j, h, t), :]
                if t:
                    first(j, h, t).start()

    for k in range(8):
        tsrc[k : k + 1, :] = line[:, k * TILE : (k + 1) * TILE].astype(F32)
    tz[rows(z * 8, 8), :] = tsrc[...]
    for h in parts:
        for t in range(4):
            for j in units:
                core_copy(j, h, t).wait_send()
    pl.semaphore_wait(known.at[0], 2)
    signal(known.at[1], on_z(2))
    signal(known.at[1], on_z(NZ - 2))

    def add_first(h):
        for j in units:
            for t in ring:
                first(j, h, t).wait()
            at = rows(quarter(j, h, 0), QUARTER[h])
            landed = first_landing(h)
            packed[at, :] += land1[j, 0, landed, :] + land1[j, 1, landed, :] + land1[j, 2, landed, :]
            for t in ring:
                second(j, h, t).start()

    add_first(0)
    pl.semaphore_wait(known.at[1], 2)
    signal(known.at[2], on_z(4))
    signal(known.at[2], on_z(NZ - 4))
    add_first(1)
    pl.semaphore_wait(known.at[2], 2)

    def all_z(copy):
        def body(k, carry):
            copy(far_first(k)).start()
            return carry

        lax.fori_loop(0, NZ - 1, body, 0)

    def end_z(copy, landing, recv):
        def body(k, carry):
            t = far_first(k)
            copy(t).wait_send()
            other = (z + t) % NZ
            ref = landing(other)
            remote(ref, ref, recv.at[other], recv.at[other], sibling).wait_recv()
            return carry

        lax.fori_loop(0, NZ - 1, body, 0)

    def target_row(k):
        return tz.at[rows(k * 8, 8)]

    def t_copy(t):
        return remote(target_row(z), target_row(z), tz_s.at[t], tz_r.at[z], on_z(t))

    all_z(t_copy)

    def z_copy(h, t):
        n = t + 4
        return remote(zsrc[h].at[(z + t + NZ) % 8], zland[h].at[n], z_s.at[h, n], z_r.at[h, n], on_z(t + NZ))

    def za_copy(h):
        def copy(t):
            return remote(zout[h].at[z], zout[h].at[z], za_s.at[h, t], za_r.at[h, z], on_z(t))

        return copy

    for h in parts:
        for j in units:
            for t in ring:
                second(j, h, t).wait()
            at = rows(sixteenth(j, h, 0), SIXTEENTH[h])
            landed = second_landing(h)
            block = packed[at, :] + land2[j, 0, landed, :] + land2[j, 1, landed, :] + land2[j, 2, landed, :]
            for m in range(8):
                zsrc[h][m, j] = block[m * PIECE[h] : (m + 1) * PIECE[h], :]
        for t in AROUND:
            z_copy(h, t).start()
        zland[h][4] = zsrc[h][z % 8]

    end_z(t_copy, target_row, tz_r)
    for k in range(8):
        for low in range(4):
            ywide[low * 4 : low * 4 + 4, k * TILE : (k + 1) * TILE] = tz[pl.ds(low * 8 + k, 4, stride=32), :]
    yblock[y] = ywide[0:16, :].astype(BF16)

    def y_copy(t):
        return remote(yblock.at[y], yblock.at[y], ty_s.at[t], ty_r.at[t], on_y(t))

    for t in ring:
        y_copy(t).start()

    for h in parts:
        for t in AROUND:
            z_copy(h, t).wait()
        total = zland[h][0]
        for k in range(1, 8):
            total = total + zland[h][k]
        zout[h][z] = total
        all_z(za_copy(h))

    for t in ring:
        y_copy(t).wait_send()
        ref = yblock.at[(y + 4 - t) % 4]
        remote(ref, ref, ty_s.at[t], ty_r.at[t], sibling).wait_recv()
    for yy in range(4):
        block = yblock[yy].astype(F32)
        for low in range(4):
            ywide[low * 16 + yy * 4 : low * 16 + yy * 4 + 4, :] = block[low * 4 : low * 4 + 4, :]
    for low in range(4):
        xblock[low] = ywide[low * 16 : low * 16 + 16, :].astype(BF16)

    solver = x // 2
    stays = solver == core

    def x_copy(t):
        to = device((x + t) % 4, y, z, solver)
        return remote(xblock, rights.at[x % 2, :, core], tx_s.at[t], tx_r.at[(x % 2) * 2 + core], to)

    for t in ring:
        x_copy(t).start()
    stay = pltpu.make_async_copy(xblock, rights.at[x % 2, :, core], tx_s.at[0])

    @pl.when(stays)
    def _():
        stay.start()

    @pl.when(jnp.logical_not(stays))
    def _():
        x_copy(0).start()

    def gather(j, h, t, stage):
        if stage == 2:
            mine, theirs, size, axis = sixteenth(j, h, 0), sixteenth(j, h, 4 - t), SIXTEENTH[h], 1 - j
            send, recv = g2_s, g2_r
        else:
            mine, theirs, size, axis = quarter(j, h, 0), quarter(j, h, 4 - t), QUARTER[h], j
            send, recv = g1_s, g1_r
        a, b = out.at[rows(mine, size)], out.at[rows(theirs, size)]
        n = slot(j, h, t)
        return (
            remote(a, a, send.at[n], recv.at[n], over(axis, t)),
            remote(b, b, send.at[n], recv.at[n], over(axis, t)),
        )

    def core_gather(j, h, t, who):
        at = begin(who, j, h) + ((here[j] + 4 - t) % 4) * QUARTER[h]
        ref = out.at[rows(at, QUARTER[h])]
        n = slot(j, h, t)
        return remote(ref, ref, cag_s.at[n], cag_r.at[n], sibling)

    for h in parts:
        end_z(za_copy(h), lambda k: zout[h].at[k], za_r.at[h])
        for j in units:
            out[rows(sixteenth(j, h, 0), SIXTEENTH[h]), :] = jnp.concatenate(
                [zout[h][m, j] + zout[h][m + 8, j] for m in range(8)], axis=0
            )
            for t in ring:
                gather(j, h, t, 2)[0].start()
    for h in parts:
        for j in units:
            for t in ring:
                send, recv = gather(j, h, t, 2)
                send.wait_send()
                recv.wait_recv()
            for t in ring:
                gather(j, h, t, 1)[0].start()
            core_gather(j, h, 0, core).start()
    for h in parts:
        for t in (1, 3, 2):
            for j in units:
                gather(j, h, t, 1)[1].wait_recv()
                core_gather(j, h, t, core).start()
    for t in ring:
        x_copy(t).wait_send()
        for h in parts:
            for j in units:
                gather(j, h, t, 1)[0].wait_send()

    @pl.when(stays)
    def _():
        stay.wait()

    @pl.when(jnp.logical_not(stays))
    def _():
        x_copy(0).wait_send()

    for near in range(2):
        for who in range(2):

            @pl.when(jnp.logical_or(2 * core + near != x, who != core))
            def _():
                ref = rights.at[near, :, who]
                remote(ref, ref, tx_s.at[0], tx_r.at[near * 2 + who], sibling).wait_recv()

    for h in parts:
        for t in (0, 1, 3, 2):
            for j in units:
                core_gather(j, h, t, core).wait_send()
                core_gather(j, h, t, 1 - core).wait_recv()


def solve(damping, packed, rights, sol, side, high, low, least, res, way, image, diag, norm_ref, curve_ref):
    eye = lax.broadcasted_iota(jnp.int32, (TILE, TILE), 0) == lax.broadcasted_iota(jnp.int32, (TILE, TILE), 1)

    def tile(i, d):
        start = (i % 4) * UNIT + (i // 4) * UPPER * TILE + d * TILE
        return packed[start : start + TILE, :]

    def kept(i):
        return UPPER if i < 4 else LOWER

    def span(i):
        return slice(i * TILE, (i + 1) * TILE)

    for i in range(BLOCKS):
        diag[:, span(i)] = jnp.sum(jnp.where(eye, tile(i, 0), 0.0), axis=0, keepdims=True)
    shift = jnp.sum(diag[...], axis=1, keepdims=True) * (damping / WIDTH)
    per_shift = 1.0 / shift
    diag[...] = lax.rsqrt(diag[...] + shift)
    for i in range(BLOCKS):
        side[span(i), :] = jnp.broadcast_to(diag[:, span(i)], (TILE, TILE)).T

    def scaled(i, d):
        values = tile(i, d)
        if d == 0:
            values = values + jnp.where(eye, shift, 0.0)
        return values * side[span(i), :] * diag[:, span((i + d) % BLOCKS)]

    squares = jnp.zeros((TILE, TILE), F32)
    for i in range(BLOCKS):
        for d in range(kept(i)):
            j = (i + d) % BLOCKS
            off = tile(i, d) * per_shift
            if d == 0:
                off = jnp.where(eye, 0.0, off)
                squares = squares + 0.5 * off * off
            else:
                squares = squares + off * off
            values = scaled(i, d)
            top = values.astype(BF16)
            rest = (values - top.astype(F32)).astype(BF16)
            high[span(i), span(j)] = top
            low[span(i), span(j)] = rest
            if d:
                high[span(j), span(i)] = top.T
                low[span(j), span(i)] = rest.T
    hard = 2.0 * jnp.sum(squares) > 256.0**2

    @pl.when(hard)
    def _():
        for i in range(BLOCKS):
            for d in range(kept(i)):
                j = (i + d) % BLOCKS
                values = scaled(i, d)
                rest = values - values.astype(BF16).astype(F32)
                last = (rest - rest.astype(BF16).astype(F32)).astype(BF16)
                least[span(i), span(j)] = last
                if d:
                    least[span(j), span(i)] = last.T

    def fold(total):
        return jnp.sum(total, axis=0, keepdims=True)

    def twice(values):
        return jnp.concatenate([values, values], axis=1)

    total = jnp.zeros((TILE, RIGHTS), F32)
    for i in range(BLOCKS):
        turned = jnp.concatenate([rights[span(h), span(i)].T for h in range(RIGHTS // TILE)], axis=1)
        b = turned.astype(F32) * twice(side[span(i), :])
        res[span(i), :] = b
        way[span(i), :] = b.astype(BF16)
        sol[span(i), :] = jnp.zeros((TILE, RIGHTS), F32)
        total = total + b * b
    norm = fold(total)
    norm_ref[...] = norm
    bound = norm * jnp.where(hard, HARD_TOL * HARD_TOL, TOL * TOL)
    rough = norm * (ROUGH * ROUGH)

    def apply(*terms):
        total = jnp.zeros((CHUNK, RIGHTS), F32)
        for at in range(0, WIDTH, DOT_ROWS):
            part = slice(at, at + DOT_ROWS)
            q = jnp.dot(terms[0][part, :], way[...], preferred_element_type=F32)
            for term in terms[1:]:
                q = q + jnp.dot(term[part, :], way[...], preferred_element_type=F32)
            image[part, :] = q
            for n in range(0, DOT_ROWS, CHUNK):
                total = total + way[at + n : at + n + CHUNK, :].astype(F32) * q[n : n + CHUNK, :]
        curve_ref[...] = fold(total)

    def unfinished(carry):
        step, left, more = carry
        return jnp.logical_and(step < MAX_STEPS, left > 0.0)

    def advance(carry):
        step, left, more = carry

        @pl.when(hard)
        def _():
            apply(high, low, least)

        @pl.when(jnp.logical_and(jnp.logical_not(hard), more > 0.0))
        def _():
            apply(high, low)

        @pl.when(jnp.logical_and(jnp.logical_not(hard), jnp.logical_not(more > 0.0)))
        def _():
            apply(high)

        norm = norm_ref[...]
        curve = curve_ref[...]
        alpha = jnp.where(curve > 0.0, norm / jnp.where(curve > 0.0, curve, 1.0), 0.0)
        total = jnp.zeros((CHUNK, RIGHTS), F32)
        for at in range(0, WIDTH, CHUNK):
            part = slice(at, at + CHUNK)
            r = res[part, :] - alpha * image[part, :]
            res[part, :] = r
            total = total + r * r
        fresh = fold(total)
        beta = jnp.where(norm > 0.0, fresh / jnp.where(norm > 0.0, norm, 1.0), 0.0)
        norm_ref[...] = fresh
        for at in range(0, WIDTH, CHUNK):
            part = slice(at, at + CHUNK)
            p = way[part, :].astype(F32)
            sol[part, :] += alpha * p
            way[part, :] = (res[part, :] + beta * p).astype(BF16)
        return step + 1, jnp.max(fresh - bound), jnp.max(fresh - rough)

    lax.while_loop(unfinished, advance, (jnp.int32(0), jnp.max(norm - bound), jnp.max(norm - rough)))


def swap_halves(scale, feat, sol, side, theirs, scores, mine, send, recv):
    x, y, z, core = position()
    sibling = device(x, y, z, 1 - core)
    barrier = pltpu.get_barrier_semaphore()
    signal(barrier, sibling)
    size = WIDTH // 4
    copies = []
    for n in range(4):
        part = slice(n * size, (n + 1) * size)
        factor = side[part, :] * scale
        mine[part, :] = (sol[part, :] * jnp.concatenate([factor, factor], axis=1)).astype(BF16)
        if n == 0:
            pl.semaphore_wait(barrier, 1)
        at = pl.ds(n * size, size)
        copies.append(remote(mine.at[at], theirs.at[at], send.at[n], recv.at[n], sibling))
        copies[n].start()
    scores[...] = jnp.dot(feat[...], mine[...], preferred_element_type=F32)
    for copy in copies:
        copy.wait()


def score(feat, theirs, scores, out, held, sems):
    core = position()[3]

    def columns(who):
        return out.at[:, pl.ds(pl.multiple_of(who * RIGHTS, RIGHTS), RIGHTS)]

    own = pltpu.make_async_copy(scores, columns(core), sems.at[0])
    own.start()
    held[...] = jnp.dot(feat[...], theirs[...], preferred_element_type=F32)
    other = pltpu.make_async_copy(held, columns(1 - core), sems.at[1])
    other.start()
    own.wait()
    other.wait()


def on_device(features, targets):
    dma = pltpu.SemaphoreType.DMA
    vmem = pl.BlockSpec(memory_space=pltpu.VMEM)
    anywhere = pl.BlockSpec(memory_space=pl.ANY)
    hbm = pl.BlockSpec(memory_space=pltpu.HBM)
    packed, rights = pl.pallas_call(
        gram_sum,
        name="gram_sum",
        out_shape=(
            jax.ShapeDtypeStruct((4 * UNIT, TILE), F32),
            jax.ShapeDtypeStruct((2, 4, 2, 16, WIDTH), BF16),
        ),
        in_specs=[hbm, hbm],
        out_specs=(vmem, vmem),
        scratch_shapes=[
            pltpu.VMEM((features.shape[0], WIDTH + WIDTH // 2), BF16),
            pltpu.VMEM((4 * UNIT, TILE), F32),
            pltpu.VMEM((2 * UNIT, TILE), F32),
            pltpu.VMEM((2, 3, QUARTERS, TILE), F32),
            pltpu.VMEM((2, 3, SIXTEENTHS, TILE), F32),
            pltpu.VMEM((8, 2, PIECE[0], TILE), F32),
            pltpu.VMEM((8, 2, PIECE[1], TILE), F32),
            pltpu.VMEM((8, 2, PIECE[0], TILE), F32),
            pltpu.VMEM((8, 2, PIECE[1], TILE), F32),
            pltpu.VMEM((NZ, 2, PIECE[0], TILE), F32),
            pltpu.VMEM((NZ, 2, PIECE[1], TILE), F32),
            pltpu.VMEM((1, WIDTH), BF16),
            pltpu.VMEM((8, TILE), F32),
            pltpu.VMEM((NZ * 8, TILE), F32),
            pltpu.VMEM((4, 16, WIDTH), BF16),
            pltpu.VMEM((64, WIDTH), F32),
            pltpu.VMEM((4, 16, WIDTH), BF16),
            dma((3,)), dma((16,)), dma((16,)),
            dma((16,)), dma((16,)), dma((16,)), dma((16,)),
            dma((2, 8)), dma((2, 8)), dma((2, NZ)), dma((2, NZ)),
            dma((16,)), dma((16,)), dma((16,)), dma((16,)), dma((16,)), dma((16,)),
            dma((NZ,)), dma((NZ,)), dma((4,)), dma((4,)), dma((4,)), dma((4,)),
            pltpu.SemaphoreType.REGULAR((3,)),
        ],
        compiler_params=pltpu.CompilerParams(
            collective_id=0, has_side_effects=True, vmem_limit_bytes=40 * 2**20
        ),
    )(
        pltpu.with_memory_space_constraint(features, pltpu.HBM),
        pltpu.with_memory_space_constraint(targets, pltpu.HBM),
    )

    total_rows = features.shape[0] * lax.axis_size("loop") * lax.axis_size("group")
    sol, side = pl.pallas_call(
        functools.partial(solve, 0.05),
        name="solve",
        out_shape=(jax.ShapeDtypeStruct((WIDTH, RIGHTS), F32), jax.ShapeDtypeStruct((WIDTH, TILE), F32)),
        in_specs=[vmem, vmem],
        out_specs=(vmem, vmem),
        scratch_shapes=[
            pltpu.VMEM((WIDTH, WIDTH), BF16),
            pltpu.VMEM((WIDTH, WIDTH), BF16),
            pltpu.VMEM((WIDTH, WIDTH), BF16),
            pltpu.VMEM((WIDTH, RIGHTS), F32),
            pltpu.VMEM((WIDTH, RIGHTS), BF16),
            pltpu.VMEM((WIDTH, RIGHTS), F32),
            pltpu.VMEM((1, WIDTH), F32),
            pltpu.VMEM((1, RIGHTS), F32),
            pltpu.VMEM((1, RIGHTS), F32),
        ],
        compiler_params=pltpu.CompilerParams(vmem_limit_bytes=40 * 2**20),
    )(packed, rights.reshape(RIGHTS, WIDTH))

    theirs, scores = pl.pallas_call(
        functools.partial(swap_halves, total_rows / WIDTH**0.5),
        name="swap_halves",
        out_shape=(
            jax.ShapeDtypeStruct((WIDTH, RIGHTS), BF16),
            jax.ShapeDtypeStruct((features.shape[0], RIGHTS), F32),
        ),
        in_specs=[vmem, vmem, vmem],
        out_specs=(vmem, vmem),
        scratch_shapes=[pltpu.VMEM((WIDTH, RIGHTS), BF16), dma((4,)), dma((4,))],
        compiler_params=pltpu.CompilerParams(
            collective_id=1, has_side_effects=True, vmem_limit_bytes=16 * 2**20
        ),
    )(features, sol, side)

    return pl.pallas_call(
        score,
        name="score",
        out_shape=jax.ShapeDtypeStruct((features.shape[0], 2 * RIGHTS), F32),
        in_specs=[vmem, vmem, vmem],
        out_specs=anywhere,
        scratch_shapes=[pltpu.VMEM((features.shape[0], RIGHTS), F32), dma((2,))],
        compiler_params=pltpu.CompilerParams(vmem_limit_bytes=16 * 2**20),
    )(features, theirs, scores)


def solution(mesh):
    return jax.shard_map(
        on_device,
        mesh=mesh,
        in_specs=(P(("loop", "group"), None), P(("loop", "group"), None)),
        out_specs=P(("loop", "group"), None),
        check_vma=False,
    )
```

```python
import functools

import jax
import jax.numpy as jnp
from jax import lax
from jax.experimental import pallas as pl
from jax.experimental.pallas import tpu as pltpu
from jax.sharding import PartitionSpec as P

WIDTH = 1024
TILE = 128
BLOCKS = WIDTH // TILE
UPPER, LOWER = 5, 4
UNIT = (UPPER + LOWER) * TILE
NZ = 16
AROUND = (-4, 3, -3, 2, -2, 1, -1)
START = (0, UPPER * TILE)
SIZE = (UPPER * TILE, LOWER * TILE)
QUARTER = tuple(size // 4 for size in SIZE)
SIXTEENTH = tuple(size // 16 for size in SIZE)
PIECE = tuple(size // 8 // NZ for size in SIZE)
QUARTERS, SIXTEENTHS = sum(QUARTER), sum(SIXTEENTH)
RIGHTS = 256
TOL = 1e-4
HARD_TOL = 1e-6
ROUGH = 1e-2
MAX_STEPS = 4096
CHUNK = 32
DOT_ROWS = 1024
MESH = pl.DeviceIdType.MESH
F32 = jnp.float32
BF16 = jnp.bfloat16


def position():
    loop = lax.axis_index("loop")
    group = lax.axis_index("group")
    x = loop // 8
    y = group // 4
    z = (group % 4) * 4 + (loop // 2) % 4
    return x, y, z, loop % 2


def device(x, y, z, core):
    return (x * 8 + (z % 4) * 2 + core, y * 4 + z // 4)


def remote(src, dst, send, recv, to):
    return pltpu.make_async_remote_copy(
        src_ref=src, dst_ref=dst, send_sem=send, recv_sem=recv, device_id=to, device_id_type=MESH
    )


def signal(sem, to):
    pl.semaphore_signal(sem, inc=1, device_id=to, device_id_type=MESH)


def rows(start, size, unit=8):
    return pl.ds(pl.multiple_of(start, unit), size)


def far_first(k):
    return 8 + ((k + 1) // 2) * (1 - 2 * (k % 2))


def gram_sum(
    feat, tgt, out, rights, wide, packed, from_core, land1, land2, zsrc0, zsrc1, zland0, zland1, zout0, zout1,
    line, tsrc, tz, yblock, ywide, xblock,
    load_s, core_s, core_r, e1_s, e1_r, e2_s, e2_r, z_s, z_r, za_s, za_r,
    g2_s, g2_r, g1_s, g1_r, cag_s, cag_r, tz_s, tz_r, ty_s, ty_r, tx_s, tx_r, known,
):
    zsrc, zland, zout = (zsrc0, zsrc1), (zland0, zland1), (zout0, zout1)
    x, y, z, core = position()
    sibling = device(x, y, z, 1 - core)

    def on_x(t):
        return device((x + t) % 4, y, z, core)

    def on_y(t):
        return device(x, (y + t) % 4, z, core)

    def on_z(t):
        return device(x, y, (z + t) % NZ, core)

    def over(axis, t):
        return on_x(t) if axis == 0 else on_y(t)

    here = (x, y)
    ring = (1, 3, 2)
    parts = (0, 1)
    units = (0, 1)

    barrier = pltpu.get_barrier_semaphore()
    signal(barrier, sibling)
    for t in (1, 2, 3):
        signal(barrier, on_x(t))
        signal(barrier, on_y(t))
    signal(barrier, on_z(1))
    signal(barrier, on_z(NZ - 1))

    loads = [
        pltpu.make_async_copy(feat, wide.at[:, pl.ds(0, WIDTH)], load_s.at[0]),
        pltpu.make_async_copy(feat.at[:, pl.ds(0, WIDTH // 2)], wide.at[:, pl.ds(WIDTH, WIDTH // 2)], load_s.at[1]),
        pltpu.make_async_copy(tgt, line, load_s.at[2]),
    ]
    for load in loads:
        load.start()
    loads[0].wait()

    def begin(who, j, h):
        return (2 * who + j) * UNIT + START[h]

    def quarter(j, h, t):
        return begin(core, j, h) + ((here[j] + t) % 4) * QUARTER[h]

    def sixteenth(j, h, t):
        return quarter(j, h, 0) + ((here[1 - j] + t) % 4) * SIXTEENTH[h]

    def slot(j, h, t):
        return (h * 2 + j) * 4 + t

    def part_gram(who, j, h):
        i = 2 * who + j + 4 * h
        kept = (UPPER, LOWER)[h]
        left = wide[:, rows(i * TILE, TILE, TILE)]
        span = wide[:, rows(i * TILE, kept * TILE, TILE)]
        product = lax.dot_general(left, span, (((0,), (0,)), ((), ())), preferred_element_type=F32)
        for d in range(kept):
            packed[rows(begin(who, j, h) + d * TILE, TILE), :] = product[:, d * TILE : (d + 1) * TILE]

    def core_landing(j, h, t):
        return pl.ds((j * 4 + t) * QUARTERS + h * QUARTER[0], QUARTER[h])

    def core_copy(j, h, t):
        n = slot(j, h, t)
        at = begin(1 - core, j, h) + ((here[j] + t) % 4) * QUARTER[h]
        return remote(
            packed.at[rows(at, QUARTER[h])], from_core.at[core_landing(j, h, t)], core_s.at[n], core_r.at[n], sibling
        )

    part_gram(1 - core, 0, 0)
    pl.semaphore_wait(barrier, 9)
    core_copy(0, 0, 2).start()
    signal(known.at[0], on_z(1))
    signal(known.at[0], on_z(NZ - 1))
    part_gram(1 - core, 1, 0)
    core_copy(1, 0, 2).start()
    for t in (1, 3, 0):
        for j in units:
            core_copy(j, 0, t).start()
    loads[1].wait()
    for j in units:
        part_gram(1 - core, j, 1)
    for t in (2, 1, 3, 0):
        for j in units:
            core_copy(j, 1, t).start()
    for h in parts:
        for j in units:
            part_gram(core, j, h)
    loads[2].wait()

    def first_landing(h):
        return pl.ds(h * QUARTER[0], QUARTER[h])

    def second_landing(h):
        return pl.ds(h * SIXTEENTH[0], SIXTEENTH[h])

    def first(j, h, t):
        n = slot(j, h, t)
        return remote(
            packed.at[rows(quarter(j, h, t), QUARTER[h])], land1.at[j, t - 1, first_landing(h)],
            e1_s.at[n], e1_r.at[n], over(j, t),
        )

    def second(j, h, t):
        n = slot(j, h, t)
        return remote(
            packed.at[rows(sixteenth(j, h, t), SIXTEENTH[h])], land2.at[j, t - 1, second_landing(h)],
            e2_s.at[n], e2_r.at[n], over(1 - j, t),
        )

    for h in parts:
        for t in (2, 1, 3, 0):
            for j in units:
                core_copy(j, h, t).wait_recv()
                packed[rows(quarter(j, h, t), QUARTER[h]), :] += from_core[core_landing(j, h, t), :]
                if t:
                    first(j, h, t).start()

    for k in range(8):
        tsrc[k : k + 1, :] = line[:, k * TILE : (k + 1) * TILE].astype(F32)
    tz[rows(z * 8, 8), :] = tsrc[...]
    for h in parts:
        for t in range(4):
            for j in units:
                core_copy(j, h, t).wait_send()
    pl.semaphore_wait(known.at[0], 2)
    signal(known.at[1], on_z(2))
    signal(known.at[1], on_z(NZ - 2))

    def add_first(h):
        for j in units:
            for t in ring:
                first(j, h, t).wait()
            at = rows(quarter(j, h, 0), QUARTER[h])
            landed = first_landing(h)
            packed[at, :] += land1[j, 0, landed, :] + land1[j, 1, landed, :] + land1[j, 2, landed, :]
            for t in ring:
                second(j, h, t).start()

    add_first(0)
    pl.semaphore_wait(known.at[1], 2)
    signal(known.at[2], on_z(4))
    signal(known.at[2], on_z(NZ - 4))
    add_first(1)
    pl.semaphore_wait(known.at[2], 2)

    def all_z(copy):
        def body(k, carry):
            copy(far_first(k)).start()
            return carry

        lax.fori_loop(0, NZ - 1, body, 0)

    def end_z(copy, landing, recv):
        def body(k, carry):
            t = far_first(k)
            copy(t).wait_send()
            other = (z + t) % NZ
            ref = landing(other)
            remote(ref, ref, recv.at[other], recv.at[other], sibling).wait_recv()
            return carry

        lax.fori_loop(0, NZ - 1, body, 0)

    def target_row(k):
        return tz.at[rows(k * 8, 8)]

    def t_copy(t):
        return remote(target_row(z), target_row(z), tz_s.at[t], tz_r.at[z], on_z(t))

    all_z(t_copy)

    def z_copy(h, t):
        n = t + 4
        return remote(zsrc[h].at[(z + t + NZ) % 8], zland[h].at[n], z_s.at[h, n], z_r.at[h, n], on_z(t + NZ))

    def za_copy(h):
        def copy(t):
            return remote(zout[h].at[z], zout[h].at[z], za_s.at[h, t], za_r.at[h, z], on_z(t))

        return copy

    for h in parts:
        for j in units:
            for t in ring:
                second(j, h, t).wait()
            at = rows(sixteenth(j, h, 0), SIXTEENTH[h])
            landed = second_landing(h)
            block = packed[at, :] + land2[j, 0, landed, :] + land2[j, 1, landed, :] + land2[j, 2, landed, :]
            for m in range(8):
                zsrc[h][m, j] = block[m * PIECE[h] : (m + 1) * PIECE[h], :]
        for t in AROUND:
            z_copy(h, t).start()
        zland[h][4] = zsrc[h][z % 8]

    end_z(t_copy, target_row, tz_r)
    for k in range(8):
        for low in range(4):
            ywide[low * 4 : low * 4 + 4, k * TILE : (k + 1) * TILE] = tz[pl.ds(low * 8 + k, 4, stride=32), :]
    yblock[y] = ywide[0:16, :].astype(BF16)

    def y_copy(t):
        return remote(yblock.at[y], yblock.at[y], ty_s.at[t], ty_r.at[t], on_y(t))

    for t in ring:
        y_copy(t).start()

    for h in parts:
        for t in AROUND:
            z_copy(h, t).wait()
        total = zland[h][0]
        for k in range(1, 8):
            total = total + zland[h][k]
        zout[h][z] = total
        all_z(za_copy(h))

    for t in ring:
        y_copy(t).wait_send()
        ref = yblock.at[(y + 4 - t) % 4]
        remote(ref, ref, ty_s.at[t], ty_r.at[t], sibling).wait_recv()
    for yy in range(4):
        block = yblock[yy].astype(F32)
        for low in range(4):
            ywide[low * 16 + yy * 4 : low * 16 + yy * 4 + 4, :] = block[low * 4 : low * 4 + 4, :]
    for low in range(4):
        xblock[low] = ywide[low * 16 : low * 16 + 16, :].astype(BF16)

    solver = x // 2
    stays = solver == core

    def x_copy(t):
        to = device((x + t) % 4, y, z, solver)
        return remote(xblock, rights.at[x % 2, :, core], tx_s.at[t], tx_r.at[(x % 2) * 2 + core], to)

    for t in ring:
        x_copy(t).start()
    stay = pltpu.make_async_copy(xblock, rights.at[x % 2, :, core], tx_s.at[0])

    @pl.when(stays)
    def _():
        stay.start()

    @pl.when(jnp.logical_not(stays))
    def _():
        x_copy(0).start()

    def gather(j, h, t, stage):
        if stage == 2:
            mine, theirs, size, axis = sixteenth(j, h, 0), sixteenth(j, h, 4 - t), SIXTEENTH[h], 1 - j
            send, recv = g2_s, g2_r
        else:
            mine, theirs, size, axis = quarter(j, h, 0), quarter(j, h, 4 - t), QUARTER[h], j
            send, recv = g1_s, g1_r
        a, b = out.at[rows(mine, size)], out.at[rows(theirs, size)]
        n = slot(j, h, t)
        return (
            remote(a, a, send.at[n], recv.at[n], over(axis, t)),
            remote(b, b, send.at[n], recv.at[n], over(axis, t)),
        )

    def core_gather(j, h, t, who):
        at = begin(who, j, h) + ((here[j] + 4 - t) % 4) * QUARTER[h]
        ref = out.at[rows(at, QUARTER[h])]
        n = slot(j, h, t)
        return remote(ref, ref, cag_s.at[n], cag_r.at[n], sibling)

    for h in parts:
        end_z(za_copy(h), lambda k: zout[h].at[k], za_r.at[h])
        for j in units:
            out[rows(sixteenth(j, h, 0), SIXTEENTH[h]), :] = jnp.concatenate(
                [zout[h][m, j] + zout[h][m + 8, j] for m in range(8)], axis=0
            )
            for t in ring:
                gather(j, h, t, 2)[0].start()
    for h in parts:
        for j in units:
            for t in ring:
                send, recv = gather(j, h, t, 2)
                send.wait_send()
                recv.wait_recv()
            for t in ring:
                gather(j, h, t, 1)[0].start()
            core_gather(j, h, 0, core).start()
    for h in parts:
        for t in (1, 3, 2):
            for j in units:
                gather(j, h, t, 1)[1].wait_recv()
                core_gather(j, h, t, core).start()
    for t in ring:
        x_copy(t).wait_send()
        for h in parts:
            for j in units:
                gather(j, h, t, 1)[0].wait_send()

    @pl.when(stays)
    def _():
        stay.wait()

    @pl.when(jnp.logical_not(stays))
    def _():
        x_copy(0).wait_send()

    for near in range(2):
        for who in range(2):

            @pl.when(jnp.logical_or(2 * core + near != x, who != core))
            def _():
                ref = rights.at[near, :, who]
                remote(ref, ref, tx_s.at[0], tx_r.at[near * 2 + who], sibling).wait_recv()

    for h in parts:
        for t in (0, 1, 3, 2):
            for j in units:
                core_gather(j, h, t, core).wait_send()
                core_gather(j, h, t, 1 - core).wait_recv()


def solve(damping, packed, rights, sol, side, high, low, least, res, way, image, diag, norm_ref, curve_ref):
    eye = lax.broadcasted_iota(jnp.int32, (TILE, TILE), 0) == lax.broadcasted_iota(jnp.int32, (TILE, TILE), 1)

    def tile(i, d):
        start = (i % 4) * UNIT + (i // 4) * UPPER * TILE + d * TILE
        return packed[start : start + TILE, :]

    def kept(i):
        return UPPER if i < 4 else LOWER

    def span(i):
        return slice(i * TILE, (i + 1) * TILE)

    for i in range(BLOCKS):
        diag[:, span(i)] = jnp.sum(jnp.where(eye, tile(i, 0), 0.0), axis=0, keepdims=True)
    shift = jnp.sum(diag[...], axis=1, keepdims=True) * (damping / WIDTH)
    per_shift = 1.0 / shift
    diag[...] = lax.rsqrt(diag[...] + shift)
    for i in range(BLOCKS):
        side[span(i), :] = jnp.broadcast_to(diag[:, span(i)], (TILE, TILE)).T

    def scaled(i, d):
        values = tile(i, d)
        if d == 0:
            values = values + jnp.where(eye, shift, 0.0)
        return values * side[span(i), :] * diag[:, span((i + d) % BLOCKS)]

    squares = jnp.zeros((TILE, TILE), F32)
    for i in range(BLOCKS):
        for d in range(kept(i)):
            j = (i + d) % BLOCKS
            off = tile(i, d) * per_shift
            if d == 0:
                off = jnp.where(eye, 0.0, off)
                squares = squares + 0.5 * off * off
            else:
                squares = squares + off * off
            values = scaled(i, d)
            top = values.astype(BF16)
            rest = (values - top.astype(F32)).astype(BF16)
            high[span(i), span(j)] = top
            low[span(i), span(j)] = rest
            if d:
                high[span(j), span(i)] = top.T
                low[span(j), span(i)] = rest.T
    hard = 2.0 * jnp.sum(squares) > 256.0**2

    @pl.when(hard)
    def _():
        for i in range(BLOCKS):
            for d in range(kept(i)):
                j = (i + d) % BLOCKS
                values = scaled(i, d)
                rest = values - values.astype(BF16).astype(F32)
                last = (rest - rest.astype(BF16).astype(F32)).astype(BF16)
                least[span(i), span(j)] = last
                if d:
                    least[span(j), span(i)] = last.T

    def fold(total):
        return jnp.sum(total, axis=0, keepdims=True)

    def twice(values):
        return jnp.concatenate([values, values], axis=1)

    total = jnp.zeros((TILE, RIGHTS), F32)
    for i in range(BLOCKS):
        turned = jnp.concatenate([rights[span(h), span(i)].T for h in range(RIGHTS // TILE)], axis=1)
        b = turned.astype(F32) * twice(side[span(i), :])
        res[span(i), :] = b
        way[span(i), :] = b.astype(BF16)
        sol[span(i), :] = jnp.zeros((TILE, RIGHTS), F32)
        total = total + b * b
    norm = fold(total)
    norm_ref[...] = norm
    bound = norm * jnp.where(hard, HARD_TOL * HARD_TOL, TOL * TOL)
    rough = norm * (ROUGH * ROUGH)

    def apply(*terms):
        total = jnp.zeros((CHUNK, RIGHTS), F32)
        for at in range(0, WIDTH, DOT_ROWS):
            part = slice(at, at + DOT_ROWS)
            q = jnp.dot(terms[0][part, :], way[...], preferred_element_type=F32)
            for term in terms[1:]:
                q = q + jnp.dot(term[part, :], way[...], preferred_element_type=F32)
            image[part, :] = q
            for n in range(0, DOT_ROWS, CHUNK):
                total = total + way[at + n : at + n + CHUNK, :].astype(F32) * q[n : n + CHUNK, :]
        curve_ref[...] = fold(total)

    def unfinished(carry):
        step, left, more = carry
        return jnp.logical_and(step < MAX_STEPS, left > 0.0)

    def advance(carry):
        step, left, more = carry

        @pl.when(hard)
        def _():
            apply(high, low, least)

        @pl.when(jnp.logical_and(jnp.logical_not(hard), more > 0.0))
        def _():
            apply(high, low)

        @pl.when(jnp.logical_and(jnp.logical_not(hard), jnp.logical_not(more > 0.0)))
        def _():
            apply(high)

        norm = norm_ref[...]
        curve = curve_ref[...]
        alpha = jnp.where(curve > 0.0, norm / jnp.where(curve > 0.0, curve, 1.0), 0.0)
        total = jnp.zeros((CHUNK, RIGHTS), F32)
        for at in range(0, WIDTH, CHUNK):
            part = slice(at, at + CHUNK)
            r = res[part, :] - alpha * image[part, :]
            res[part, :] = r
            total = total + r * r
        fresh = fold(total)
        beta = jnp.where(norm > 0.0, fresh / jnp.where(norm > 0.0, norm, 1.0), 0.0)
        norm_ref[...] = fresh
        for at in range(0, WIDTH, CHUNK):
            part = slice(at, at + CHUNK)
            p = way[part, :].astype(F32)
            sol[part, :] += alpha * p
            way[part, :] = (res[part, :] + beta * p).astype(BF16)
        return step + 1, jnp.max(fresh - bound), jnp.max(fresh - rough)

    lax.while_loop(unfinished, advance, (jnp.int32(0), jnp.max(norm - bound), jnp.max(norm - rough)))


def swap_halves(scale, feat, sol, side, theirs, scores, mine, send, recv):
    x, y, z, core = position()
    sibling = device(x, y, z, 1 - core)
    barrier = pltpu.get_barrier_semaphore()
    signal(barrier, sibling)
    size = WIDTH // 4
    copies = []
    for n in range(4):
        part = slice(n * size, (n + 1) * size)
        factor = side[part, :] * scale
        mine[part, :] = (sol[part, :] * jnp.concatenate([factor, factor], axis=1)).astype(BF16)
        if n == 0:
            pl.semaphore_wait(barrier, 1)
        at = pl.ds(n * size, size)
        copies.append(remote(mine.at[at], theirs.at[at], send.at[n], recv.at[n], sibling))
        copies[n].start()
    scores[...] = jnp.dot(feat[...], mine[...], preferred_element_type=F32)
    for copy in copies:
        copy.wait()


def score(feat, theirs, scores, out, held, sems):
    core = position()[3]

    def columns(who):
        return out.at[:, pl.ds(pl.multiple_of(who * RIGHTS, RIGHTS), RIGHTS)]

    own = pltpu.make_async_copy(scores, columns(core), sems.at[0])
    own.start()
    held[...] = jnp.dot(feat[...], theirs[...], preferred_element_type=F32)
    other = pltpu.make_async_copy(held, columns(1 - core), sems.at[1])
    other.start()
    own.wait()
    other.wait()


def on_device(features, targets):
    dma = pltpu.SemaphoreType.DMA
    vmem = pl.BlockSpec(memory_space=pltpu.VMEM)
    anywhere = pl.BlockSpec(memory_space=pl.ANY)
    hbm = pl.BlockSpec(memory_space=pltpu.HBM)
    packed, rights = pl.pallas_call(
        gram_sum,
        name="gram_sum",
        out_shape=(
            jax.ShapeDtypeStruct((4 * UNIT, TILE), F32),
            jax.ShapeDtypeStruct((2, 4, 2, 16, WIDTH), BF16),
        ),
        in_specs=[hbm, hbm],
        out_specs=(vmem, vmem),
        scratch_shapes=[
            pltpu.VMEM((features.shape[0], WIDTH + WIDTH // 2), BF16),
            pltpu.VMEM((4 * UNIT, TILE), F32),
            pltpu.VMEM((2 * UNIT, TILE), F32),
            pltpu.VMEM((2, 3, QUARTERS, TILE), F32),
            pltpu.VMEM((2, 3, SIXTEENTHS, TILE), F32),
            pltpu.VMEM((8, 2, PIECE[0], TILE), F32),
            pltpu.VMEM((8, 2, PIECE[1], TILE), F32),
            pltpu.VMEM((8, 2, PIECE[0], TILE), F32),
            pltpu.VMEM((8, 2, PIECE[1], TILE), F32),
            pltpu.VMEM((NZ, 2, PIECE[0], TILE), F32),
            pltpu.VMEM((NZ, 2, PIECE[1], TILE), F32),
            pltpu.VMEM((1, WIDTH), BF16),
            pltpu.VMEM((8, TILE), F32),
            pltpu.VMEM((NZ * 8, TILE), F32),
            pltpu.VMEM((4, 16, WIDTH), BF16),
            pltpu.VMEM((64, WIDTH), F32),
            pltpu.VMEM((4, 16, WIDTH), BF16),
            dma((3,)), dma((16,)), dma((16,)),
            dma((16,)), dma((16,)), dma((16,)), dma((16,)),
            dma((2, 8)), dma((2, 8)), dma((2, NZ)), dma((2, NZ)),
            dma((16,)), dma((16,)), dma((16,)), dma((16,)), dma((16,)), dma((16,)),
            dma((NZ,)), dma((NZ,)), dma((4,)), dma((4,)), dma((4,)), dma((4,)),
            pltpu.SemaphoreType.REGULAR((3,)),
        ],
        compiler_params=pltpu.CompilerParams(
            collective_id=0, has_side_effects=True, vmem_limit_bytes=40 * 2**20
        ),
    )(
        pltpu.with_memory_space_constraint(features, pltpu.HBM),
        pltpu.with_memory_space_constraint(targets, pltpu.HBM),
    )

    total_rows = features.shape[0] * lax.axis_size("loop") * lax.axis_size("group")
    sol, side = pl.pallas_call(
        functools.partial(solve, 0.05),
        name="solve",
        out_shape=(jax.ShapeDtypeStruct((WIDTH, RIGHTS), F32), jax.ShapeDtypeStruct((WIDTH, TILE), F32)),
        in_specs=[vmem, vmem],
        out_specs=(vmem, vmem),
        scratch_shapes=[
            pltpu.VMEM((WIDTH, WIDTH), BF16),
            pltpu.VMEM((WIDTH, WIDTH), BF16),
            pltpu.VMEM((WIDTH, WIDTH), BF16),
            pltpu.VMEM((WIDTH, RIGHTS), F32),
            pltpu.VMEM((WIDTH, RIGHTS), BF16),
            pltpu.VMEM((WIDTH, RIGHTS), F32),
            pltpu.VMEM((1, WIDTH), F32),
            pltpu.VMEM((1, RIGHTS), F32),
            pltpu.VMEM((1, RIGHTS), F32),
        ],
        compiler_params=pltpu.CompilerParams(vmem_limit_bytes=40 * 2**20),
    )(packed, rights.reshape(RIGHTS, WIDTH))

    theirs, scores = pl.pallas_call(
        functools.partial(swap_halves, total_rows / WIDTH**0.5),
        name="swap_halves",
        out_shape=(
            jax.ShapeDtypeStruct((WIDTH, RIGHTS), BF16),
            jax.ShapeDtypeStruct((features.shape[0], RIGHTS), F32),
        ),
        in_specs=[vmem, vmem, vmem],
        out_specs=(vmem, vmem),
        scratch_shapes=[pltpu.VMEM((WIDTH, RIGHTS), BF16), dma((4,)), dma((4,))],
        compiler_params=pltpu.CompilerParams(
            collective_id=1, has_side_effects=True, vmem_limit_bytes=16 * 2**20
        ),
    )(features, sol, side)

    return pl.pallas_call(
        score,
        name="score",
        out_shape=jax.ShapeDtypeStruct((features.shape[0], 2 * RIGHTS), F32),
        in_specs=[vmem, vmem, vmem],
        out_specs=anywhere,
        scratch_shapes=[pltpu.VMEM((features.shape[0], RIGHTS), F32), dma((2,))],
        compiler_params=pltpu.CompilerParams(vmem_limit_bytes=16 * 2**20),
    )(features, theirs, scores)


def solution(mesh):
    return jax.shard_map(
        on_device,
        mesh=mesh,
        in_specs=(P(("loop", "group"), None), P(("loop", "group"), None)),
        out_specs=P(("loop", "group"), None),
        check_vma=False,
    )
```
